32 devices in a mesh: space: 8 (over z, y), rhs: 4 (over x, core).
Axes of the slice: x: 2, y: 2, z: 4, core: 2. Of those that a mesh axis runs over, the one named last changes fastest.
Arguments:
- rhs_vec: float32 [64, 8192], P('rhs', 'space'), may hold values from -40 to 40
- self_coef: float32 [8192], P('space'), may hold values from 2 to 4
- near_mats: bfloat16 [64, 8, 128, 128], P('space'), may hold values from -0.1875 to 0.1875
- near_ids: int32 [64, 8], P('space'), may hold values from 0 to 63, as said below
- near_count: int32 [64], P('space'), may hold values from 3 to 8, as said below
- interp: bfloat16 [64, 128, 32], P('space'), may hold values from -0.5 to 0.5
- skel_idx: int32 [64, 32], P('space'), may hold values from 0 to 127, as said below
- coupling: bfloat16 [2048, 4, 512], P('space', 'rhs'), may hold values from -0.0625 to 0.0625
- diag_prec: float32 [8192], P('space'), may hold values from 1.5 to 4
- low_rank: float32 [8192, 512], P('space'), may hold values from -0.029646353 to 0.029646353
Outputs:
- solution: float32 [64, 8192], P('rhs', 'space')
The draws below stay inside these ranges and needn't reach their ends.
Inputs may be any that keep to these rules, and one draw needn't show every extreme that they name: `near_ids`: slot 0 of each block names the block itself, slot 1 a block of the region before it (of its own region for the first region), slot 2 a block of the region after it (of its own region for the last region); every entry names a block of the same 8-block region or of the region before or after it. `near_count`: some regions use all 8 slots in every block. `skel_idx`: each row holds 32 distinct panel numbers of its block, rising.
All inputs are finite; a program needn't handle non-finite values.
Results may differ from the reference program's by a relative error of at most 0.001.
Values may be sent and summed in bfloat16 or wider, within the bound.
No kernel may reach another device: no remote copies, remote signals or barrier semaphores. Data moves between devices by JAX's collectives and lax.ppermute only.
A program may use at most 64 MiB of HBM per device.

```python
import math
import jax
import jax.numpy as jnp
from jax import lax

BLK = 128
RANK = 32
LOWR = 512
EXC = 64
K_MAX = 8
NB_DEV = 8
NBLOCKS = 64
PANELS = 8192
SKQ = 64
NSKEL = 2048
N_SPACE = 8
N_RHS = 4


def factor_draw(key):
    scale_one = (PANELS * 5 // 4) ** (-0.5)
    base = jnp.clip(jax.random.normal(jax.random.fold_in(key, 41), (PANELS, LOWR), jnp.float32), -3.0, 3.0)
    return base * scale_one


def draw_low_rank(key, part):
    return factor_draw(key)


def draw_rhs_vec(key, part):
    factor = factor_draw(key)
    mix_scale = math.sqrt(10.0 * PANELS / LOWR)
    mixing = jax.random.normal(jax.random.fold_in(key, 42), (LOWR, EXC), jnp.float32) * mix_scale
    aligned = jnp.transpose(jnp.dot(factor, mixing, precision=lax.Precision.HIGHEST))
    noise = jnp.clip(jax.random.normal(jax.random.fold_in(key, 43), (EXC, PANELS), jnp.float32), -6.0, 6.0) * 4.0
    return jnp.clip(noise + aligned, -40.0, 40.0)


def draw_near_ids(key, part):
    block = jnp.arange(NBLOCKS, dtype=jnp.int32)
    region = block // NB_DEV
    last_region = NBLOCKS // NB_DEV - 1
    lowest = jnp.maximum(0, (region - 1) * NB_DEV)
    highest = jnp.minimum(NBLOCKS, (region + 2) * NB_DEV)
    raw_ids = jax.random.randint(jax.random.fold_in(key, 21), (NBLOCKS, K_MAX), 0, 3 * NB_DEV)
    chosen = lowest[:, None] + raw_ids % (highest - lowest)[:, None]
    side_raw = jax.random.randint(jax.random.fold_in(key, 22), (NBLOCKS, 2), 0, NB_DEV)
    before = jnp.maximum(region - 1, 0) * NB_DEV + side_raw[:, 0]
    after = jnp.minimum(region + 1, last_region) * NB_DEV + side_raw[:, 1]
    chosen = chosen.at[:, 0].set(block)
    chosen = chosen.at[:, 1].set(before)
    chosen = chosen.at[:, 2].set(after)
    return chosen.astype(jnp.int32)


def draw_near_count(key, part):
    heavy = jax.random.randint(jax.random.fold_in(key, 11), (NBLOCKS // NB_DEV,), 0, 4) == 0
    heavy = heavy.at[0].set(True)
    light = jax.random.randint(jax.random.fold_in(key, 12), (NBLOCKS,), 3, max(4, K_MAX // 2 + 1))
    heavy_blocks = jnp.repeat(heavy, NB_DEV)
    return jnp.where(heavy_blocks, K_MAX, light).astype(jnp.int32)


def draw_skel_idx(key, part):
    row_keys = jax.random.split(jax.random.fold_in(key, 31), NBLOCKS)
    chosen = jax.vmap(lambda row_key: jax.random.permutation(row_key, BLK)[:RANK])(row_keys)
    return jnp.sort(chosen, axis=1).astype(jnp.int32)


def block_scale(stream_key, dims, cuts, low, largest):
    level, own = 1.0, jax.random.fold_in(stream_key, 6)
    for dim, blocks in cuts:
        heights = jnp.exp(jax.random.uniform(jax.random.fold_in(own, dim), (blocks,), jnp.float32, low / len(cuts), largest / len(cuts)))
        level = level * jnp.repeat(heights, dims[dim] // blocks).reshape([-1 if axis == dim else 1 for axis in range(len(dims))])
    return level


def gaussian(key, dims, deviation, limit, cuts=(), kind=jnp.bfloat16):
    array = deviation * jax.random.normal(key, dims, jnp.float32)
    if cuts:
        array = array * block_scale(key, dims, cuts, -0.22, 0.18)
    return jnp.clip(array, -limit, limit).astype(kind)


def setup_inputs(seed: int = 0) -> dict:
    key_list = jax.random.split(jax.random.key(seed), 11)
    rhs_vec = draw_rhs_vec(jax.random.fold_in(key_list[10], 71), 0)
    self_coef = jnp.clip(jnp.exp(math.log(4.0) - 0.6931472 * jax.random.uniform(key_list[1], (PANELS,), jnp.float32) ** block_scale(key_list[1], (PANELS,), ((0, 8),), -0.2, 0.2)), 2.0, 4.0)
    near_mats = gaussian(key_list[2], (NBLOCKS, K_MAX, BLK, BLK), (BLK * K_MAX) ** -0.5, 0.1875, ((0, 8),))
    near_ids = draw_near_ids(jax.random.fold_in(key_list[10], 71), 0)
    near_count = draw_near_count(jax.random.fold_in(key_list[10], 71), 0)
    interp = gaussian(key_list[5], (NBLOCKS, BLK, RANK), BLK ** -0.5, 0.5, ((0, 8),))
    skel_idx = draw_skel_idx(jax.random.fold_in(key_list[10], 71), 0)
    coupling = gaussian(key_list[7], (NSKEL, N_RHS, N_SPACE * SKQ), (4 * NSKEL) ** -0.5, 0.0625, ((0, 8), (1, 4)))
    diag_prec = jnp.clip(jnp.exp(math.log(4.0) - 0.98082925 * jax.random.uniform(key_list[8], (PANELS,), jnp.float32) ** block_scale(key_list[8], (PANELS,), ((0, 8),), -0.2, 0.2)), 1.5, 4.0)
    low_rank = draw_low_rank(jax.random.fold_in(key_list[10], 71), 0)
    return {"rhs_vec": rhs_vec, "self_coef": self_coef, "near_mats": near_mats, "near_ids": near_ids, "near_count": near_count, "interp": interp, "skel_idx": skel_idx, "coupling": coupling, "diag_prec": diag_prec, "low_rank": low_rank}


HIGH = lax.Precision.HIGHEST
EPS = 1e-06

def givens_pair(start_len, diag_one, below_one, upper_two, diag_two, below_two):
    radius_one = jnp.sqrt(diag_one * diag_one + below_one * below_one)
    cos_one = diag_one / radius_one
    sin_one = below_one / radius_one
    upper = cos_one * upper_two + sin_one * diag_two
    lower = cos_one * diag_two - sin_one * upper_two
    radius_two = jnp.sqrt(lower * lower + below_two * below_two)
    step_two = lower / radius_two * (-sin_one * start_len) / radius_two
    step_one = (cos_one * start_len - upper * step_two) / radius_one
    return (step_one, step_two)

def reference(rhs_vec, self_coef, near_mats, near_ids, near_count, interp, skel_idx, coupling, diag_prec, low_rank):
    excitations = rhs_vec.shape[0]
    onehot = (skel_idx[:, :, None] == jnp.arange(BLK, dtype=jnp.int32)[None, None, :]).astype(jnp.float32)
    restrict = onehot + jnp.swapaxes(interp.astype(jnp.float32), 1, 2)
    live_slots = (jnp.arange(K_MAX, dtype=jnp.int32)[None, :] < near_count[:, None]).astype(jnp.bfloat16)
    slot_mats = near_mats.astype(jnp.float32)
    coupling_blocks = coupling.reshape(NBLOCKS, RANK, N_RHS, N_SPACE * SKQ)

    def precond(vector):
        projected = jnp.dot(vector, low_rank, precision=HIGH)
        return diag_prec[None, :] * vector - jnp.dot(projected, low_rank.T, precision=HIGH)

    def operate(field):
        field_low = field.astype(jnp.bfloat16)
        blocks = field_low.reshape(excitations, NBLOCKS, BLK)

        def near_row(row_blocks):
            picked = row_blocks[near_ids] * live_slots[:, :, None]
            return jnp.einsum('bkij,bkj->bi', slot_mats, picked.astype(jnp.float32), precision=HIGH)
        near = lax.map(near_row, blocks)
        charges = jnp.einsum('brj,ebj->ebr', restrict, blocks.astype(jnp.float32), precision=HIGH)
        packed = charges.astype(jnp.bfloat16).reshape(excitations, N_SPACE, N_RHS, SKQ)
        charges_in = jnp.transpose(packed, (0, 2, 1, 3)).reshape(excitations, N_RHS, N_SPACE * SKQ).astype(jnp.float32)

        def far_block(rows):
            return jnp.einsum('gqc,eqc->eg', rows.astype(jnp.float32), charges_in, precision=HIGH)
        far_field = jnp.transpose(lax.map(far_block, coupling_blocks), (1, 0, 2))
        far_pot = jnp.einsum('brj,ebr->ebj', restrict, far_field, precision=HIGH)
        return self_coef[None, :] * field + near.reshape(excitations, PANELS) + far_pot.reshape(excitations, PANELS)
    start_len = jnp.sqrt(lax.optimization_barrier(jnp.sum(rhs_vec * rhs_vec, axis=1)) + EPS)
    first_dir = rhs_vec / start_len[:, None]
    first_pre = precond(first_dir)
    residue = operate(first_pre)
    diag_one = lax.optimization_barrier(jnp.sum(residue * first_dir, axis=1))
    residue = residue - diag_one[:, None] * first_dir
    below_one = jnp.sqrt(lax.optimization_barrier(jnp.sum(residue * residue, axis=1)) + EPS)
    second_dir = residue / below_one[:, None]
    second_pre = precond(second_dir)
    residue = operate(second_pre)
    upper_two = lax.optimization_barrier(jnp.sum(residue * first_dir, axis=1))
    diag_two = lax.optimization_barrier(jnp.sum(residue * second_dir, axis=1))
    residue = residue - upper_two[:, None] * first_dir
    residue = residue - diag_two[:, None] * second_dir
    below_two = jnp.sqrt(lax.optimization_barrier(jnp.sum(residue * residue, axis=1)) + EPS)
    step_one, step_two = givens_pair(start_len, diag_one, below_one, upper_two, diag_two, below_two)
    return step_one[:, None] * first_pre + step_two[:, None] * second_pre
```

```python
import jax
import jax.numpy as jnp
from jax import lax
from jax.sharding import PartitionSpec as P

HIGH = lax.Precision.HIGH
EPS = 1e-06
BF = jnp.bfloat16
AXIS = "space"


def swap(values, mask, count):
    return lax.ppermute(values, AXIS, [(i, i ^ mask) for i in range(count)])


def total(values, count):
    if count != 8:
        return lax.psum(values, AXIS)
    pair = values + swap(values, 1, count)
    return (pair + swap(pair, 2, count)) + (swap(pair, 4, count) + swap(pair, 6, count))


def total_small(values, count):
    if count != 8:
        return lax.psum(values, AXIS)
    spread = jnp.broadcast_to(values[None], (count,) + values.shape)
    return jnp.sum(lax.all_to_all(spread, AXIS, 0, 0), axis=0)


def exchange(field, charges, count, region):
    excitations, panels = field.shape
    rank = charges.shape[1]
    if count != 8:
        ends = count - 1
        lower = lax.ppermute(field, AXIS, [(i, i + 1) for i in range(ends)])
        upper = lax.ppermute(field, AXIS, [(i + 1, i) for i in range(ends)])
        return [lower, field, upper], lax.all_gather(charges, AXIS)
    own = jnp.concatenate([field, charges], axis=1)
    near = swap(own, 1, count)
    pair = jnp.concatenate([charges, near[:, panels:], near[:, :panels]], axis=1)
    two = swap(pair, 2, count)
    four = swap(pair[:, : 2 * rank], 4, count)
    six = swap(pair, 6, count)
    by_mask = []
    for part in (pair, two, four, six):
        by_mask += [part[:, :rank], part[:, rank : 2 * rank]]
    stacked = jnp.stack(by_mask)
    order = jnp.arange(count, dtype=jnp.int32) ^ region
    return [field, near[:, :panels], two[:, 2 * rank :], six[:, 2 * rank :]], stacked[order]


def block_places(near_ids, block_count, count, region):
    if count != 8:
        return near_ids - (region - 1) * block_count
    source = near_ids // block_count
    slot = jnp.where(
        source == region,
        0,
        jnp.where(source == region ^ 1, 1, jnp.where(source == region ^ 3, 2, 3)),
    )
    return slot * block_count + near_ids % block_count


def givens_pair(start_len, diag_one, below_one, upper_two, diag_two, below_two):
    radius_one = jnp.sqrt(diag_one * diag_one + below_one * below_one)
    cos_one = diag_one / radius_one
    sin_one = below_one / radius_one
    upper = cos_one * upper_two + sin_one * diag_two
    lower = cos_one * diag_two - sin_one * upper_two
    radius_two = jnp.sqrt(lower * lower + below_two * below_two)
    step_two = lower / radius_two * (-sin_one * start_len) / radius_two
    step_one = (cos_one * start_len - upper * step_two) / radius_one
    return (step_one, step_two)


def dots(vector, others):
    return jnp.stack([jnp.sum(vector * other, axis=1) for other in others], axis=1)


def on_device(
    rhs_vec,
    self_coef,
    near_mats,
    near_ids,
    near_count,
    interp,
    skel_idx,
    coupling,
    diag_prec,
    low_rank,
):
    excitations, panels = rhs_vec.shape
    block_count, slot_count, block_width, _ = near_mats.shape
    skel_rank = interp.shape[2]
    quarters = lax.axis_size("rhs")
    count = lax.axis_size(AXIS)
    quarter_len = skel_rank * block_count // quarters
    low_rank_width = low_rank.shape[1]
    region = lax.axis_index(AXIS)
    onehot = (
        skel_idx[:, :, None] == jnp.arange(block_width, dtype=jnp.int32)[None, None, :]
    ).astype(BF)
    weights = jnp.swapaxes(interp, 1, 2)
    restrict_in = jnp.concatenate([onehot, weights], axis=2)
    restrict_out = jnp.concatenate([onehot, weights, onehot, weights], axis=1)
    places = block_places(near_ids, block_count, count, region)
    live_slots = jnp.arange(slot_count, dtype=jnp.int32)[None, :] < near_count[:, None]
    full_rows = lax.all_gather(coupling, "rhs", axis=1, tiled=True)
    full_rows = full_rows.reshape(skel_rank * block_count, quarters, count, quarter_len)

    def project(vector):
        return jnp.dot(vector, low_rank, precision=HIGH)

    def precond(vector, projected):
        return diag_prec[None, :] * vector - jnp.dot(projected, low_rank.T, precision=HIGH)

    def operate(field):
        field_low = field.astype(BF)
        own_blocks = field_low.reshape(excitations, block_count, block_width)
        charges = jnp.einsum(
            "brj,ebj->ebr",
            restrict_in,
            jnp.concatenate([own_blocks, own_blocks], axis=2),
            preferred_element_type=jnp.float32,
        )
        packed = charges.astype(BF).reshape(excitations, skel_rank * block_count)
        sources, charges_in = exchange(field_low, packed, count, region)
        blocks = jnp.concatenate(
            [part.reshape(excitations, block_count, block_width) for part in sources], axis=1
        )
        picked = blocks[:, places] * live_slots[None, :, :, None].astype(BF)
        near = jnp.einsum("bkij,ebkj->ebi", near_mats, picked, preferred_element_type=jnp.float32)
        far_field = jnp.einsum(
            "gqsj,seqj->eg",
            full_rows,
            charges_in.reshape(count, excitations, quarters, quarter_len),
            preferred_element_type=jnp.float32,
        ).reshape(excitations, block_count, skel_rank)
        far_high = far_field.astype(BF)
        far_low = (far_field - far_high.astype(jnp.float32)).astype(BF)
        far_pot = jnp.einsum(
            "brj,ebr->ebj",
            restrict_out,
            jnp.concatenate([far_high, far_high, far_low, far_low], axis=2),
            preferred_element_type=jnp.float32,
        )
        return (
            self_coef[None, :] * field
            + near.reshape(excitations, panels)
            + far_pot.reshape(excitations, panels)
        )

    def project_and_dots(vector, others):
        tail = dots(vector, others)
        tail = jnp.pad(tail, ((0, 0), (0, 128 - len(others))))
        summed = total(jnp.concatenate([project(vector), tail], axis=1), count)
        return summed[:, :low_rank_width], [
            summed[:, low_rank_width + i][:, None] for i in range(len(others))
        ]

    rhs_proj, (rhs_sq,) = project_and_dots(rhs_vec, [rhs_vec])
    start_len = jnp.sqrt(rhs_sq + EPS)
    first_dir = rhs_vec / start_len
    first_proj = rhs_proj / start_len
    first_sq = rhs_sq / (start_len * start_len)
    first_pre = precond(first_dir, first_proj)
    residue = operate(first_pre)
    res_proj, (diag_one, res_sq) = project_and_dots(residue, [first_dir, residue])
    below_sq = res_sq - diag_one * diag_one * (2.0 - first_sq)
    below_one = jnp.sqrt(jnp.maximum(below_sq, 0.0) + EPS)
    second_dir = (residue - diag_one * first_dir) / below_one
    second_proj = (res_proj - diag_one * first_proj) / below_one
    second_pre = precond(second_dir, second_proj)
    residue = operate(second_pre)
    tail = total_small(
        dots(residue, [first_dir, second_dir, residue]).T, count
    )
    upper_two, diag_two, res_sq = [tail[i][:, None] for i in range(3)]
    cross = diag_one * (1.0 - first_sq) / below_one
    second_sq = jnp.maximum(below_sq, 0.0) / (below_one * below_one)
    left_sq = (
        res_sq
        - upper_two * upper_two * (2.0 - first_sq)
        - diag_two * diag_two * (2.0 - second_sq)
        + 2.0 * upper_two * diag_two * cross
    )
    below_two = jnp.sqrt(jnp.maximum(left_sq, 0.0) + EPS)
    step_one, step_two = givens_pair(
        start_len, diag_one, below_one, upper_two, diag_two, below_two
    )
    return step_one * first_pre + step_two * second_pre


def solution(mesh):
    placed = (
        P("rhs", "space"),
        P("space"),
        P("space", None, None, None),
        P("space", None),
        P("space"),
        P("space", None, None),
        P("space", None),
        P("space", "rhs", None),
        P("space"),
        P("space", None),
    )
    return jax.shard_map(
        on_device, mesh=mesh, in_specs=placed, out_specs=P("rhs", "space"), check_vma=False
    )
```

```python
import jax
import jax.numpy as jnp
from jax import lax
from jax.experimental import pallas as pl
from jax.experimental.pallas import tpu as pltpu
from jax.sharding import PartitionSpec as P

EPS = 1e-06
F32 = jnp.float32
BF = jnp.bfloat16
AXIS = "space"
LANES = 128
HALF = 64


def swap(values, mask, count):
    return lax.ppermute(values, AXIS, [(i, i ^ mask) for i in range(count)])


def split(values):
    high = values.astype(BF)
    return high, (values - high.astype(F32)).astype(BF)


def dot_nn(left, right):
    return lax.dot_general(left, right, (((1,), (0,)), ((), ())), preferred_element_type=F32)


def dot_nt(left, right):
    return lax.dot_general(left, right, (((1,), (1,)), ((), ())), preferred_element_type=F32)


def dot_wide(dot, vector, high, low):
    rows = vector.shape[0]
    vec_high, vec_low = split(vector)
    first = dot(jnp.concatenate([vec_high, vec_low], axis=0), high)
    return first[:rows] + first[rows:] + dot(vec_high, low)


def row_sum(values):
    return jnp.sum(values, axis=1, keepdims=True)


def put_scalars(columns, rows):
    lane = lax.broadcasted_iota(jnp.int32, (rows, LANES), 1)
    out = jnp.zeros((rows, LANES), F32)
    for index, column in enumerate(columns):
        out = jnp.where(lane == index, column, out)
    return out


def column(values, index):
    return values[:, index : index + 1]


def charge_rows(field_low, maps_ref, send_ref, panels, quarters):
    width = panels // quarters
    for quarter in range(quarters):
        rows = slice(quarter * width, (quarter + 1) * width)
        both = dot_nn(field_low[:, rows], maps_ref[rows, :])
        start = panels + quarter * LANES
        send_ref[:, start : start + LANES] = (both[:, :LANES] + both[:, LANES:]).astype(BF)


def open_kernel(rhs_ref, factor_ref, out_ref, high_ref, low_ref):
    step = pl.program_id(0)
    width = factor_ref.shape[1]
    rhs = rhs_ref[...]
    high, low = split(factor_ref[...])
    high_ref[...] = high
    low_ref[...] = low
    part = dot_wide(dot_nn, rhs, high, low)
    tail = put_scalars([row_sum(rhs * rhs)], rhs.shape[0])

    @pl.when(step == 0)
    def _():
        out_ref[:, :width] = part
        out_ref[:, width:] = tail

    @pl.when(step > 0)
    def _():
        out_ref[:, :width] += part
        out_ref[:, width:] += tail


def first_kernel(quarters, parts, *refs):
    sums = refs[:parts]
    rhs_ref, diag_ref, high_ref, low_ref, maps_ref = refs[parts : parts + 5]
    dir_ref, pre_ref, send_ref, keep_ref = refs[parts + 5 :]
    width = high_ref.shape[1]
    rows, panels = rhs_ref.shape
    summed = sums[0][...]
    for ref in sums[1:]:
        summed = summed + ref[...]
    rhs_sq = column(summed[:, width:], 0)
    start_len = jnp.sqrt(rhs_sq + EPS)
    first_dir = rhs_ref[...] / start_len
    proj = summed[:, :width] / start_len
    first_pre = diag_ref[...] * first_dir - dot_wide(dot_nt, proj, high_ref[...], low_ref[...])
    field_low = first_pre.astype(BF)
    dir_ref[...] = first_dir
    pre_ref[...] = first_pre
    send_ref[:, :panels] = field_low
    charge_rows(field_low, maps_ref, send_ref, panels, quarters)
    keep_ref[:, :width] = proj
    keep_ref[:, width:] = put_scalars([start_len, rhs_sq / (start_len * start_len)], rows)


def apply_matrix(
    quarters, sources, place_ref, region_ref, field_refs, charge_refs, field, self_ref, mats_ref,
    coupling_ref, maps_ref, blocks_ref, charges_ref
):
    rows, panels = field.shape
    block_count, slots, block, _ = mats_ref.shape
    for index, ref in enumerate(field_refs):
        for b in range(block_count):
            blocks_ref[index * block_count + b] = ref[:, b * block : (b + 1) * block]
    blocks_ref[sources * block_count] = jnp.zeros((rows, block), BF)
    pairs = charges_ref.shape[0]
    if len(charge_refs) == pairs:
        for index, (ref, start) in enumerate(charge_refs):
            charges_ref[(region_ref[0] // 2) ^ index] = ref[:, start : start + quarters * LANES]
    else:
        charges_ref[...] = charge_refs[0][0][...]
    far = jnp.zeros((rows, coupling_ref.shape[1]), F32)
    for quarter in range(quarters):
        lanes = slice(quarter * LANES, (quarter + 1) * LANES)
        charge = jnp.concatenate([charges_ref[t, :, lanes] for t in range(pairs)], axis=1)
        far = far + dot_nt(charge, coupling_ref[quarter])
    odd = (region_ref[0] % 2) == 1
    per = panels // quarters
    out = []
    for quarter in range(quarters):
        start = (quarter // 2) * LANES
        chunk = far[:, start : start + LANES]
        turned = pltpu.roll(chunk, HALF, 1)
        chunk = jnp.where(odd, turned, chunk) if quarter % 2 == 0 else jnp.where(odd, chunk, turned)
        high, low = split(chunk)
        both = jnp.concatenate([high, low], axis=0)
        pot = dot_nt(
            jnp.concatenate([both, both], axis=1), maps_ref[quarter * per : (quarter + 1) * per, :]
        )
        out.append(pot[:rows] + pot[rows:])
    for b in range(block_count):
        picked = jnp.concatenate([blocks_ref[place_ref[b, k]] for k in range(slots)], axis=1)
        mats = jnp.concatenate([mats_ref[b, k] for k in range(slots)], axis=1)
        near = dot_nt(picked, mats)
        quarter, rest = divmod(b * block, per)
        cols = slice(b * block, (b + 1) * block)
        out_b = near + out[quarter][:, rest : rest + block]
        yield cols, out_b + self_ref[:, cols] * field[:, cols]


def second_kernel(quarters, nfields, ncharges, charge_starts, place_ref, region_ref, *refs):
    field_refs = refs[:nfields]
    charge_refs = list(zip(refs[nfields : nfields + ncharges], charge_starts))
    refs = refs[nfields + ncharges :]
    dir_ref, pre_ref, self_ref, mats_ref, coupling_ref, maps_ref, high_ref, low_ref = refs[:8]
    res_ref, out_ref, blocks_ref, charges_ref = refs[8:]
    width = high_ref.shape[1]
    rows = pre_ref.shape[0]
    for cols, values in apply_matrix(
        quarters, nfields, place_ref, region_ref, field_refs, charge_refs, pre_ref, self_ref,
        mats_ref, coupling_ref, maps_ref, blocks_ref, charges_ref
    ):
        res_ref[:, cols] = values
    res = res_ref[...]
    out_ref[:, :width] = dot_wide(dot_nn, res, high_ref[...], low_ref[...])
    out_ref[:, width:] = put_scalars([row_sum(res * dir_ref[...]), row_sum(res * res)], rows)


def third_kernel(quarters, parts, *refs):
    sums = refs[:parts]
    res_ref, dir_ref, keep_ref, diag_ref, high_ref, low_ref, maps_ref = refs[parts : parts + 7]
    next_ref, pre_ref, send_ref, scalars_ref = refs[parts + 7 :]
    width = high_ref.shape[1]
    rows, panels = res_ref.shape
    summed = sums[0][...]
    for ref in sums[1:]:
        summed = summed + ref[...]
    keep = keep_ref[:, width:]
    start_len, first_sq = column(keep, 0), column(keep, 1)
    diag_one, res_sq = column(summed[:, width:], 0), column(summed[:, width:], 1)
    below_sq = jnp.maximum(res_sq - diag_one * diag_one * (2.0 - first_sq), 0.0)
    below_one = jnp.sqrt(below_sq + EPS)
    second_dir = (res_ref[...] - diag_one * dir_ref[...]) / below_one
    proj = (summed[:, :width] - diag_one * keep_ref[:, :width]) / below_one
    pre = diag_ref[...] * second_dir - dot_wide(dot_nt, proj, high_ref[...], low_ref[...])
    field_low = pre.astype(BF)
    next_ref[...] = second_dir
    pre_ref[...] = pre
    send_ref[:, :panels] = field_low
    charge_rows(field_low, maps_ref, send_ref, panels, quarters)
    cross = diag_one * (1.0 - first_sq) / below_one
    second_sq = below_sq / (below_one * below_one)
    scalars_ref[...] = put_scalars(
        [start_len, first_sq, diag_one, below_one, cross, second_sq], rows
    )


def fourth_kernel(quarters, nfields, ncharges, charge_starts, place_ref, region_ref, *refs):
    field_refs = refs[:nfields]
    charge_refs = list(zip(refs[nfields : nfields + ncharges], charge_starts))
    refs = refs[nfields + ncharges :]
    dir_ref, next_ref, pre_ref, self_ref, mats_ref, coupling_ref, maps_ref = refs[:7]
    out_ref, blocks_ref, charges_ref = refs[7:]
    rows = pre_ref.shape[0]
    block = mats_ref.shape[2]
    upper = jnp.zeros((rows, block), F32)
    diag = jnp.zeros((rows, block), F32)
    square = jnp.zeros((rows, block), F32)
    for cols, values in apply_matrix(
        quarters, nfields, place_ref, region_ref, field_refs, charge_refs, pre_ref, self_ref,
        mats_ref, coupling_ref, maps_ref, blocks_ref, charges_ref
    ):
        upper = upper + values * dir_ref[:, cols]
        diag = diag + values * next_ref[:, cols]
        square = square + values * values
    out_ref[...] = put_scalars([row_sum(upper), row_sum(diag), row_sum(square)], rows)


def givens_pair(start_len, diag_one, below_one, upper_two, diag_two, below_two):
    radius_one = jnp.sqrt(diag_one * diag_one + below_one * below_one)
    cos_one = diag_one / radius_one
    sin_one = below_one / radius_one
    upper = cos_one * upper_two + sin_one * diag_two
    lower = cos_one * diag_two - sin_one * upper_two
    radius_two = jnp.sqrt(lower * lower + below_two * below_two)
    step_two = lower / radius_two * (-sin_one * start_len) / radius_two
    step_one = (cos_one * start_len - upper * step_two) / radius_one
    return (step_one, step_two)


def last_kernel(sums_ref, scalars_ref, first_ref, second_ref, out_ref):
    summed = jnp.sum(sums_ref[...], axis=0)
    start_len, first_sq, diag_one, below_one, cross, second_sq = [
        column(scalars_ref[...], i) for i in range(6)
    ]
    upper_two, diag_two, res_sq = [column(summed, i) for i in range(3)]
    left_sq = (
        res_sq
        - upper_two * upper_two * (2.0 - first_sq)
        - diag_two * diag_two * (2.0 - second_sq)
        + 2.0 * upper_two * diag_two * cross
    )
    below_two = jnp.sqrt(jnp.maximum(left_sq, 0.0) + EPS)
    step_one, step_two = givens_pair(
        start_len, diag_one, below_one, upper_two, diag_two, below_two
    )
    out_ref[...] = step_one * first_ref[...] + step_two * second_ref[...]


def sum_parts(values, count):
    if count != 8:
        return [lax.psum(values, AXIS)]
    pair = values + swap(values, 1, count)
    return [pair, swap(pair, 2, count), swap(pair, 4, count), swap(pair, 6, count)]


def exchange(send, panels, count):
    field, charges = send[:, :panels], send[:, panels:]
    if count != 8:
        ends = count - 1
        lower = lax.ppermute(field, AXIS, [(i, i + 1) for i in range(ends)])
        upper = lax.ppermute(field, AXIS, [(i + 1, i) for i in range(ends)])
        every = lax.all_gather(charges, AXIS)
        every = every.reshape((count // 2, 2) + charges.shape)
        return [lower, send, upper], [every[:, 0] + every[:, 1]], [0]
    near = swap(send, 1, count)
    pair = charges + near[:, panels:]
    onward = jnp.concatenate([near[:, :panels], pair], axis=1)
    two = swap(onward, 2, count)
    four = swap(pair, 4, count)
    six = swap(onward, 6, count)
    return [send, near, two, six], [pair, two, four, six], [0, panels, 0, panels]


def block_places(near_ids, near_count, block_count, count, region):
    sources = 4 if count == 8 else 3
    if count == 8:
        source = near_ids // block_count
        slot = jnp.where(
            source == region,
            0,
            jnp.where(source == region ^ 1, 1, jnp.where(source == region ^ 3, 2, 3)),
        )
        places = slot * block_count + near_ids % block_count
    else:
        places = near_ids - (region - 1) * block_count
    live = jnp.arange(near_ids.shape[1], dtype=jnp.int32)[None, :] < near_count[:, None]
    return jnp.where(live, places, sources * block_count)


def skeleton_maps(interp, skel_idx, block, odd):
    panel = jnp.arange(block, dtype=jnp.int32)
    onehot = (skel_idx[:, None, :] == panel[None, :, None]).astype(BF)
    second = (jnp.arange(interp.shape[0]) % 2 == 1)[:, None, None]

    def place(part):
        zero = jnp.zeros_like(part)
        wide = jnp.concatenate(
            [jnp.where(second, zero, part), jnp.where(second, part, zero)], axis=2
        )
        none = jnp.zeros_like(wide)
        return jnp.concatenate([jnp.where(odd, none, wide), jnp.where(odd, wide, none)], axis=2)

    maps = jnp.concatenate([place(onehot), place(interp)], axis=2)
    return maps.reshape(-1, maps.shape[2])


def call(kernel, out_shapes, args, scratch=(), scalars=0):
    specs = [pl.BlockSpec(memory_space=pltpu.SMEM)] * scalars
    specs += [pl.BlockSpec(memory_space=pltpu.VMEM)] * (len(args) - scalars)
    outs = [pl.BlockSpec(memory_space=pltpu.VMEM)] * len(out_shapes)
    return pl.pallas_call(
        kernel,
        out_shape=[jax.ShapeDtypeStruct(shape, kind) for shape, kind in out_shapes],
        in_specs=specs,
        out_specs=outs,
        scratch_shapes=list(scratch),
        compiler_params=pltpu.CompilerParams(vmem_limit_bytes=40 * 2**20),
    )(*args)


def on_device(
    rhs_vec,
    self_coef,
    near_mats,
    near_ids,
    near_count,
    interp,
    skel_idx,
    coupling,
    diag_prec,
    low_rank,
):
    rows, panels = rhs_vec.shape
    block_count, slots, block, _ = near_mats.shape
    skeletons = coupling.shape[0]
    quarters = lax.axis_size("rhs")
    count = lax.axis_size(AXIS)
    width = low_rank.shape[1]
    region = lax.axis_index(AXIS)
    full_rows = lax.all_gather(coupling[:, 0, :], "rhs")
    places = block_places(near_ids, near_count, block_count, count, region)
    maps = skeleton_maps(interp, skel_idx, block, region % 2 == 1)
    where = jnp.full((1,), region, jnp.int32)
    self_row = self_coef[None, :]
    diag_row = diag_prec[None, :]
    wide = width + LANES
    long = panels + quarters * LANES

    steps = 4
    depth = panels // steps
    payload, high, low = pl.pallas_call(
        open_kernel,
        grid=(steps,),
        out_shape=[
            jax.ShapeDtypeStruct((rows, wide), F32),
            jax.ShapeDtypeStruct((panels, width), BF),
            jax.ShapeDtypeStruct((panels, width), BF),
        ],
        in_specs=[
            pl.BlockSpec((rows, depth), lambda i: (0, i)),
            pl.BlockSpec((depth, width), lambda i: (i, 0)),
        ],
        out_specs=[
            pl.BlockSpec((rows, wide), lambda i: (0, 0)),
            pl.BlockSpec((depth, width), lambda i: (i, 0)),
            pl.BlockSpec((depth, width), lambda i: (i, 0)),
        ],
    )(rhs_vec, low_rank)

    sums = sum_parts(payload, count)
    first_dir, first_pre, send, keep = call(
        lambda *refs: first_kernel(quarters, len(sums), *refs),
        [((rows, panels), F32), ((rows, panels), F32), ((rows, long), BF), ((rows, wide), F32)],
        [*sums, rhs_vec, diag_row, high, low, maps],
    )
    fields, charges, starts = exchange(send, panels, count)
    nf, nc = len(fields), len(charges)
    scratch = [
        pltpu.VMEM((nf * block_count + 1, rows, block), BF),
        pltpu.VMEM((count // 2, rows, quarters * LANES), BF),
    ]
    residue, payload = call(
        lambda *refs: second_kernel(quarters, nf, nc, starts, *refs),
        [((rows, panels), F32), ((rows, wide), F32)],
        [places, where, *fields, *charges, first_dir, first_pre, self_row, near_mats, full_rows,
         maps, high, low],
        scratch,
        2,
    )
    sums = sum_parts(payload, count)
    second_dir, second_pre, send, scalars = call(
        lambda *refs: third_kernel(quarters, len(sums), *refs),
        [((rows, panels), F32), ((rows, panels), F32), ((rows, long), BF), ((rows, LANES), F32)],
        [*sums, residue, first_dir, keep, diag_row, high, low, maps],
    )
    fields, charges, starts = exchange(send, panels, count)
    (tail,) = call(
        lambda *refs: fourth_kernel(quarters, nf, nc, starts, *refs),
        [((rows, LANES), F32)],
        [places, where, *fields, *charges, first_dir, second_dir, second_pre,
         self_row, near_mats, full_rows, maps],
        scratch,
        2,
    )
    if count == 8:
        spread = jnp.broadcast_to(tail[None], (count,) + tail.shape)
        tails = lax.all_to_all(spread, AXIS, 0, 0)
    else:
        tails = lax.psum(tail, AXIS)[None]
    (result,) = call(last_kernel, [((rows, panels), F32)], [tails, scalars, first_pre, second_pre])
    return result


def solution(mesh):
    placed = (
        P("rhs", "space"),
        P("space"),
        P("space", None, None, None),
        P("space", None),
        P("space"),
        P("space", None, None),
        P("space", None),
        P("space", "rhs", None),
        P("space"),
        P("space", None),
    )
    return jax.shard_map(
        on_device, mesh=mesh, in_specs=placed, out_specs=P("rhs", "space"), check_vma=False
    )
```

```python
import math

import jax
import jax.numpy as jnp
from jax import lax
from jax.experimental import pallas as pl
from jax.experimental.pallas import tpu as pltpu
from jax.sharding import PartitionSpec as P

EPS = 1e-06
F32 = jnp.float32
BF = jnp.bfloat16
AXIS = "space"
LANES = 128
HALF = 64


def swap(values, mask, count):
    return lax.ppermute(values, AXIS, [(i, i ^ mask) for i in range(count)])


def split(values):
    high = values.astype(BF)
    return high, (values - high.astype(F32)).astype(BF)


def dot_nn(left, right):
    return lax.dot_general(left, right, (((1,), (0,)), ((), ())), preferred_element_type=F32)


def dot_nt(left, right):
    return lax.dot_general(left, right, (((1,), (1,)), ((), ())), preferred_element_type=F32)


def dot_wide(dot, vector, high, low):
    rows = vector.shape[0]
    vec_high, vec_low = split(vector)
    first = dot(jnp.concatenate([vec_high, vec_low], axis=0), high)
    return first[:rows] + first[rows:] + dot(vec_high, low)


def row_sum(values):
    return jnp.sum(values, axis=1, keepdims=True)


def put_scalars(columns, rows):
    lane = lax.broadcasted_iota(jnp.int32, (rows, LANES), 1)
    out = jnp.zeros((rows, LANES), F32)
    for index, column in enumerate(columns):
        out = jnp.where(lane == index, column, out)
    return out


def column(values, index):
    return values[:, index : index + 1]


def charge_rows(field_low, maps_ref, send_ref):
    rows, panels = field_low.shape
    quarters, _, width = maps_ref.shape
    for quarter in range(quarters):
        both = dot_nt(field_low[:, quarter * width : (quarter + 1) * width], maps_ref[quarter])
        start = panels + quarter * LANES
        send_ref[:, start : start + LANES] = (both[:, :LANES] + both[:, LANES:]).astype(BF)


def maps_kernel(weights_ref, skel_ref, maps_ref):
    block_count, rank, block = weights_ref.shape
    quarters = maps_ref.shape[0]
    per = block_count // quarters
    odd_start = pl.multiple_of((lax.axis_index(AXIS) % 2) * HALF, HALF)
    maps_ref[...] = jnp.zeros(maps_ref.shape, BF)
    skel = jnp.concatenate(
        [skel_ref[...].astype(F32), jnp.zeros((block_count, LANES - rank), F32)], axis=1
    ).T
    panel = lax.broadcasted_iota(jnp.int32, (rank, block), 1).astype(F32)
    for b in range(block_count):
        quarter, index = divmod(b, per)
        start = odd_start + index * rank
        cols = slice(index * block, (index + 1) * block)
        hot = jnp.where(skel[:rank, b : b + 1] == panel, 1.0, 0.0).astype(BF)
        maps_ref[quarter, pl.ds(start, rank), cols] = hot
        maps_ref[quarter, pl.ds(start + LANES, rank), cols] = weights_ref[b]


def onward_kernel(send_ref, near_ref, onward_ref, pair_ref):
    panels = near_ref.shape[1] - pair_ref.shape[1]
    pair = send_ref[:, panels:] + near_ref[:, panels:]
    onward_ref[:, :panels] = near_ref[:, :panels]
    onward_ref[:, panels:] = pair
    pair_ref[...] = pair


def open_kernel(parts, rhs_hbm, factor_hbm, diag_hbm, self_hbm, out_ref, rhs_ref, diag_ref,
                self_ref, held_ref, sems):
    panels, width = factor_hbm.shape
    rows = rhs_ref.shape[0]
    depth = panels // parts
    loads = [
        pltpu.make_async_copy(source, target, sems.at[parts + index])
        for index, (source, target) in enumerate(
            [(rhs_hbm, rhs_ref), (diag_hbm, diag_ref), (self_hbm, self_ref)]
        )
    ]
    for load in loads:
        load.start()
    copies = []
    for part in range(parts):
        span = pl.ds(part * depth, depth)
        copies.append(
            pltpu.make_async_copy(factor_hbm.at[span], held_ref.at[span], sems.at[part])
        )
        copies[-1].start()
    loads[0].wait()
    rhs = rhs_ref[...]
    out_ref[:, width:] = put_scalars([row_sum(rhs * rhs)], rows)
    total = jnp.zeros((rows, width), F32)
    for part in range(parts):
        span = slice(part * depth, (part + 1) * depth)
        copies[part].wait()
        high, low = split(held_ref[span, :])
        total = total + dot_wide(dot_nn, rhs[:, span], high, low)
    out_ref[:, :width] = total
    for load in loads[1:]:
        load.wait()


def first_kernel(parts, *refs):
    sums = refs[:parts]
    rhs_ref, diag_ref, factor_ref, maps_ref = refs[parts : parts + 4]
    dir_ref, pre_ref, send_ref, keep_ref, high_ref, low_ref = refs[parts + 4 :]
    width = factor_ref.shape[1]
    high_ref[...], low_ref[...] = split(factor_ref[...])
    rows, panels = rhs_ref.shape
    summed = sums[0][...]
    for ref in sums[1:]:
        summed = summed + ref[...]
    rhs_sq = column(summed[:, width:], 0)
    start_len = jnp.sqrt(rhs_sq + EPS)
    first_dir = rhs_ref[...] / start_len
    proj = summed[:, :width] / start_len
    first_pre = diag_ref[...] * first_dir - dot_wide(dot_nt, proj, high_ref[...], low_ref[...])
    field_low = first_pre.astype(BF)
    dir_ref[...] = first_dir
    pre_ref[...] = first_pre
    send_ref[:, :panels] = field_low
    charge_rows(field_low, maps_ref, send_ref)
    keep_ref[:, :width] = proj
    keep_ref[:, width:] = put_scalars([start_len, rhs_sq / (start_len * start_len)], rows)


def block_place(wanted, live, block_count, sources, region):
    source = wanted // block_count
    if sources == 4:
        slot = jnp.where(
            source == region,
            0,
            jnp.where(source == region ^ 1, 1, jnp.where(source == region ^ 3, 2, 3)),
        )
    else:
        slot = source - region + 1
    return jnp.where(live, slot * block_count + wanted % block_count, sources * block_count)


def apply_matrix(
    ids_ref, live_ref, field_refs, charge_refs, field, self_ref, mats_ref, coupling_refs, maps_ref,
    blocks_ref, charges_ref
):
    rows, panels = field.shape
    block_count, slots, block, _ = mats_ref.shape
    quarters, pairs = charges_ref.shape[:2]
    sources = len(field_refs)
    gathered = len(coupling_refs) == 1
    region = lax.axis_index(AXIS)
    first_quarter = 0 if gathered else lax.axis_index("rhs")
    for index, ref in enumerate(field_refs):
        for b in range(block_count):
            blocks_ref[index * block_count + b] = ref[:, b * block : (b + 1) * block]
    blocks_ref[sources * block_count] = jnp.zeros((rows, block), BF)
    for quarter in range(quarters):
        for index in range(pairs):
            if len(charge_refs) == pairs:
                ref, start = charge_refs[index]
                start += quarter * LANES
                charge = ref[:, start : start + LANES]
                charges_ref[quarter, (region // 2) ^ index] = charge
            else:
                lanes = slice(quarter * LANES, (quarter + 1) * LANES)
                charges_ref[quarter, index] = charge_refs[0][0][index, :, lanes]
    far = jnp.zeros((rows, coupling_refs[0].shape[-2]), F32)
    for index in range(quarters):
        quarter = first_quarter ^ index
        charge = jnp.concatenate([charges_ref[quarter, t] for t in range(pairs)], axis=1)
        rows_in = coupling_refs[0][index] if gathered else coupling_refs[index][...]
        far = far + dot_nt(charge, rows_in)
    odd = (region % 2) == 1
    per = panels // quarters
    out = []
    for quarter in range(quarters):
        start = (quarter // 2) * LANES
        chunk = far[:, start : start + LANES]
        turned = pltpu.roll(chunk, HALF, 1)
        chunk = jnp.where(odd, turned, chunk) if quarter % 2 == 0 else jnp.where(odd, chunk, turned)
        high, low = split(chunk)
        both = jnp.concatenate([high, low], axis=0)
        pot = dot_nn(jnp.concatenate([both, both], axis=1), maps_ref[quarter])
        out.append(pot[:rows] + pot[rows:])
    for b in range(block_count):
        places = [
            block_place(ids_ref[b, k], k < live_ref[b], block_count, sources, region)
            for k in range(slots)
        ]
        picked = jnp.concatenate([blocks_ref[place] for place in places], axis=1)
        mats = jnp.concatenate([mats_ref[b, k] for k in range(slots)], axis=1)
        near = dot_nt(picked, mats)
        quarter, rest = divmod(b * block, per)
        cols = slice(b * block, (b + 1) * block)
        out_b = near + out[quarter][:, rest : rest + block]
        yield cols, out_b + self_ref[:, cols] * field[:, cols]


def second_kernel(nfields, ncharges, charge_starts, ids_ref, live_ref, *refs):
    field_refs = refs[:nfields]
    charge_refs = list(zip(refs[nfields : nfields + ncharges], charge_starts))
    refs = refs[nfields + ncharges :]
    dir_ref, pre_ref, self_ref, mats_ref, maps_ref, high_ref, low_ref = refs[:7]
    *coupling_refs, res_ref, out_ref, blocks_ref, charges_ref = refs[7:]
    width = high_ref.shape[1]
    rows = pre_ref.shape[0]
    for cols, values in apply_matrix(
        ids_ref, live_ref, field_refs, charge_refs, pre_ref, self_ref, mats_ref, coupling_refs,
        maps_ref, blocks_ref, charges_ref
    ):
        res_ref[:, cols] = values
    res = res_ref[...]
    out_ref[:, :width] = dot_wide(dot_nn, res, high_ref[...], low_ref[...])
    out_ref[:, width:] = put_scalars([row_sum(res * dir_ref[...]), row_sum(res * res)], rows)


def third_kernel(parts, *refs):
    sums = refs[:parts]
    res_ref, dir_ref, keep_ref, diag_ref, high_ref, low_ref, maps_ref = refs[parts : parts + 7]
    next_ref, pre_ref, send_ref, scalars_ref = refs[parts + 7 :]
    width = high_ref.shape[1]
    rows, panels = res_ref.shape
    summed = sums[0][...]
    for ref in sums[1:]:
        summed = summed + ref[...]
    keep = keep_ref[:, width:]
    start_len, first_sq = column(keep, 0), column(keep, 1)
    diag_one, res_sq = column(summed[:, width:], 0), column(summed[:, width:], 1)
    below_sq = jnp.maximum(res_sq - diag_one * diag_one * (2.0 - first_sq), 0.0)
    below_one = jnp.sqrt(below_sq + EPS)
    second_dir = (res_ref[...] - diag_one * dir_ref[...]) / below_one
    proj = (summed[:, :width] - diag_one * keep_ref[:, :width]) / below_one
    pre = diag_ref[...] * second_dir - dot_wide(dot_nt, proj, high_ref[...], low_ref[...])
    field_low = pre.astype(BF)
    next_ref[...] = second_dir
    pre_ref[...] = pre
    send_ref[:, :panels] = field_low
    charge_rows(field_low, maps_ref, send_ref)
    cross = diag_one * (1.0 - first_sq) / below_one
    second_sq = below_sq / (below_one * below_one)
    scalars_ref[...] = put_scalars(
        [start_len, first_sq, diag_one, below_one, cross, second_sq], rows
    )


def fourth_kernel(nfields, ncharges, charge_starts, ids_ref, live_ref, *refs):
    field_refs = refs[:nfields]
    charge_refs = list(zip(refs[nfields : nfields + ncharges], charge_starts))
    refs = refs[nfields + ncharges :]
    dir_ref, next_ref, pre_ref, self_ref, mats_ref, maps_ref = refs[:6]
    *coupling_refs, out_ref, blocks_ref, charges_ref = refs[6:]
    rows = pre_ref.shape[0]
    block = mats_ref.shape[2]
    upper = jnp.zeros((rows, block), F32)
    diag = jnp.zeros((rows, block), F32)
    square = jnp.zeros((rows, block), F32)
    for cols, values in apply_matrix(
        ids_ref, live_ref, field_refs, charge_refs, pre_ref, self_ref, mats_ref, coupling_refs,
        maps_ref, blocks_ref, charges_ref
    ):
        upper = upper + values * dir_ref[:, cols]
        diag = diag + values * next_ref[:, cols]
        square = square + values * values
    scalars = put_scalars([row_sum(upper), row_sum(diag), row_sum(square)], rows)
    for index in range(out_ref.shape[0]):
        out_ref[index] = scalars


def givens_pair(start_len, diag_one, below_one, upper_two, diag_two, below_two):
    radius_one = jnp.sqrt(diag_one * diag_one + below_one * below_one)
    cos_one = diag_one / radius_one
    sin_one = below_one / radius_one
    upper = cos_one * upper_two + sin_one * diag_two
    lower = cos_one * diag_two - sin_one * upper_two
    radius_two = jnp.sqrt(lower * lower + below_two * below_two)
    step_two = lower / radius_two * (-sin_one * start_len) / radius_two
    step_one = (cos_one * start_len - upper * step_two) / radius_one
    return (step_one, step_two)


def last_kernel(sums_ref, scalars_ref, first_ref, second_ref, out_ref):
    summed = jnp.sum(sums_ref[...], axis=0)
    start_len, first_sq, diag_one, below_one, cross, second_sq = [
        column(scalars_ref[...], i) for i in range(6)
    ]
    upper_two, diag_two, res_sq = [column(summed, i) for i in range(3)]
    left_sq = (
        res_sq
        - upper_two * upper_two * (2.0 - first_sq)
        - diag_two * diag_two * (2.0 - second_sq)
        + 2.0 * upper_two * diag_two * cross
    )
    below_two = jnp.sqrt(jnp.maximum(left_sq, 0.0) + EPS)
    step_one, step_two = givens_pair(
        start_len, diag_one, below_one, upper_two, diag_two, below_two
    )
    out_ref[...] = step_one * first_ref[...] + step_two * second_ref[...]


def sum_parts(values, count):
    if count != 8:
        return [lax.psum(values, AXIS)]
    pair = values + swap(values, 1, count)
    return [pair, swap(pair, 2, count), swap(pair, 4, count), swap(pair, 6, count)]


def exchange(send, panels, count):
    if count != 8:
        field, charges = send[:, :panels], send[:, panels:]
        ends = count - 1
        lower = lax.ppermute(field, AXIS, [(i, i + 1) for i in range(ends)])
        upper = lax.ppermute(field, AXIS, [(i + 1, i) for i in range(ends)])
        every = lax.all_gather(charges, AXIS)
        every = every.reshape((count // 2, 2) + charges.shape)
        return [lower, send, upper], [every[:, 0] + every[:, 1]], [0]
    near = swap(send, 1, count)
    rows, long = send.shape
    onward, pair = call(
        "onward", onward_kernel, [((rows, long), BF), ((rows, long - panels), BF)], [send, near]
    )
    two = swap(onward, 2, count)
    four = swap(pair, 4, count)
    six = swap(onward, 6, count)
    return [send, near, two, six], [pair, two, four, six], [0, panels, 0, panels]


def gather_quarters(coupling, quarters, count, early):
    if count != 8 or quarters != 4:
        return [lax.all_gather(coupling, "rhs")], early

    def other(values, mask):
        return lax.ppermute(values, "rhs", [(i, i ^ mask) for i in range(quarters)])

    coupling, early = lax.optimization_barrier((coupling, early))
    far = other(coupling, 2)
    return [coupling, far], early


def finish_quarters(rows, quarters, late):
    if len(rows) == 1:
        return rows, late

    def other(values, mask):
        return lax.ppermute(values, "rhs", [(i, i ^ mask) for i in range(quarters)])

    own, far, late = lax.optimization_barrier((*rows, late))
    return [own, other(own, 1), far, other(far, 1)], late


def nbytes(shape, kind):
    return math.prod(shape) * jnp.dtype(kind).itemsize


def room(*arrays):
    return pltpu.CompilerParams(
        vmem_limit_bytes=sum(nbytes(a.shape, a.dtype) for a in arrays) * 5 // 4 + 4 * 2**20
    )


def call(name, kernel, out_shapes, args, scratch=(), scalars=0, far=()):
    out_shapes = [jax.ShapeDtypeStruct(shape, kind) for shape, kind in out_shapes]
    args = [pltpu.with_memory_space_constraint(x, pltpu.HBM) if i in far else x
            for i, x in enumerate(args)]
    specs = [
        pl.BlockSpec(
            memory_space=pltpu.SMEM if i < scalars else pltpu.HBM if i in far else pltpu.VMEM
        )
        for i in range(len(args))
    ]
    outs = [pl.BlockSpec(memory_space=pltpu.VMEM)] * len(out_shapes)
    held = [x for i, x in enumerate(args) if i not in far]
    held += [x for x in scratch if getattr(x, "memory_space", None) == pltpu.VMEM]
    return pl.pallas_call(
        kernel,
        name=name,
        out_shape=out_shapes,
        in_specs=specs,
        out_specs=outs,
        scratch_shapes=list(scratch),
        compiler_params=room(*held, *out_shapes),
    )(*args)


def on_device(
    rhs_vec,
    self_coef,
    near_mats,
    near_ids,
    near_count,
    interp,
    skel_idx,
    coupling,
    diag_prec,
    low_rank,
):
    rows, panels = rhs_vec.shape
    block_count, slots, block, _ = near_mats.shape
    skeletons = coupling.shape[0]
    quarters = lax.axis_size("rhs")
    count = lax.axis_size(AXIS)
    width = low_rank.shape[1]
    region = lax.axis_index(AXIS)
    (maps,) = call(
        "maps",
        maps_kernel,
        [((quarters, 2 * LANES, panels // quarters), BF)],
        [jnp.swapaxes(interp, 1, 2), skel_idx],
    )
    wide = width + LANES
    long = panels + quarters * LANES

    parts = 4
    payload, rhs_near, diag_row, self_row = call(
        "open",
        lambda *refs: open_kernel(parts, *refs),
        [((rows, wide), F32), ((rows, panels), F32), ((1, panels), F32), ((1, panels), F32)],
        [rhs_vec, low_rank, diag_prec[None, :], self_coef[None, :]],
        [pltpu.VMEM((panels, width), F32), pltpu.SemaphoreType.DMA((parts + 3,))],
        far=(0, 1, 2, 3),
    )

    some_rows, payload = gather_quarters(coupling[:, 0, :], quarters, count, payload)
    sums = sum_parts(payload, count)
    first_dir, first_pre, send, keep, high, low = call(
        "first",
        lambda *refs: first_kernel(len(sums), *refs),
        [((rows, panels), F32), ((rows, panels), F32), ((rows, long), BF), ((rows, wide), F32),
         (low_rank.shape, BF), (low_rank.shape, BF)],
        [*sums, rhs_near, diag_row, low_rank, maps],
    )
    full_rows, send = finish_quarters(some_rows, quarters, send)
    fields, charges, starts = exchange(send, panels, count)
    nf, nc = len(fields), len(charges)
    scratch = [
        pltpu.VMEM((nf * block_count + 1, rows, block), BF),
        pltpu.VMEM((quarters, count // 2, rows, LANES), BF),
    ]
    residue, payload = call(
        "second",
        lambda *refs: second_kernel(nf, nc, starts, *refs),
        [((rows, panels), F32), ((rows, wide), F32)],
        [near_ids, near_count, *fields, *charges, first_dir, first_pre, self_row, near_mats, maps,
         high, low, *full_rows],
        scratch,
        2,
    )
    sums = sum_parts(payload, count)
    second_dir, second_pre, send, scalars = call(
        "third",
        lambda *refs: third_kernel(len(sums), *refs),
        [((rows, panels), F32), ((rows, panels), F32), ((rows, long), BF), ((rows, LANES), F32)],
        [*sums, residue, first_dir, keep, diag_row, high, low, maps],
    )
    fields, charges, starts = exchange(send, panels, count)
    (tails,) = call(
        "fourth",
        lambda *refs: fourth_kernel(nf, nc, starts, *refs),
        [((count if count == 8 else 1, rows, LANES), F32)],
        [near_ids, near_count, *fields, *charges, first_dir, second_dir, second_pre,
         self_row, near_mats, maps, *full_rows],
        scratch,
        2,
    )
    tails = lax.all_to_all(tails, AXIS, 0, 0) if count == 8 else lax.psum(tails, AXIS)
    (result,) = call("last", last_kernel, [((rows, panels), F32)], [tails, scalars, first_pre, second_pre])
    return result


def solution(mesh):
    placed = (
        P("rhs", "space"),
        P("space"),
        P("space", None, None, None),
        P("space", None),
        P("space"),
        P("space", None, None),
        P("space", None),
        P("space", "rhs", None),
        P("space"),
        P("space", None),
    )
    return jax.shard_map(
        on_device, mesh=mesh, in_specs=placed, out_specs=P("rhs", "space"), check_vma=False
    )
```

```python
import math

import jax
import jax.numpy as jnp
from jax import lax
from jax.experimental import pallas as pl
from jax.experimental.pallas import tpu as pltpu
from jax.sharding import PartitionSpec as P

EPS = 1e-06
F32 = jnp.float32
BF = jnp.bfloat16
AXIS = "space"
LANES = 128
HALF = 64


def swap(values, mask, count):
    return lax.ppermute(values, AXIS, [(i, i ^ mask) for i in range(count)])


def split(values):
    high = values.astype(BF)
    return high, (values - high.astype(F32)).astype(BF)


def dot_nn(left, right):
    return lax.dot_general(left, right, (((1,), (0,)), ((), ())), preferred_element_type=F32)


def dot_nt(left, right):
    return lax.dot_general(left, right, (((1,), (1,)), ((), ())), preferred_element_type=F32)


def dot_wide(dot, vector, high, low):
    rows = vector.shape[0]
    vec_high, vec_low = split(vector)
    first = dot(jnp.concatenate([vec_high, vec_low], axis=0), high)
    return first[:rows] + first[rows:] + dot(vec_high, low)


def row_sum(values):
    return jnp.sum(values, axis=1, keepdims=True)


def put_scalars(columns, rows):
    lane = lax.broadcasted_iota(jnp.int32, (rows, LANES), 1)
    out = jnp.zeros((rows, LANES), F32)
    for index, column in enumerate(columns):
        out = jnp.where(lane == index, column, out)
    return out


def column(values, index):
    return values[:, index : index + 1]


def charge_rows(field_low, maps_ref, send_ref):
    rows, panels = field_low.shape
    quarters, _, width = maps_ref.shape
    for quarter in range(quarters):
        both = dot_nt(field_low[:, quarter * width : (quarter + 1) * width], maps_ref[quarter])
        start = panels + quarter * LANES
        send_ref[:, start : start + LANES] = (both[:, :LANES] + both[:, LANES:]).astype(BF)


def maps_kernel(weights_ref, skel_ref, maps_ref):
    block_count, rank, block = weights_ref.shape
    quarters = maps_ref.shape[0]
    per = block_count // quarters
    odd_start = pl.multiple_of((lax.axis_index(AXIS) % 2) * HALF, HALF)
    maps_ref[...] = jnp.zeros(maps_ref.shape, BF)
    skel = jnp.concatenate(
        [skel_ref[...].astype(F32), jnp.zeros((block_count, LANES - rank), F32)], axis=1
    ).T
    panel = lax.broadcasted_iota(jnp.int32, (rank, block), 1).astype(F32)
    for b in range(block_count):
        quarter, index = divmod(b, per)
        start = odd_start + index * rank
        cols = slice(index * block, (index + 1) * block)
        hot = jnp.where(skel[:rank, b : b + 1] == panel, 1.0, 0.0).astype(BF)
        maps_ref[quarter, pl.ds(start, rank), cols] = hot
        maps_ref[quarter, pl.ds(start + LANES, rank), cols] = weights_ref[b]


def onward_kernel(send_ref, near_ref, onward_ref, pair_ref):
    panels = near_ref.shape[1] - pair_ref.shape[1]
    pair = send_ref[:, panels:] + near_ref[:, panels:]
    onward_ref[:, :panels] = near_ref[:, :panels]
    onward_ref[:, panels:] = pair
    pair_ref[...] = pair


def open_kernel(parts, rhs_hbm, factor_hbm, diag_hbm, self_hbm, out_ref, rhs_ref, diag_ref,
                self_ref, held_ref, sems):
    panels, width = factor_hbm.shape
    rows = rhs_ref.shape[0]
    depth = panels // parts
    loads = [
        pltpu.make_async_copy(source, target, sems.at[parts + index])
        for index, (source, target) in enumerate(
            [(rhs_hbm, rhs_ref), (diag_hbm, diag_ref), (self_hbm, self_ref)]
        )
    ]
    for load in loads:
        load.start()
    copies = []
    for part in range(parts):
        span = pl.ds(part * depth, depth)
        copies.append(
            pltpu.make_async_copy(factor_hbm.at[span], held_ref.at[span], sems.at[part])
        )
        copies[-1].start()
    loads[0].wait()
    rhs = rhs_ref[...]
    out_ref[:, width:] = put_scalars([row_sum(rhs * rhs)], rows)
    total = jnp.zeros((rows, width), F32)
    for part in range(parts):
        span = slice(part * depth, (part + 1) * depth)
        copies[part].wait()
        high, low = split(held_ref[span, :])
        total = total + dot_wide(dot_nn, rhs[:, span], high, low)
    out_ref[:, :width] = total
    for load in loads[1:]:
        load.wait()


def first_kernel(parts, *refs):
    sums = refs[:parts]
    rhs_ref, diag_ref, factor_ref, maps_ref = refs[parts : parts + 4]
    dir_ref, pre_ref, send_ref, keep_ref, high_ref, low_ref = refs[parts + 4 :]
    width = factor_ref.shape[1]
    high_ref[...], low_ref[...] = split(factor_ref[...])
    rows, panels = rhs_ref.shape
    summed = sums[0][...]
    for ref in sums[1:]:
        summed = summed + ref[...]
    rhs_sq = column(summed[:, width:], 0)
    start_len = jnp.sqrt(rhs_sq + EPS)
    first_dir = rhs_ref[...] / start_len
    proj = summed[:, :width] / start_len
    first_pre = diag_ref[...] * first_dir - dot_wide(dot_nt, proj, high_ref[...], low_ref[...])
    field_low = first_pre.astype(BF)
    dir_ref[...] = first_dir
    pre_ref[...] = first_pre
    send_ref[:, :panels] = field_low
    charge_rows(field_low, maps_ref, send_ref)
    keep_ref[:, :width] = proj
    keep_ref[:, width:] = put_scalars([start_len, rhs_sq / (start_len * start_len)], rows)


def block_place(wanted, live, block_count, sources, region):
    source = wanted // block_count
    if sources == 4:
        slot = jnp.where(
            source == region,
            0,
            jnp.where(source == region ^ 1, 1, jnp.where(source == region ^ 3, 2, 3)),
        )
    else:
        slot = source - region + 1
    return jnp.where(live, slot * block_count + wanted % block_count, sources * block_count)


def near_kernel(sources, ids_ref, live_ref, *refs):
    field_refs = refs[:sources]
    mats_ref, near_ref, blocks_ref = refs[sources:]
    rows, panels = near_ref.shape
    block_count, slots, block, _ = mats_ref.shape
    region = lax.axis_index(AXIS)
    for index, ref in enumerate(field_refs):
        for b in range(block_count):
            blocks_ref[index * block_count + b] = ref[:, b * block : (b + 1) * block]
    blocks_ref[sources * block_count] = jnp.zeros((rows, block), BF)
    for b in range(block_count):
        places = [
            block_place(ids_ref[b, k], k < live_ref[b], block_count, sources, region)
            for k in range(slots)
        ]
        picked = jnp.concatenate([blocks_ref[place] for place in places], axis=1)
        mats = jnp.concatenate([mats_ref[b, k] for k in range(slots)], axis=1)
        near_ref[:, b * block : (b + 1) * block] = dot_nt(picked, mats)


def apply_matrix(field_ref, self_ref, near_ref, charge_refs, coupling_refs, maps_ref, charges_ref):
    rows, panels = field_ref.shape
    quarters, pairs = charges_ref.shape[:2]
    gathered = len(coupling_refs) == 1
    region = lax.axis_index(AXIS)
    first_quarter = 0 if gathered else lax.axis_index("rhs")
    for quarter in range(quarters):
        for index in range(pairs):
            if len(charge_refs) == pairs:
                ref, start = charge_refs[index]
                start += quarter * LANES
                charge = ref[:, start : start + LANES]
                charges_ref[quarter, (region // 2) ^ index] = charge
            else:
                lanes = slice(quarter * LANES, (quarter + 1) * LANES)
                charges_ref[quarter, index] = charge_refs[0][0][index, :, lanes]
    far = jnp.zeros((rows, coupling_refs[0].shape[-2]), F32)
    for index in range(quarters):
        quarter = first_quarter ^ index
        charge = jnp.concatenate([charges_ref[quarter, t] for t in range(pairs)], axis=1)
        rows_in = coupling_refs[0][index] if gathered else coupling_refs[index][...]
        far = far + dot_nt(charge, rows_in)
    odd = (region % 2) == 1
    per = panels // quarters
    for quarter in range(quarters):
        start = (quarter // 2) * LANES
        chunk = far[:, start : start + LANES]
        turned = pltpu.roll(chunk, HALF, 1)
        chunk = jnp.where(odd, turned, chunk) if quarter % 2 == 0 else jnp.where(odd, chunk, turned)
        high, low = split(chunk)
        both = jnp.concatenate([high, low], axis=0)
        pot = dot_nn(jnp.concatenate([both, both], axis=1), maps_ref[quarter])
        cols = slice(quarter * per, (quarter + 1) * per)
        near = near_ref[:, cols] + (pot[:rows] + pot[rows:])
        yield cols, near + self_ref[:, cols] * field_ref[:, cols]


def second_kernel(charge_starts, *refs):
    parts = len(charge_starts)
    charge_refs = list(zip(refs[:parts], charge_starts))
    dir_ref, pre_ref, self_ref, near_ref, maps_ref, high_ref, low_ref = refs[parts : parts + 7]
    *coupling_refs, res_ref, out_ref, charges_ref = refs[parts + 7 :]
    width = high_ref.shape[1]
    rows = pre_ref.shape[0]
    for cols, values in apply_matrix(
        pre_ref, self_ref, near_ref, charge_refs, coupling_refs, maps_ref, charges_ref
    ):
        res_ref[:, cols] = values
    res = res_ref[...]
    out_ref[:, :width] = dot_wide(dot_nn, res, high_ref[...], low_ref[...])
    out_ref[:, width:] = put_scalars([row_sum(res * dir_ref[...]), row_sum(res * res)], rows)


def third_kernel(parts, *refs):
    sums = refs[:parts]
    res_ref, dir_ref, keep_ref, diag_ref, high_ref, low_ref, maps_ref = refs[parts : parts + 7]
    next_ref, pre_ref, send_ref, scalars_ref = refs[parts + 7 :]
    width = high_ref.shape[1]
    rows, panels = res_ref.shape
    summed = sums[0][...]
    for ref in sums[1:]:
        summed = summed + ref[...]
    keep = keep_ref[:, width:]
    start_len, first_sq = column(keep, 0), column(keep, 1)
    diag_one, res_sq = column(summed[:, width:], 0), column(summed[:, width:], 1)
    below_sq = jnp.maximum(res_sq - diag_one * diag_one * (2.0 - first_sq), 0.0)
    below_one = jnp.sqrt(below_sq + EPS)
    second_dir = (res_ref[...] - diag_one * dir_ref[...]) / below_one
    proj = (summed[:, :width] - diag_one * keep_ref[:, :width]) / below_one
    pre = diag_ref[...] * second_dir - dot_wide(dot_nt, proj, high_ref[...], low_ref[...])
    field_low = pre.astype(BF)
    next_ref[...] = second_dir
    pre_ref[...] = pre
    send_ref[:, :panels] = field_low
    charge_rows(field_low, maps_ref, send_ref)
    cross = diag_one * (1.0 - first_sq) / below_one
    second_sq = below_sq / (below_one * below_one)
    scalars_ref[...] = put_scalars(
        [start_len, first_sq, diag_one, below_one, cross, second_sq], rows
    )


def fourth_kernel(charge_starts, *refs):
    parts = len(charge_starts)
    charge_refs = list(zip(refs[:parts], charge_starts))
    dir_ref, next_ref, pre_ref, self_ref, near_ref, maps_ref = refs[parts : parts + 6]
    *coupling_refs, out_ref, charges_ref = refs[parts + 6 :]
    rows = pre_ref.shape[0]
    upper = diag = square = 0.0
    for cols, values in apply_matrix(
        pre_ref, self_ref, near_ref, charge_refs, coupling_refs, maps_ref, charges_ref
    ):
        upper = upper + row_sum(values * dir_ref[:, cols])
        diag = diag + row_sum(values * next_ref[:, cols])
        square = square + row_sum(values * values)
    out_ref[...] = put_scalars([upper, diag, square], rows)


def givens_pair(start_len, diag_one, below_one, upper_two, diag_two, below_two):
    radius_one = jnp.sqrt(diag_one * diag_one + below_one * below_one)
    cos_one = diag_one / radius_one
    sin_one = below_one / radius_one
    upper = cos_one * upper_two + sin_one * diag_two
    lower = cos_one * diag_two - sin_one * upper_two
    radius_two = jnp.sqrt(lower * lower + below_two * below_two)
    step_two = lower / radius_two * (-sin_one * start_len) / radius_two
    step_one = (cos_one * start_len - upper * step_two) / radius_one
    return (step_one, step_two)


def last_kernel(parts, *refs):
    scalars_ref, first_ref, second_ref, out_ref = refs[parts:]
    summed = refs[0][...]
    for ref in refs[1:parts]:
        summed = summed + ref[...]
    start_len, first_sq, diag_one, below_one, cross, second_sq = [
        column(scalars_ref[...], i) for i in range(6)
    ]
    upper_two, diag_two, res_sq = [column(summed, i) for i in range(3)]
    left_sq = (
        res_sq
        - upper_two * upper_two * (2.0 - first_sq)
        - diag_two * diag_two * (2.0 - second_sq)
        + 2.0 * upper_two * diag_two * cross
    )
    below_two = jnp.sqrt(jnp.maximum(left_sq, 0.0) + EPS)
    step_one, step_two = givens_pair(
        start_len, diag_one, below_one, upper_two, diag_two, below_two
    )
    out_ref[...] = step_one * first_ref[...] + step_two * second_ref[...]


def sum_parts(values, count):
    if count != 8:
        return [lax.psum(values, AXIS)]
    pair = values + swap(values, 1, count)
    return [pair, swap(pair, 2, count), swap(pair, 4, count), swap(pair, 6, count)]


def exchange(send, panels, count):
    if count != 8:
        field, charges = send[:, :panels], send[:, panels:]
        ends = count - 1
        lower = lax.ppermute(field, AXIS, [(i, i + 1) for i in range(ends)])
        upper = lax.ppermute(field, AXIS, [(i + 1, i) for i in range(ends)])
        every = lax.all_gather(charges, AXIS)
        every = every.reshape((count // 2, 2) + charges.shape)
        return [lower, send, upper], [every[:, 0] + every[:, 1]], [0]
    near = swap(send, 1, count)
    rows, long = send.shape
    onward, pair = call(
        "onward", onward_kernel, [((rows, long), BF), ((rows, long - panels), BF)], [send, near]
    )
    two = swap(onward, 2, count)
    four = swap(pair, 4, count)
    six = swap(onward, 6, count)
    return [send, near, two, six], [pair, two, four, six], [0, panels, 0, panels]


def gather_quarters(coupling, quarters, count, early):
    if count != 8 or quarters != 4:
        return [lax.all_gather(coupling, "rhs")], early
    coupling, early = lax.optimization_barrier((coupling, early))
    return [coupling, lax.ppermute(coupling, "rhs", [(i, i ^ 2) for i in range(quarters)])], early


def finish_quarters(rows, quarters, late):
    if len(rows) == 1:
        return rows, late
    own, far, late = lax.optimization_barrier((*rows, late))
    near, other = [lax.ppermute(x, "rhs", [(i, i ^ 1) for i in range(quarters)]) for x in (own, far)]
    return [own, near, far, other], late


def nbytes(shape, kind):
    return math.prod(shape) * jnp.dtype(kind).itemsize


def room(*arrays):
    return pltpu.CompilerParams(
        vmem_limit_bytes=sum(nbytes(a.shape, a.dtype) for a in arrays) * 5 // 4 + 4 * 2**20
    )


def call(name, kernel, out_shapes, args, scratch=(), scalars=0, far=()):
    out_shapes = [jax.ShapeDtypeStruct(shape, kind) for shape, kind in out_shapes]
    args = [pltpu.with_memory_space_constraint(x, pltpu.HBM) if i in far else x
            for i, x in enumerate(args)]
    specs = [
        pl.BlockSpec(
            memory_space=pltpu.SMEM if i < scalars else pltpu.HBM if i in far else pltpu.VMEM
        )
        for i in range(len(args))
    ]
    outs = [pl.BlockSpec(memory_space=pltpu.VMEM)] * len(out_shapes)
    held = [x for i, x in enumerate(args) if i not in far]
    held += [x for x in scratch if getattr(x, "memory_space", None) == pltpu.VMEM]
    return pl.pallas_call(
        kernel,
        name=name,
        out_shape=out_shapes,
        in_specs=specs,
        out_specs=outs,
        scratch_shapes=list(scratch),
        compiler_params=room(*held, *out_shapes),
    )(*args)


def on_device(
    rhs_vec,
    self_coef,
    near_mats,
    near_ids,
    near_count,
    interp,
    skel_idx,
    coupling,
    diag_prec,
    low_rank,
):
    rows, panels = rhs_vec.shape
    block_count, slots, block, _ = near_mats.shape
    skeletons = coupling.shape[0]
    quarters = lax.axis_size("rhs")
    count = lax.axis_size(AXIS)
    width = low_rank.shape[1]
    region = lax.axis_index(AXIS)
    (maps,) = call(
        "maps",
        maps_kernel,
        [((quarters, 2 * LANES, panels // quarters), BF)],
        [jnp.swapaxes(interp, 1, 2), skel_idx],
    )
    wide = width + LANES
    long = panels + quarters * LANES

    parts = 4
    payload, rhs_near, diag_row, self_row = call(
        "open",
        lambda *refs: open_kernel(parts, *refs),
        [((rows, wide), F32), ((rows, panels), F32), ((1, panels), F32), ((1, panels), F32)],
        [rhs_vec, low_rank, diag_prec[None, :], self_coef[None, :]],
        [pltpu.VMEM((panels, width), F32), pltpu.SemaphoreType.DMA((parts + 3,))],
        far=(0, 1, 2, 3),
    )

    some_rows, payload = gather_quarters(coupling[:, 0, :], quarters, count, payload)
    sums = sum_parts(payload, count)
    first_dir, first_pre, send, keep, high, low = call(
        "first",
        lambda *refs: first_kernel(len(sums), *refs),
        [((rows, panels), F32), ((rows, panels), F32), ((rows, long), BF), ((rows, wide), F32),
         (low_rank.shape, BF), (low_rank.shape, BF)],
        [*sums, rhs_near, diag_row, low_rank, maps],
    )
    full_rows, send = finish_quarters(some_rows, quarters, send)
    fields, charges, starts = exchange(send, panels, count)

    def near_product(fields):
        (near,) = call(
            "near",
            lambda *refs: near_kernel(len(fields), *refs),
            [((rows, panels), F32)],
            [near_ids, near_count, *fields, near_mats],
            [pltpu.VMEM((len(fields) * block_count + 1, rows, block), BF)],
            2,
        )
        return near

    near = near_product(fields)
    scratch = [pltpu.VMEM((quarters, count // 2, rows, LANES), BF)]
    residue, payload = call(
        "second",
        lambda *refs: second_kernel(starts, *refs),
        [((rows, panels), F32), ((rows, wide), F32)],
        [*charges, first_dir, first_pre, self_row, near, maps, high, low, *full_rows],
        scratch,
    )
    sums = sum_parts(payload, count)
    second_dir, second_pre, send, scalars = call(
        "third",
        lambda *refs: third_kernel(len(sums), *refs),
        [((rows, panels), F32), ((rows, panels), F32), ((rows, long), BF), ((rows, LANES), F32)],
        [*sums, residue, first_dir, keep, diag_row, high, low, maps],
    )
    fields, charges, starts = exchange(send, panels, count)
    near = near_product(fields)
    (tail,) = call(
        "fourth",
        lambda *refs: fourth_kernel(starts, *refs),
        [((rows, LANES), F32)],
        [*charges, first_dir, second_dir, second_pre, self_row, near, maps, *full_rows],
        scratch,
    )
    sums = sum_parts(tail, count)
    (result,) = call(
        "last",
        lambda *refs: last_kernel(len(sums), *refs),
        [((rows, panels), F32)],
        [*sums, scalars, first_pre, second_pre],
    )
    return result


def solution(mesh):
    placed = (
        P("rhs", "space"),
        P("space"),
        P("space", None, None, None),
        P("space", None),
        P("space"),
        P("space", None, None),
        P("space", None),
        P("space", "rhs", None),
        P("space"),
        P("space", None),
    )
    return jax.shard_map(
        on_device, mesh=mesh, in_specs=placed, out_specs=P("rhs", "space"), check_vma=False
    )
```

```python
import math

import jax
import jax.numpy as jnp
from jax import lax
from jax.experimental import pallas as pl
from jax.experimental.pallas import tpu as pltpu
from jax.sharding import PartitionSpec as P

EPS = 1e-06
F32 = jnp.float32
BF = jnp.bfloat16
AXIS = "space"
LANES = 128
HALF = 64


def swap(values, mask, count):
    return lax.ppermute(values, AXIS, [(i, i ^ mask) for i in range(count)])


def split(values):
    high = values.astype(BF)
    return high, (values - high.astype(F32)).astype(BF)


def dot_nn(left, right):
    return lax.dot_general(left, right, (((1,), (0,)), ((), ())), preferred_element_type=F32)


def dot_nt(left, right):
    return lax.dot_general(left, right, (((1,), (1,)), ((), ())), preferred_element_type=F32)


def dot_wide(dot, vector, high, low):
    rows = vector.shape[0]
    vec_high, vec_low = split(vector)
    first = dot(jnp.concatenate([vec_high, vec_low], axis=0), high)
    return first[:rows] + first[rows:] + dot(vec_high, low)


def row_sum(values):
    return jnp.sum(values, axis=1, keepdims=True)


def put_scalars(columns, rows):
    lane = lax.broadcasted_iota(jnp.int32, (rows, LANES), 1)
    out = jnp.zeros((rows, LANES), F32)
    for index, column in enumerate(columns):
        out = jnp.where(lane == index, column, out)
    return out


def column(values, index):
    return values[:, index : index + 1]


def charge_rows(field_low, maps_ref, send_ref):
    rows, panels = field_low.shape
    quarters, _, width = maps_ref.shape
    for quarter in range(quarters):
        both = dot_nt(field_low[:, quarter * width : (quarter + 1) * width], maps_ref[quarter])
        start = panels + quarter * LANES
        send_ref[:, start : start + LANES] = (both[:, :LANES] + both[:, LANES:]).astype(BF)


def maps_kernel(sources, ids_ref, live_ref, weights_ref, skel_ref, maps_ref, places_ref):
    block_count, rank, block = weights_ref.shape
    quarters = maps_ref.shape[0]
    per = block_count // quarters
    odd_start = pl.multiple_of((lax.axis_index(AXIS) % 2) * HALF, HALF)
    maps_ref[...] = jnp.zeros(maps_ref.shape, BF)
    skel = jnp.concatenate(
        [skel_ref[...].astype(F32), jnp.zeros((block_count, LANES - rank), F32)], axis=1
    ).T
    panel = lax.broadcasted_iota(jnp.int32, (rank, block), 1).astype(F32)
    for b in range(block_count):
        quarter, index = divmod(b, per)
        start = odd_start + index * rank
        cols = slice(index * block, (index + 1) * block)
        hot = jnp.where(skel[:rank, b : b + 1] == panel, 1.0, 0.0).astype(BF)
        maps_ref[quarter, pl.ds(start, rank), cols] = hot
        maps_ref[quarter, pl.ds(start + LANES, rank), cols] = weights_ref[b]
    wanted = ids_ref[...]
    slots = wanted.shape[1]
    slot = lax.broadcasted_iota(jnp.int32, wanted.shape, 1)
    row = lax.broadcasted_iota(jnp.int32, wanted.shape, 0)
    counts = live_ref[...]
    live = slot < 0
    for b in range(block_count):
        live = live | ((row == b) & (slot < counts[0, b]))
    region = lax.axis_index(AXIS)
    place = block_place(wanted, live, block_count, sources, region).astype(F32)
    scale = jnp.where(slot % 4 == 0, 1.0, jnp.where(slot % 4 == 1, 64.0, 4096.0))
    scale = jnp.where(slot % 4 == 3, 262144.0, scale)
    lane = lax.broadcasted_iota(jnp.int32, (block_count, LANES), 1)
    packed = jnp.zeros((block_count, LANES), F32)
    for group in range(slots // 4):
        part = row_sum(jnp.where(slot // 4 == group, place * scale, 0.0))
        packed = jnp.where(lane == group, part, packed)
    places_ref[...] = packed.astype(jnp.int32)


def onward_kernel(send_ref, near_ref, onward_ref, pair_ref):
    panels = near_ref.shape[1] - pair_ref.shape[1]
    pair = send_ref[:, panels:] + near_ref[:, panels:]
    onward_ref[:, :panels] = near_ref[:, :panels]
    onward_ref[:, panels:] = pair
    pair_ref[...] = pair


def open_kernel(parts, rhs_hbm, factor_hbm, diag_hbm, self_hbm, out_ref, rhs_ref, diag_ref,
                self_ref, high_ref, low_ref, held_ref, sems):
    panels, width = factor_hbm.shape
    rows = rhs_ref.shape[0]
    depth = panels // parts
    loads = [
        pltpu.make_async_copy(source, target, sems.at[parts + index])
        for index, (source, target) in enumerate(
            [(rhs_hbm, rhs_ref), (diag_hbm, diag_ref), (self_hbm, self_ref)]
        )
    ]
    for load in loads:
        load.start()
    copies = []
    for part in range(parts):
        span = pl.ds(part * depth, depth)
        copies.append(
            pltpu.make_async_copy(factor_hbm.at[span], held_ref.at[span], sems.at[part])
        )
        copies[-1].start()
    loads[0].wait()
    rhs = rhs_ref[...]
    out_ref[:, width:] = put_scalars([row_sum(rhs * rhs)], rows)
    total = jnp.zeros((rows, width), F32)
    for part in range(parts):
        span = slice(part * depth, (part + 1) * depth)
        copies[part].wait()
        high, low = split(held_ref[span, :])
        high_ref[span, :] = high
        low_ref[span, :] = low
        total = total + dot_wide(dot_nn, rhs[:, span], high, low)
    out_ref[:, :width] = total
    for load in loads[1:]:
        load.wait()


def first_kernel(parts, *refs):
    sums = refs[:parts]
    rhs_ref, diag_ref, high_ref, low_ref, maps_ref = refs[parts : parts + 5]
    dir_ref, pre_ref, send_ref, keep_ref = refs[parts + 5 :]
    width = high_ref.shape[1]
    rows, panels = rhs_ref.shape
    summed = sums[0][...]
    for ref in sums[1:]:
        summed = summed + ref[...]
    rhs_sq = column(summed[:, width:], 0)
    start_len = jnp.sqrt(rhs_sq + EPS)
    first_dir = rhs_ref[...] / start_len
    proj = summed[:, :width] / start_len
    first_pre = diag_ref[...] * first_dir - dot_wide(dot_nt, proj, high_ref[...], low_ref[...])
    field_low = first_pre.astype(BF)
    dir_ref[...] = first_dir
    pre_ref[...] = first_pre
    send_ref[:, :panels] = field_low
    charge_rows(field_low, maps_ref, send_ref)
    keep_ref[:, :width] = proj
    keep_ref[:, width:] = put_scalars([start_len, rhs_sq / (start_len * start_len)], rows)


def block_place(wanted, live, block_count, sources, region):
    source = wanted // block_count
    if sources == 4:
        slot = jnp.where(
            source == region,
            0,
            jnp.where(source == region ^ 1, 1, jnp.where(source == region ^ 3, 2, 3)),
        )
    else:
        slot = source - region + 1
    return jnp.where(live, slot * block_count + wanted % block_count, sources * block_count)


def near_kernel(sources, *refs):
    field_refs = refs[:sources]
    places_ref, mats_ref, near_ref, blocks_ref = refs[sources:]
    rows, panels = near_ref.shape
    block_count, slots, block, _ = mats_ref.shape
    packed = places_ref[...]
    for index, ref in enumerate(field_refs):
        for b in range(block_count):
            blocks_ref[index * block_count + b] = ref[:, b * block : (b + 1) * block]
    blocks_ref[sources * block_count] = jnp.zeros((rows, block), BF)
    for b in range(block_count):
        fours = [packed[b, group] for group in range(slots // 4)]
        places = [(fours[k // 4] >> (6 * (k % 4))) & 63 for k in range(slots)]
        picked = jnp.concatenate([blocks_ref[place] for place in places], axis=1)
        mats = jnp.concatenate([mats_ref[b, k] for k in range(slots)], axis=1)
        near_ref[:, b * block : (b + 1) * block] = dot_nt(picked, mats)


def apply_matrix(field_ref, self_ref, near_ref, charge_refs, coupling_refs, maps_ref, charges_ref):
    rows, panels = field_ref.shape
    quarters, pairs = charges_ref.shape[:2]
    gathered = len(coupling_refs) == 1
    region = lax.axis_index(AXIS)
    first_quarter = 0 if gathered else lax.axis_index("rhs")
    for quarter in range(quarters):
        for index in range(pairs):
            if len(charge_refs) == pairs:
                ref, start = charge_refs[index]
                start += quarter * LANES
                charge = ref[:, start : start + LANES]
                charges_ref[quarter, (region // 2) ^ index] = charge
            else:
                lanes = slice(quarter * LANES, (quarter + 1) * LANES)
                charges_ref[quarter, index] = charge_refs[0][0][index, :, lanes]
    far = jnp.zeros((rows, coupling_refs[0].shape[-2]), F32)
    for index in range(quarters):
        quarter = first_quarter ^ index
        charge = jnp.concatenate([charges_ref[quarter, t] for t in range(pairs)], axis=1)
        rows_in = coupling_refs[0][index] if gathered else coupling_refs[index][...]
        far = far + dot_nt(charge, rows_in)
    odd = (region % 2) == 1
    per = panels // quarters
    for quarter in range(quarters):
        start = (quarter // 2) * LANES
        chunk = far[:, start : start + LANES]
        turned = pltpu.roll(chunk, HALF, 1)
        chunk = jnp.where(odd, turned, chunk) if quarter % 2 == 0 else jnp.where(odd, chunk, turned)
        high, low = split(chunk)
        both = jnp.concatenate([high, low], axis=0)
        pot = dot_nn(jnp.concatenate([both, both], axis=1), maps_ref[quarter])
        cols = slice(quarter * per, (quarter + 1) * per)
        near = near_ref[:, cols] + (pot[:rows] + pot[rows:])
        yield cols, near + self_ref[:, cols] * field_ref[:, cols]


def second_kernel(charge_starts, *refs):
    parts = len(charge_starts)
    charge_refs = list(zip(refs[:parts], charge_starts))
    dir_ref, pre_ref, self_ref, near_ref, maps_ref, high_ref, low_ref = refs[parts : parts + 7]
    *coupling_refs, res_ref, out_ref, charges_ref = refs[parts + 7 :]
    width = high_ref.shape[1]
    rows = pre_ref.shape[0]
    for cols, values in apply_matrix(
        pre_ref, self_ref, near_ref, charge_refs, coupling_refs, maps_ref, charges_ref
    ):
        res_ref[:, cols] = values
    res = res_ref[...]
    out_ref[:, :width] = dot_wide(dot_nn, res, high_ref[...], low_ref[...])
    out_ref[:, width:] = put_scalars([row_sum(res * dir_ref[...]), row_sum(res * res)], rows)


def third_kernel(parts, *refs):
    sums = refs[:parts]
    res_ref, dir_ref, keep_ref, diag_ref, high_ref, low_ref, maps_ref = refs[parts : parts + 7]
    next_ref, pre_ref, send_ref, scalars_ref = refs[parts + 7 :]
    width = high_ref.shape[1]
    rows, panels = res_ref.shape
    summed = sums[0][...]
    for ref in sums[1:]:
        summed = summed + ref[...]
    keep = keep_ref[:, width:]
    start_len, first_sq = column(keep, 0), column(keep, 1)
    diag_one, res_sq = column(summed[:, width:], 0), column(summed[:, width:], 1)
    below_sq = jnp.maximum(res_sq - diag_one * diag_one * (2.0 - first_sq), 0.0)
    below_one = jnp.sqrt(below_sq + EPS)
    second_dir = (res_ref[...] - diag_one * dir_ref[...]) / below_one
    proj = (summed[:, :width] - diag_one * keep_ref[:, :width]) / below_one
    pre = diag_ref[...] * second_dir - dot_wide(dot_nt, proj, high_ref[...], low_ref[...])
    field_low = pre.astype(BF)
    next_ref[...] = second_dir
    pre_ref[...] = pre
    send_ref[:, :panels] = field_low
    charge_rows(field_low, maps_ref, send_ref)
    cross = diag_one * (1.0 - first_sq) / below_one
    second_sq = below_sq / (below_one * below_one)
    scalars_ref[...] = put_scalars(
        [start_len, first_sq, diag_one, below_one, cross, second_sq], rows
    )


def fourth_kernel(charge_starts, *refs):
    parts = len(charge_starts)
    charge_refs = list(zip(refs[:parts], charge_starts))
    dir_ref, next_ref, pre_ref, self_ref, near_ref, maps_ref = refs[parts : parts + 6]
    *coupling_refs, out_ref, charges_ref = refs[parts + 6 :]
    rows = pre_ref.shape[0]
    upper = diag = square = 0.0
    for cols, values in apply_matrix(
        pre_ref, self_ref, near_ref, charge_refs, coupling_refs, maps_ref, charges_ref
    ):
        upper = upper + row_sum(values * dir_ref[:, cols])
        diag = diag + row_sum(values * next_ref[:, cols])
        square = square + row_sum(values * values)
    out_ref[...] = put_scalars([upper, diag, square], rows)


def givens_pair(start_len, diag_one, below_one, upper_two, diag_two, below_two):
    radius_one = jnp.sqrt(diag_one * diag_one + below_one * below_one)
    cos_one = diag_one / radius_one
    sin_one = below_one / radius_one
    upper = cos_one * upper_two + sin_one * diag_two
    lower = cos_one * diag_two - sin_one * upper_two
    radius_two = jnp.sqrt(lower * lower + below_two * below_two)
    step_two = lower / radius_two * (-sin_one * start_len) / radius_two
    step_one = (cos_one * start_len - upper * step_two) / radius_one
    return (step_one, step_two)


def last_kernel(parts, *refs):
    scalars_ref, first_ref, second_ref, out_ref = refs[parts:]
    summed = refs[0][...]
    for ref in refs[1:parts]:
        summed = summed + ref[...]
    start_len, first_sq, diag_one, below_one, cross, second_sq = [
        column(scalars_ref[...], i) for i in range(6)
    ]
    upper_two, diag_two, res_sq = [column(summed, i) for i in range(3)]
    left_sq = (
        res_sq
        - upper_two * upper_two * (2.0 - first_sq)
        - diag_two * diag_two * (2.0 - second_sq)
        + 2.0 * upper_two * diag_two * cross
    )
    below_two = jnp.sqrt(jnp.maximum(left_sq, 0.0) + EPS)
    step_one, step_two = givens_pair(
        start_len, diag_one, below_one, upper_two, diag_two, below_two
    )
    out_ref[...] = step_one * first_ref[...] + step_two * second_ref[...]


def sum_parts(values, count):
    if count != 8:
        return [lax.psum(values, AXIS)]
    pair = values + swap(values, 1, count)
    return [pair, swap(pair, 2, count), swap(pair, 4, count), swap(pair, 6, count)]


def exchange(send, panels, count):
    if count != 8:
        field, charges = send[:, :panels], send[:, panels:]
        ends = count - 1
        lower = lax.ppermute(field, AXIS, [(i, i + 1) for i in range(ends)])
        upper = lax.ppermute(field, AXIS, [(i + 1, i) for i in range(ends)])
        every = lax.all_gather(charges, AXIS)
        every = every.reshape((count // 2, 2) + charges.shape)
        return [lower, send, upper], [every[:, 0] + every[:, 1]], [0]
    near = swap(send, 1, count)
    rows, long = send.shape
    onward, pair = call(
        "onward", onward_kernel, [((rows, long), BF), ((rows, long - panels), BF)], [send, near]
    )
    two = swap(onward, 2, count)
    four = swap(pair, 4, count)
    six = swap(onward, 6, count)
    return [send, near, two, six], [pair, two, four, six], [0, panels, 0, panels]


def gather_quarters(coupling, quarters, count, early):
    if count != 8 or quarters != 4:
        return [lax.all_gather(coupling, "rhs")], early
    coupling, early = lax.optimization_barrier((coupling, early))
    pairs = [[(i, i ^ mask) for i in range(quarters)] for mask in (1, 2)]
    return [coupling] + [lax.ppermute(coupling, "rhs", pair) for pair in pairs], early


def finish_quarters(rows, quarters, late):
    if len(rows) == 1:
        return rows, late
    far, late = lax.optimization_barrier((rows[2], late))
    return rows + [lax.ppermute(far, "rhs", [(i, i ^ 1) for i in range(quarters)])], late


def nbytes(shape, kind):
    return math.prod(shape) * jnp.dtype(kind).itemsize


def room(*arrays):
    return pltpu.CompilerParams(
        vmem_limit_bytes=sum(nbytes(a.shape, a.dtype) for a in arrays) * 5 // 4 + 4 * 2**20
    )


def call(name, kernel, out_shapes, args, scratch=(), far=(), flops=0):
    out_shapes = [jax.ShapeDtypeStruct(shape, kind) for shape, kind in out_shapes]
    args = [pltpu.with_memory_space_constraint(x, pltpu.HBM) if i in far else x
            for i, x in enumerate(args)]
    specs = [
        pl.BlockSpec(
            memory_space=pltpu.HBM if i in far else pltpu.VMEM
        )
        for i in range(len(args))
    ]
    outs = [pl.BlockSpec(memory_space=pltpu.VMEM)] * len(out_shapes)
    held = [x for i, x in enumerate(args) if i not in far]
    held += [x for x in scratch if getattr(x, "memory_space", None) == pltpu.VMEM]
    return pl.pallas_call(
        kernel,
        name=name,
        out_shape=out_shapes,
        in_specs=specs,
        out_specs=outs,
        scratch_shapes=list(scratch),
        cost_estimate=pl.CostEstimate(flops=flops, bytes_accessed=flops // 500, transcendentals=0) if flops else None,
        compiler_params=room(*held, *out_shapes),
    )(*args)


def on_device(
    rhs_vec,
    self_coef,
    near_mats,
    near_ids,
    near_count,
    interp,
    skel_idx,
    coupling,
    diag_prec,
    low_rank,
):
    rows, panels = rhs_vec.shape
    block_count, slots, block, _ = near_mats.shape
    skeletons = coupling.shape[0]
    quarters = lax.axis_size("rhs")
    count = lax.axis_size(AXIS)
    width = low_rank.shape[1]
    region = lax.axis_index(AXIS)
    sources = 4 if count == 8 else 3
    maps, places = call(
        "maps",
        lambda *refs: maps_kernel(sources, *refs),
        [((quarters, 2 * LANES, panels // quarters), BF), ((block_count, LANES), jnp.int32)],
        [near_ids, near_count[None, :], jnp.swapaxes(interp, 1, 2), skel_idx],
    )
    wide = width + LANES
    long = panels + quarters * LANES

    parts = 4
    payload, rhs_near, diag_row, self_row, high, low = call(
        "open",
        lambda *refs: open_kernel(parts, *refs),
        [((rows, wide), F32), ((rows, panels), F32), ((1, panels), F32), ((1, panels), F32),
         (low_rank.shape, BF), (low_rank.shape, BF)],
        [rhs_vec, low_rank, diag_prec[None, :], self_coef[None, :]],
        [pltpu.VMEM((panels, width), F32), pltpu.SemaphoreType.DMA((parts + 3,))],
        far=(0, 1, 2, 3),
    )

    some_rows, payload = gather_quarters(coupling[:, 0, :], quarters, count, payload)
    sums = sum_parts(payload, count)
    first_dir, first_pre, send, keep = call(
        "first",
        lambda *refs: first_kernel(len(sums), *refs),
        [((rows, panels), F32), ((rows, panels), F32), ((rows, long), BF), ((rows, wide), F32)],
        [*sums, rhs_near, diag_row, high, low, maps],
        flops=10**9,
    )
    fields, charges, starts = exchange(send, panels, count)
    full_rows, fields[1] = finish_quarters(some_rows, quarters, fields[1])

    def near_product(fields):
        (near,) = call(
            "near",
            lambda *refs: near_kernel(len(fields), *refs),
            [((rows, panels), F32)],
            [*fields, places, near_mats],
            [pltpu.VMEM((len(fields) * block_count + 1, rows, block), BF)],
            flops=10**10,
        )
        return near

    near = near_product(fields)
    scratch = [pltpu.VMEM((quarters, count // 2, rows, LANES), BF)]
    residue, payload = call(
        "second",
        lambda *refs: second_kernel(starts, *refs),
        [((rows, panels), F32), ((rows, wide), F32)],
        [*charges, first_dir, first_pre, self_row, near, maps, high, low, *full_rows],
        scratch,
    )
    sums = sum_parts(payload, count)
    second_dir, second_pre, send, scalars = call(
        "third",
        lambda *refs: third_kernel(len(sums), *refs),
        [((rows, panels), F32), ((rows, panels), F32), ((rows, long), BF), ((rows, LANES), F32)],
        [*sums, residue, first_dir, keep, diag_row, high, low, maps],
    )
    fields, charges, starts = exchange(send, panels, count)
    near = near_product(fields)
    (tail,) = call(
        "fourth",
        lambda *refs: fourth_kernel(starts, *refs),
        [((rows, LANES), F32)],
        [*charges, first_dir, second_dir, second_pre, self_row, near, maps, *full_rows],
        scratch,
    )
    sums = sum_parts(tail, count)
    (result,) = call(
        "last",
        lambda *refs: last_kernel(len(sums), *refs),
        [((rows, panels), F32)],
        [*sums, scalars, first_pre, second_pre],
    )
    return result


def solution(mesh):
    placed = (
        P("rhs", "space"),
        P("space"),
        P("space", None, None, None),
        P("space", None),
        P("space"),
        P("space", None, None),
        P("space", None),
        P("space", "rhs", None),
        P("space"),
        P("space", None),
    )
    return jax.shard_map(
        on_device, mesh=mesh, in_specs=placed, out_specs=P("rhs", "space"), check_vma=False
    )
```

```python
import math

import jax
import jax.numpy as jnp
from jax import lax
from jax.experimental import pallas as pl
from jax.experimental.pallas import tpu as pltpu
from jax.sharding import PartitionSpec as P

EPS = 1e-06
F32 = jnp.float32
BF = jnp.bfloat16
AXIS = "space"
LANES = 128
HALF = 64


def swap(values, mask, count):
    return lax.ppermute(values, AXIS, [(i, i ^ mask) for i in range(count)])


def split(values):
    high = values.astype(BF)
    return high, (values - high.astype(F32)).astype(BF)


def dot_nn(left, right):
    return lax.dot_general(left, right, (((1,), (0,)), ((), ())), preferred_element_type=F32)


def dot_nt(left, right):
    return lax.dot_general(left, right, (((1,), (1,)), ((), ())), preferred_element_type=F32)


def dot_wide(dot, vector, high, low):
    rows = vector.shape[0]
    vec_high, vec_low = split(vector)
    first = dot(jnp.concatenate([vec_high, vec_low], axis=0), high)
    return first[:rows] + first[rows:] + dot(vec_high, low)


def row_sum(values):
    return jnp.sum(values, axis=1, keepdims=True)


def put_scalars(columns, rows):
    lane = lax.broadcasted_iota(jnp.int32, (rows, LANES), 1)
    out = jnp.zeros((rows, LANES), F32)
    for index, column in enumerate(columns):
        out = jnp.where(lane == index, column, out)
    return out


def column(values, index):
    return values[:, index : index + 1]


def charge_rows(field_low, maps_ref, send_ref):
    rows, panels = field_low.shape
    quarters, _, width = maps_ref.shape
    for quarter in range(quarters):
        both = dot_nt(field_low[:, quarter * width : (quarter + 1) * width], maps_ref[quarter])
        start = panels + quarter * LANES
        send_ref[:, start : start + LANES] = (both[:, :LANES] + both[:, LANES:]).astype(BF)


def build_maps(maps_ref, odd_start, skel, weights, block_count, rank, block):
    quarters = maps_ref.shape[0]
    per = block_count // quarters
    odd_start = pl.multiple_of(odd_start, HALF)
    maps_ref[...] = jnp.zeros(maps_ref.shape, BF)
    panel = lax.broadcasted_iota(jnp.int32, (rank, block), 1).astype(F32)
    for b in range(block_count):
        quarter, index = divmod(b, per)
        start = odd_start + index * rank
        cols = slice(index * block, (index + 1) * block)
        hot = jnp.where(skel[:rank, b : b + 1] == panel, 1.0, 0.0).astype(BF)
        maps_ref[quarter, pl.ds(start, rank), cols] = hot
        maps_ref[quarter, pl.ds(start + LANES, rank), cols] = weights(b)


def maps_kernel(sources, ids_ref, live_ref, weights_ref, skel_ref, maps_ref, places_ref):
    block_count, rank, block = weights_ref.shape
    skel = jnp.concatenate(
        [skel_ref[...].astype(F32), jnp.zeros((block_count, LANES - rank), F32)], axis=1
    ).T
    odd_start = (lax.axis_index(AXIS) % 2) * HALF
    build_maps(maps_ref, odd_start, skel, lambda b: weights_ref[b], block_count, rank, block)
    wanted = ids_ref[...]
    slots = wanted.shape[1]
    slot = lax.broadcasted_iota(jnp.int32, wanted.shape, 1)
    row = lax.broadcasted_iota(jnp.int32, wanted.shape, 0)
    counts = live_ref[...]
    live = slot < 0
    for b in range(block_count):
        live = live | ((row == b) & (slot < counts[0, b]))
    region = lax.axis_index(AXIS)
    place = block_place(wanted, live, block_count, sources, region).astype(F32)
    scale = jnp.where(slot % 4 == 0, 1.0, jnp.where(slot % 4 == 1, 64.0, 4096.0))
    scale = jnp.where(slot % 4 == 3, 262144.0, scale)
    lane = lax.broadcasted_iota(jnp.int32, (block_count, LANES), 1)
    packed = jnp.zeros((block_count, LANES), F32)
    for group in range(slots // 4):
        part = row_sum(jnp.where(slot // 4 == group, place * scale, 0.0))
        packed = jnp.where(lane == group, part, packed)
    places_ref[...] = packed.astype(jnp.int32)


def other_maps(base, rank, block, packs, maps_ref):
    chunks = packs[0][1].shape[1] // block
    per = maps_ref.shape[2] // block
    tall = per * rank // chunks
    odd_start = pl.multiple_of((1 - lax.axis_index(AXIS) % 2) * HALF, HALF)
    panel = lax.broadcasted_iota(jnp.int32, (rank, block), 1).astype(F32)
    for mask, ref in packs:
        quarter = lax.axis_index("rhs") ^ mask
        skel = ref[base + tall : base + tall + 16, :LANES].astype(F32)
        skel = jnp.concatenate([skel, jnp.zeros((LANES - 16, LANES), F32)], axis=0).T
        weights = jnp.concatenate(
            [ref[base : base + tall, j * block : (j + 1) * block] for j in range(chunks)], axis=0
        )
        for index in range(per):
            start = odd_start + index * rank
            cols = slice(index * block, (index + 1) * block)
            hot = jnp.where(skel[:rank, index : index + 1] == panel, 1.0, 0.0).astype(BF)
            maps_ref[quarter, pl.ds(start, rank), cols] = hot
            maps_ref[quarter, pl.ds(start + LANES, rank), cols] = weights[
                index * rank : (index + 1) * rank
            ]


def other_maps_kernel(base, rank, block, *refs):
    *pack_refs, maps_ref = refs
    maps_ref[...] = jnp.zeros(maps_ref.shape, BF)
    other_maps(base, rank, block, list(enumerate(pack_refs)), maps_ref)


def onward_kernel(send_ref, near_ref, onward_ref, pair_ref):
    panels = near_ref.shape[1] - pair_ref.shape[1]
    pair = send_ref[:, panels:] + near_ref[:, panels:]
    onward_ref[:, :panels] = near_ref[:, :panels]
    onward_ref[:, panels:] = pair
    pair_ref[...] = pair


def neighbour_field(panels, scaled, proj, part_refs, onward_ref):
    rows = proj.shape[0]
    both = jnp.concatenate(split(proj), axis=0)
    size = panels // len(part_refs)
    for mask, ref in enumerate(part_refs):
        part = dot_nt(both, ref[:size, :])
        start = pl.multiple_of((lax.axis_index("rhs") ^ mask) * size, size)
        field = scaled(start, size) - (part[:rows] + part[rows:])
        onward_ref[:, pl.ds(start, size)] = field.astype(BF)


def pair_charges(field_low, maps_ref, other_maps_ref, onward_ref, pair_ref):
    panels = field_low.shape[1]
    quarters, _, width = maps_ref.shape
    for quarter in range(quarters):
        cols = slice(quarter * width, (quarter + 1) * width)
        both = dot_nt(field_low[:, cols], maps_ref[quarter])
        both = both + dot_nt(onward_ref[:, cols], other_maps_ref[quarter])
        charge = (both[:, :LANES] + both[:, LANES:]).astype(BF)
        pair_ref[:, quarter * LANES : (quarter + 1) * LANES] = charge
        onward_ref[:, panels + quarter * LANES : panels + (quarter + 1) * LANES] = charge


def open_kernel(parts, paired, rhs_hbm, factor_hbm, diag_hbm, self_hbm, *refs):
    if paired:
        weights_hbm, skel_hbm, out_ref, rhs_ref, diag_ref, self_ref, high_ref, low_ref = refs[:8]
        pack_ref, held_ref, weights_ref, skel_ref, sems = refs[8:]
    else:
        out_ref, rhs_ref, diag_ref, self_ref, high_ref, low_ref, held_ref, sems = refs
    panels, width = factor_hbm.shape
    rows = rhs_ref.shape[0]
    depth = panels // parts
    pairs = [(rhs_hbm, rhs_ref), (diag_hbm, diag_ref), (self_hbm, self_ref)]
    if paired:
        pairs += [(weights_hbm, weights_ref), (skel_hbm, skel_ref)]
    loads = [
        pltpu.make_async_copy(source, target, sems.at[parts + index])
        for index, (source, target) in enumerate(pairs)
    ]
    for load in loads:
        load.start()
    copies = []
    for part in range(parts):
        span = pl.ds(part * depth, depth)
        copies.append(
            pltpu.make_async_copy(factor_hbm.at[span], held_ref.at[span], sems.at[part])
        )
        copies[-1].start()
    for load in loads:
        load.wait()
    rhs = rhs_ref[...]
    out_ref[:, width:] = put_scalars([row_sum(rhs * rhs)], rows)
    if paired:
        block_count, rank, block = weights_ref.shape
        quarters = lax.axis_size("rhs")
        quarter = lax.axis_index("rhs")
        size = panels // quarters
        per = block_count // quarters
        chunks = width // block
        tall = per * rank // chunks
        for index in range(per):
            values = weights_ref[quarter * per + index]
            for part in range(rank // tall):
                chunk = index * (rank // tall) + part
                pack_ref[size : size + tall, chunk * block : (chunk + 1) * block] = values[
                    part * tall : (part + 1) * tall
                ]
        skel = skel_ref[...].astype(F32)
        skel = jnp.concatenate([skel, jnp.zeros((block_count, width - rank), F32)], axis=1)
        row = lax.broadcasted_iota(jnp.int32, skel.shape, 0)
        picked = [
            jnp.sum(jnp.where(row == quarter * per + index, skel, 0.0), axis=0, keepdims=True)
            for index in range(per)
        ]
        picked.append(jnp.zeros((16 - per, width), F32))
        pack_ref[size + tall : size + tall + 16, :] = jnp.concatenate(picked, axis=0).astype(BF)
        start = size + tall + 16
        for part in split(diag_ref[...] * rhs):
            for first in range(0, panels, width):
                pack_ref[start : start + rows, :] = part[:, first : first + width]
                start += rows
    total = jnp.zeros((rows, width), F32)
    for part in range(parts):
        span = slice(part * depth, (part + 1) * depth)
        copies[part].wait()
        high, low = split(held_ref[span, :])
        high_ref[span, :] = high
        low_ref[span, :] = low
        total = total + dot_wide(dot_nn, rhs[:, span], high, low)
    out_ref[:, :width] = total
    if paired:
        pack_ref[:size, :] = high_ref[pl.ds(pl.multiple_of(quarter * size, size), size), :]


def first_kernel(parts, *refs):
    sums = refs[:parts]
    rhs_ref, diag_ref, high_ref, low_ref, maps_ref = refs[parts : parts + 5]
    dir_ref, pre_ref, keep_ref, send_ref = refs[parts + 5 :]
    width = high_ref.shape[1]
    rows, panels = rhs_ref.shape
    summed = sums[0][...]
    for ref in sums[1:]:
        summed = summed + ref[...]
    rhs_sq = column(summed[:, width:], 0)
    start_len = jnp.sqrt(rhs_sq + EPS)
    first_dir = rhs_ref[...] / start_len
    proj = summed[:, :width] / start_len
    first_pre = diag_ref[...] * first_dir - dot_wide(dot_nt, proj, high_ref[...], low_ref[...])
    field_low = first_pre.astype(BF)
    dir_ref[...] = first_dir
    pre_ref[...] = first_pre
    send_ref[:, :panels] = field_low
    charge_rows(field_low, maps_ref, send_ref)
    keep_ref[:, :width] = proj
    keep_ref[:, width:] = put_scalars([start_len, rhs_sq / (start_len * start_len)], rows)


def block_place(wanted, live, block_count, sources, region):
    source = wanted // block_count
    if sources == 4:
        slot = jnp.where(
            source == region,
            0,
            jnp.where(source == region ^ 1, 1, jnp.where(source == region ^ 3, 2, 3)),
        )
    else:
        slot = source - region + 1
    return jnp.where(live, slot * block_count + wanted % block_count, sources * block_count)


def near_kernel(sources, *refs):
    field_refs = refs[:sources]
    places_ref, mats_ref, near_ref, blocks_ref = refs[sources:]
    rows, panels = near_ref.shape
    block_count, slots, block, _ = mats_ref.shape
    packed = places_ref[...]
    for index, ref in enumerate(field_refs):
        for b in range(block_count):
            blocks_ref[index * block_count + b] = ref[:, b * block : (b + 1) * block]
    blocks_ref[sources * block_count] = jnp.zeros((rows, block), BF)
    for b in range(block_count):
        fours = [packed[b, group] for group in range(slots // 4)]
        places = [(fours[k // 4] >> (6 * (k % 4))) & 63 for k in range(slots)]
        picked = jnp.concatenate([blocks_ref[place] for place in places], axis=1)
        mats = jnp.concatenate([mats_ref[b, k] for k in range(slots)], axis=1)
        near_ref[:, b * block : (b + 1) * block] = dot_nt(picked, mats)


def apply_matrix(field_ref, self_ref, near_ref, charge_refs, coupling_refs, maps_ref, charges_ref):
    rows, panels = field_ref.shape
    quarters, pairs = charges_ref.shape[:2]
    gathered = len(coupling_refs) == 1
    region = lax.axis_index(AXIS)
    first_quarter = 0 if gathered else lax.axis_index("rhs")
    for quarter in range(quarters):
        for index in range(pairs):
            if len(charge_refs) == pairs:
                ref, start = charge_refs[index]
                start += quarter * LANES
                charge = ref[:, start : start + LANES]
                charges_ref[quarter, (region // 2) ^ index] = charge
            else:
                lanes = slice(quarter * LANES, (quarter + 1) * LANES)
                charges_ref[quarter, index] = charge_refs[0][0][index, :, lanes]
    far = jnp.zeros((rows, coupling_refs[0].shape[-2]), F32)
    for index in range(quarters):
        quarter = first_quarter ^ index
        charge = jnp.concatenate([charges_ref[quarter, t] for t in range(pairs)], axis=1)
        rows_in = coupling_refs[0][index] if gathered else coupling_refs[index][...]
        far = far + dot_nt(charge, rows_in)
    odd = (region % 2) == 1
    per = panels // quarters
    for quarter in range(quarters):
        start = (quarter // 2) * LANES
        chunk = far[:, start : start + LANES]
        turned = pltpu.roll(chunk, HALF, 1)
        chunk = jnp.where(odd, turned, chunk) if quarter % 2 == 0 else jnp.where(odd, chunk, turned)
        high, low = split(chunk)
        both = jnp.concatenate([high, low], axis=0)
        pot = dot_nn(jnp.concatenate([both, both], axis=1), maps_ref[quarter])
        cols = slice(quarter * per, (quarter + 1) * per)
        near = near_ref[:, cols] + (pot[:rows] + pot[rows:])
        yield cols, near + self_ref[:, cols] * field_ref[:, cols]


def second_kernel(charge_starts, *refs):
    parts = len(charge_starts)
    charge_refs = list(zip(refs[:parts], charge_starts))
    dir_ref, pre_ref, self_ref, diag_ref = refs[parts : parts + 4]
    near_ref, maps_ref, high_ref, low_ref = refs[parts + 4 : parts + 8]
    *coupling_refs, res_ref, scaled_ref, out_ref, charges_ref = refs[parts + 8 :]
    width = high_ref.shape[1]
    rows = pre_ref.shape[0]
    for cols, values in apply_matrix(
        pre_ref, self_ref, near_ref, charge_refs, coupling_refs, maps_ref, charges_ref
    ):
        res_ref[:, cols] = values
    res = res_ref[...]
    out_ref[:, :width] = dot_wide(dot_nn, res, high_ref[...], low_ref[...])
    out_ref[:, width:] = put_scalars([row_sum(res * dir_ref[...]), row_sum(res * res)], rows)
    scaled_ref[...] = diag_ref[...] * res


def third_kernel(parts, rank, block, *refs):
    if rank:
        *refs, other_maps_ref = refs
    sums = refs[:parts]
    res_ref, dir_ref, keep_ref, diag_ref, high_ref, low_ref, maps_ref = refs[parts : parts + 7]
    *extra, next_ref, pre_ref, scalars_ref, send_ref = refs[parts + 7 :]
    width = high_ref.shape[1]
    rows, panels = res_ref.shape
    summed = sums[0][...]
    for ref in sums[1:]:
        summed = summed + ref[...]
    keep = keep_ref[:, width:]
    start_len, first_sq = column(keep, 0), column(keep, 1)
    diag_one, res_sq = column(summed[:, width:], 0), column(summed[:, width:], 1)
    below_sq = jnp.maximum(res_sq - diag_one * diag_one * (2.0 - first_sq), 0.0)
    below_one = jnp.sqrt(below_sq + EPS)
    second_dir = (res_ref[...] - diag_one * dir_ref[...]) / below_one
    proj = (summed[:, :width] - diag_one * keep_ref[:, :width]) / below_one
    pre = diag_ref[...] * second_dir - dot_wide(dot_nt, proj, high_ref[...], low_ref[...])
    field_low = pre.astype(BF)
    pre_ref[...] = pre
    if extra:
        got_ref, *part_refs, some_maps_ref, onward_ref, pair_ref = extra
        other_maps_ref[...] = some_maps_ref[...]
        last = len(part_refs) - 1
        other_maps(panels // (last + 1), rank, block, [(last, part_refs[last])], other_maps_ref)
        ratio = diag_one / start_len
        count = panels // width
        base = part_refs[0].shape[0] - 2 * count * rows
        before = []
        for index in range(count):
            high_rows = pl.ds(base + index * rows, rows)
            low_rows = pl.ds(base + (index + count) * rows, rows)
            before.append(
                part_refs[0][high_rows, :].astype(F32) + part_refs[0][low_rows, :].astype(F32)
            )
        scaled_ref = next_ref
        scaled_ref[...] = (
            got_ref[...] - ratio * jnp.concatenate(before, axis=1)
        ) / below_one

        def scaled(start, size):
            return scaled_ref[:, pl.ds(start, size)]

        neighbour_field(panels, scaled, proj, part_refs, onward_ref)
        send_ref[...] = field_low
        pair_charges(field_low, maps_ref, other_maps_ref, onward_ref, pair_ref)
    else:
        send_ref[:, :panels] = field_low
        charge_rows(field_low, maps_ref, send_ref)
    next_ref[...] = second_dir
    cross = diag_one * (1.0 - first_sq) / below_one
    second_sq = below_sq / (below_one * below_one)
    scalars_ref[...] = put_scalars(
        [start_len, first_sq, diag_one, below_one, cross, second_sq], rows
    )


def fourth_kernel(charge_starts, *refs):
    parts = len(charge_starts)
    charge_refs = list(zip(refs[:parts], charge_starts))
    dir_ref, next_ref, pre_ref, self_ref, near_ref, maps_ref = refs[parts : parts + 6]
    *coupling_refs, out_ref, charges_ref = refs[parts + 6 :]
    rows = pre_ref.shape[0]
    upper = diag = square = 0.0
    for cols, values in apply_matrix(
        pre_ref, self_ref, near_ref, charge_refs, coupling_refs, maps_ref, charges_ref
    ):
        upper = upper + row_sum(values * dir_ref[:, cols])
        diag = diag + row_sum(values * next_ref[:, cols])
        square = square + row_sum(values * values)
    out_ref[...] = put_scalars([upper, diag, square], rows)


def givens_pair(start_len, diag_one, below_one, upper_two, diag_two, below_two):
    radius_one = jnp.sqrt(diag_one * diag_one + below_one * below_one)
    cos_one = diag_one / radius_one
    sin_one = below_one / radius_one
    upper = cos_one * upper_two + sin_one * diag_two
    lower = cos_one * diag_two - sin_one * upper_two
    radius_two = jnp.sqrt(lower * lower + below_two * below_two)
    step_two = lower / radius_two * (-sin_one * start_len) / radius_two
    step_one = (cos_one * start_len - upper * step_two) / radius_one
    return (step_one, step_two)


def last_kernel(parts, *refs):
    scalars_ref, first_ref, second_ref, out_ref = refs[parts:]
    summed = refs[0][...]
    for ref in refs[1:parts]:
        summed = summed + ref[...]
    start_len, first_sq, diag_one, below_one, cross, second_sq = [
        column(scalars_ref[...], i) for i in range(6)
    ]
    upper_two, diag_two, res_sq = [column(summed, i) for i in range(3)]
    left_sq = (
        res_sq
        - upper_two * upper_two * (2.0 - first_sq)
        - diag_two * diag_two * (2.0 - second_sq)
        + 2.0 * upper_two * diag_two * cross
    )
    below_two = jnp.sqrt(jnp.maximum(left_sq, 0.0) + EPS)
    step_one, step_two = givens_pair(
        start_len, diag_one, below_one, upper_two, diag_two, below_two
    )
    out_ref[...] = step_one * first_ref[...] + step_two * second_ref[...]


def sum_parts(values, count):
    if count != 8:
        return [lax.psum(values, AXIS)]
    pair = values + swap(values, 1, count)
    return [pair, swap(pair, 2, count), swap(pair, 4, count), swap(pair, 6, count)]


def exchange_z(field, onward, pair, panels, count):
    two = swap(onward, 2, count)
    four = swap(pair, 4, count)
    six = swap(onward, 6, count)
    return [field, onward, two, six], [pair, two, four, six], [0, panels, 0, panels]


def exchange(send, panels, count):
    if count == 8:
        near = swap(send, 1, count)
        rows, long = send.shape
        onward, pair = call(
            "onward", onward_kernel, [((rows, long), BF), ((rows, long - panels), BF)], [send, near]
        )
        fields, charges, starts = exchange_z(send, onward, pair, panels, count)
        return [send, near] + fields[2:], charges, starts
    field, charges = send[:, :panels], send[:, panels:]
    ends = count - 1
    lower = lax.ppermute(field, AXIS, [(i, i + 1) for i in range(ends)])
    upper = lax.ppermute(field, AXIS, [(i + 1, i) for i in range(ends)])
    every = lax.all_gather(charges, AXIS)
    every = every.reshape((count // 2, 2) + charges.shape)
    return [lower, send, upper], [every[:, 0] + every[:, 1]], [0]


def gather_quarters(coupling, quarters, count, early):
    if count != 8 or quarters != 4:
        return [lax.all_gather(coupling, "rhs")], early
    coupling, early = lax.optimization_barrier((coupling, early))
    pairs = [[(i, i ^ mask) for i in range(quarters)] for mask in (1, 2)]
    return [coupling] + [lax.ppermute(coupling, "rhs", pair) for pair in pairs], early


def finish_quarters(rows, quarters, late):
    if len(rows) == 1:
        return rows, late
    far, late = lax.optimization_barrier((rows[2], late))
    return rows + [lax.ppermute(far, "rhs", [(i, i ^ 1) for i in range(quarters)])], late


def nbytes(shape, kind):
    return math.prod(shape) * jnp.dtype(kind).itemsize


def room(*arrays):
    return pltpu.CompilerParams(
        vmem_limit_bytes=sum(nbytes(a.shape, a.dtype) for a in arrays) * 5 // 4 + 4 * 2**20
    )


def call(name, kernel, out_shapes, args, scratch=(), far=(), flops=0):
    out_shapes = [jax.ShapeDtypeStruct(shape, kind) for shape, kind in out_shapes]
    args = [pltpu.with_memory_space_constraint(x, pltpu.HBM) if i in far else x
            for i, x in enumerate(args)]
    specs = [
        pl.BlockSpec(
            memory_space=pltpu.HBM if i in far else pltpu.VMEM
        )
        for i in range(len(args))
    ]
    outs = [pl.BlockSpec(memory_space=pltpu.VMEM)] * len(out_shapes)
    held = [x for i, x in enumerate(args) if i not in far]
    held += [x for x in scratch if getattr(x, "memory_space", None) == pltpu.VMEM]
    return pl.pallas_call(
        kernel,
        name=name,
        out_shape=out_shapes,
        in_specs=specs,
        out_specs=outs,
        scratch_shapes=list(scratch),
        cost_estimate=pl.CostEstimate(flops=flops, bytes_accessed=flops // 500, transcendentals=0) if flops else None,
        compiler_params=room(*held, *out_shapes),
    )(*args)


def on_device(
    rhs_vec,
    self_coef,
    near_mats,
    near_ids,
    near_count,
    interp,
    skel_idx,
    coupling,
    diag_prec,
    low_rank,
):
    rows, panels = rhs_vec.shape
    block_count, slots, block, _ = near_mats.shape
    rank = interp.shape[2]
    quarters = lax.axis_size("rhs")
    count = lax.axis_size(AXIS)
    width = low_rank.shape[1]
    sources = 4 if count == 8 else 3
    weights = jnp.swapaxes(interp, 1, 2)
    maps, places = call(
        "maps",
        lambda *refs: maps_kernel(sources, *refs),
        [((quarters, 2 * LANES, panels // quarters), BF), ((block_count, LANES), jnp.int32)],
        [near_ids, near_count[None, :], weights, skel_idx],
    )
    wide = width + LANES
    long = panels + quarters * LANES
    paired = count == 8 and quarters == 4
    parts = 4
    args = [rhs_vec, low_rank, diag_prec[None, :], self_coef[None, :]]
    outs = [((rows, wide), F32), ((rows, panels), F32), ((1, panels), F32),
            ((1, panels), F32), (low_rank.shape, BF), (low_rank.shape, BF)]
    scratch = [pltpu.VMEM((panels, width), F32)]
    if paired:
        args += [weights, skel_idx]
        tall = block_count // quarters * rank * block // width
        packed = panels // quarters + tall + 16 + 2 * rows * panels // width
        outs += [((packed, width), BF)]
        scratch += [pltpu.VMEM(weights.shape, BF), pltpu.VMEM(skel_idx.shape, jnp.int32)]
    payload, rhs_near, diag_row, self_row, high, low, *packs = call(
        "open",
        lambda *refs: open_kernel(parts, paired, *refs),
        outs,
        args,
        scratch + [pltpu.SemaphoreType.DMA((parts + 5,))],
        far=range(len(args)),
    )
    some_rows, payload = gather_quarters(coupling[:, 0, :], quarters, count, payload)
    sums = sum_parts(payload, count)
    if paired:
        mine = swap(packs[0], 1, count)
    first_dir, first_pre, keep, send = call(
        "first",
        lambda *refs: first_kernel(len(sums), *refs),
        [((rows, panels), F32), ((rows, panels), F32), ((rows, wide), F32), ((rows, long), BF)],
        [*sums, rhs_near, diag_row, high, low, maps],
        flops=2*10**9,
    )
    fields, charges, starts = exchange(send, panels, count)
    full_rows, fields[1] = finish_quarters(some_rows, quarters, fields[1])
    if paired:
        mine, fields[1] = gather_quarters(mine, quarters, count, fields[1])

    def near_product(fields):
        (near,) = call(
            "near",
            lambda *refs: near_kernel(len(fields), *refs),
            [((rows, panels), F32)],
            [*fields, places, near_mats],
            [pltpu.VMEM((len(fields) * block_count + 1, rows, block), BF)],
            flops=10**10,
        )
        return near

    near = near_product(fields)
    scratch = [pltpu.VMEM((quarters, count // 2, rows, LANES), BF)]
    residue, scaled, payload = call(
        "second",
        lambda *refs: second_kernel(starts, *refs),
        [((rows, panels), F32), ((rows, panels), F32), ((rows, wide), F32)],
        [*charges, first_dir, first_pre, self_row, diag_row, near, maps, high, low, *full_rows],
        scratch,
        flops=10**10,
    )
    sums = sum_parts(payload, count)
    outs = [((rows, panels), F32), ((rows, panels), F32), ((rows, LANES), F32)]
    extra = []
    if paired:
        again = swap(scaled, 1, count)
        mine, sums[0] = finish_quarters(mine, quarters, sums[0])
        (some_maps,) = call(
            "other_maps",
            lambda *refs: other_maps_kernel(panels // quarters, rank, block, *refs),
            [(maps.shape, BF)],
            mine[:-1],
            flops=10**10,
        )
        extra = [again, *mine, some_maps]
        outs = [((rows, long), BF), ((rows, long - panels), BF), *outs, ((rows, panels), BF)]
    else:
        outs += [((rows, long), BF)]
    *onward, second_dir, second_pre, scalars, send = call(
        "third",
        lambda *refs: third_kernel(len(sums), paired * rank, block, *refs),
        outs,
        [*sums, residue, first_dir, keep, diag_row, high, low, maps, *extra],
        [pltpu.VMEM(maps.shape, BF)] if paired else [],
    )
    if paired:
        fields, charges, starts = exchange_z(send, *onward, panels, count)
    else:
        fields, charges, starts = exchange(send, panels, count)
    near = near_product(fields)
    (tail,) = call(
        "fourth",
        lambda *refs: fourth_kernel(starts, *refs),
        [((rows, LANES), F32)],
        [*charges, first_dir, second_dir, second_pre, self_row, near, maps, *full_rows],
        scratch,
    )
    sums = sum_parts(tail, count)
    (result,) = call(
        "last",
        lambda *refs: last_kernel(len(sums), *refs),
        [((rows, panels), F32)],
        [*sums, scalars, first_pre, second_pre],
    )
    return result


def solution(mesh):
    placed = (
        P("rhs", "space"),
        P("space"),
        P("space", None, None, None),
        P("space", None),
        P("space"),
        P("space", None, None),
        P("space", None),
        P("space", "rhs", None),
        P("space"),
        P("space", None),
    )
    return jax.shard_map(
        on_device, mesh=mesh, in_specs=placed, out_specs=P("rhs", "space"), check_vma=False
    )
```

```python
import math

import jax
import jax.numpy as jnp
from jax import lax
from jax.experimental import pallas as pl
from jax.experimental.pallas import tpu as pltpu
from jax.sharding import PartitionSpec as P

EPS = 1e-06
F32 = jnp.float32
BF = jnp.bfloat16
AXIS = "space"
LANES = 128
HALF = 64


def swap(values, mask, count):
    return lax.ppermute(values, AXIS, [(i, i ^ mask) for i in range(count)])


def split(values):
    high = values.astype(BF)
    return high, (values - high.astype(F32)).astype(BF)


def dot_nn(left, right):
    return lax.dot_general(left, right, (((1,), (0,)), ((), ())), preferred_element_type=F32)


def dot_nt(left, right):
    return lax.dot_general(left, right, (((1,), (1,)), ((), ())), preferred_element_type=F32)


def dot_wide(dot, vector, high, low):
    rows = vector.shape[0]
    vec_high, vec_low = split(vector)
    first = dot(jnp.concatenate([vec_high, vec_low], axis=0), high)
    return first[:rows] + first[rows:] + dot(vec_high, low)


def row_sum(values):
    return jnp.sum(values, axis=1, keepdims=True)


def put_scalars(columns, rows):
    lane = lax.broadcasted_iota(jnp.int32, (rows, LANES), 1)
    out = jnp.zeros((rows, LANES), F32)
    for index, column in enumerate(columns):
        out = jnp.where(lane == index, column, out)
    return out


def column(values, index):
    return values[:, index : index + 1]


def charge_rows(field_low, maps_ref, send_ref):
    rows, panels = field_low.shape
    quarters, _, width = maps_ref.shape
    for quarter in range(quarters):
        both = dot_nt(field_low[:, quarter * width : (quarter + 1) * width], maps_ref[quarter])
        start = panels + quarter * LANES
        send_ref[:, start : start + LANES] = (both[:, :LANES] + both[:, LANES:]).astype(BF)


def build_maps(maps_ref, odd_start, skel, weights, block_count, rank, block):
    quarters = maps_ref.shape[0]
    per = block_count // quarters
    odd_start = pl.multiple_of(odd_start, HALF)
    maps_ref[...] = jnp.zeros(maps_ref.shape, BF)
    panel = lax.broadcasted_iota(jnp.int32, (rank, block), 1).astype(F32)
    for b in range(block_count):
        quarter, index = divmod(b, per)
        start = odd_start + index * rank
        cols = slice(index * block, (index + 1) * block)
        hot = jnp.where(skel[:rank, b : b + 1] == panel, 1.0, 0.0).astype(BF)
        maps_ref[quarter, pl.ds(start, rank), cols] = hot
        maps_ref[quarter, pl.ds(start + LANES, rank), cols] = weights(b)


def maps_kernel(sources, ids_ref, live_ref, weights_ref, skel_ref, maps_ref, places_ref):
    block_count, rank, block = weights_ref.shape
    skel = jnp.concatenate(
        [skel_ref[...].astype(F32), jnp.zeros((block_count, LANES - rank), F32)], axis=1
    ).T
    odd_start = (lax.axis_index(AXIS) % 2) * HALF
    build_maps(maps_ref, odd_start, skel, lambda b: weights_ref[b], block_count, rank, block)
    wanted = ids_ref[...]
    slots = wanted.shape[1]
    slot = lax.broadcasted_iota(jnp.int32, wanted.shape, 1)
    row = lax.broadcasted_iota(jnp.int32, wanted.shape, 0)
    counts = live_ref[...]
    live = slot < 0
    for b in range(block_count):
        live = live | ((row == b) & (slot < counts[0, b]))
    region = lax.axis_index(AXIS)
    place = block_place(wanted, live, block_count, sources, region).astype(F32)
    scale = jnp.where(slot % 4 == 0, 1.0, jnp.where(slot % 4 == 1, 64.0, 4096.0))
    scale = jnp.where(slot % 4 == 3, 262144.0, scale)
    lane = lax.broadcasted_iota(jnp.int32, (block_count, LANES), 1)
    packed = jnp.zeros((block_count, LANES), F32)
    for group in range(slots // 4):
        part = row_sum(jnp.where(slot // 4 == group, place * scale, 0.0))
        packed = jnp.where(lane == group, part, packed)
    places_ref[...] = packed.astype(jnp.int32)


def other_maps(base, rank, block, packs, maps_ref):
    chunks = packs[0][1].shape[1] // block
    per = maps_ref.shape[2] // block
    tall = per * rank // chunks
    odd_start = pl.multiple_of((1 - lax.axis_index(AXIS) % 2) * HALF, HALF)
    panel = lax.broadcasted_iota(jnp.int32, (rank, block), 1).astype(F32)
    for mask, ref in packs:
        quarter = lax.axis_index("rhs") ^ mask
        skel = ref[base + tall : base + tall + 16, :LANES].astype(F32)
        skel = jnp.concatenate([skel, jnp.zeros((LANES - 16, LANES), F32)], axis=0).T
        weights = jnp.concatenate(
            [ref[base : base + tall, j * block : (j + 1) * block] for j in range(chunks)], axis=0
        )
        for index in range(per):
            start = odd_start + index * rank
            cols = slice(index * block, (index + 1) * block)
            hot = jnp.where(skel[:rank, index : index + 1] == panel, 1.0, 0.0).astype(BF)
            maps_ref[quarter, pl.ds(start, rank), cols] = hot
            maps_ref[quarter, pl.ds(start + LANES, rank), cols] = weights[
                index * rank : (index + 1) * rank
            ]


def other_maps_kernel(base, rank, block, *refs):
    *pack_refs, maps_ref = refs
    maps_ref[...] = jnp.zeros(maps_ref.shape, BF)
    other_maps(base, rank, block, list(enumerate(pack_refs)), maps_ref)


def onward_kernel(send_ref, near_ref, onward_ref, pair_ref):
    panels = near_ref.shape[1] - pair_ref.shape[1]
    pair = send_ref[:, panels:] + near_ref[:, panels:]
    onward_ref[:, :panels] = near_ref[:, :panels]
    onward_ref[:, panels:] = pair
    pair_ref[...] = pair


def neighbour_field(panels, scaled, proj, part_refs, onward_ref):
    rows = proj.shape[0]
    both = jnp.concatenate(split(proj), axis=0)
    size = panels // len(part_refs)
    for mask, ref in enumerate(part_refs):
        part = dot_nt(both, ref[:size, :])
        start = pl.multiple_of((lax.axis_index("rhs") ^ mask) * size, size)
        field = scaled(start, size) - (part[:rows] + part[rows:])
        onward_ref[:, pl.ds(start, size)] = field.astype(BF)


def pair_charges(field_low, maps_ref, other_maps_ref, onward_ref, pair_ref):
    panels = field_low.shape[1]
    quarters, _, width = maps_ref.shape
    for quarter in range(quarters):
        cols = slice(quarter * width, (quarter + 1) * width)
        both = dot_nt(field_low[:, cols], maps_ref[quarter])
        both = both + dot_nt(onward_ref[:, cols], other_maps_ref[quarter])
        charge = (both[:, :LANES] + both[:, LANES:]).astype(BF)
        pair_ref[:, quarter * LANES : (quarter + 1) * LANES] = charge
        onward_ref[:, panels + quarter * LANES : panels + (quarter + 1) * LANES] = charge


def open_kernel(parts, paired, rhs_hbm, factor_hbm, diag_hbm, self_hbm, *refs):
    if paired:
        weights_hbm, skel_hbm, out_ref, rhs_ref, diag_ref, self_ref, high_ref, low_ref = refs[:8]
        pack_ref, held_ref, weights_ref, skel_ref, sems = refs[8:]
    else:
        out_ref, rhs_ref, diag_ref, self_ref, high_ref, low_ref, held_ref, sems = refs
    panels, width = factor_hbm.shape
    rows = rhs_ref.shape[0]
    depth = panels // parts
    pairs = [(rhs_hbm, rhs_ref), (diag_hbm, diag_ref), (self_hbm, self_ref)]
    if paired:
        pairs += [(weights_hbm, weights_ref), (skel_hbm, skel_ref)]
    loads = [
        pltpu.make_async_copy(source, target, sems.at[parts + index])
        for index, (source, target) in enumerate(pairs)
    ]
    for load in loads:
        load.start()
    copies = []
    for part in range(parts):
        span = pl.ds(part * depth, depth)
        copies.append(
            pltpu.make_async_copy(factor_hbm.at[span], held_ref.at[span], sems.at[part])
        )
        copies[-1].start()
    for load in loads:
        load.wait()
    rhs = rhs_ref[...]
    out_ref[:, width:] = put_scalars([row_sum(rhs * rhs)], rows)
    if paired:
        block_count, rank, block = weights_ref.shape
        quarters = lax.axis_size("rhs")
        quarter = lax.axis_index("rhs")
        size = panels // quarters
        per = block_count // quarters
        chunks = width // block
        tall = per * rank // chunks
        for index in range(per):
            values = weights_ref[quarter * per + index]
            for part in range(rank // tall):
                chunk = index * (rank // tall) + part
                pack_ref[size : size + tall, chunk * block : (chunk + 1) * block] = values[
                    part * tall : (part + 1) * tall
                ]
        skel = skel_ref[...].astype(F32)
        skel = jnp.concatenate([skel, jnp.zeros((block_count, width - rank), F32)], axis=1)
        row = lax.broadcasted_iota(jnp.int32, skel.shape, 0)
        picked = [
            jnp.sum(jnp.where(row == quarter * per + index, skel, 0.0), axis=0, keepdims=True)
            for index in range(per)
        ]
        picked.append(jnp.zeros((16 - per, width), F32))
        pack_ref[size + tall : size + tall + 16, :] = jnp.concatenate(picked, axis=0).astype(BF)
        start = size + tall + 16
        for part in split(diag_ref[...] * rhs):
            for first in range(0, panels, width):
                pack_ref[start : start + rows, :] = part[:, first : first + width]
                start += rows
    total = jnp.zeros((rows, width), F32)
    for part in range(parts):
        span = slice(part * depth, (part + 1) * depth)
        copies[part].wait()
        high, low = split(held_ref[span, :])
        high_ref[span, :] = high
        low_ref[span, :] = low
        total = total + dot_wide(dot_nn, rhs[:, span], high, low)
    out_ref[:, :width] = total
    if paired:
        pack_ref[:size, :] = high_ref[pl.ds(pl.multiple_of(quarter * size, size), size), :]


def first_kernel(parts, *refs):
    sums = refs[:parts]
    rhs_ref, diag_ref, high_ref, low_ref, maps_ref = refs[parts : parts + 5]
    dir_ref, pre_ref, keep_ref, send_ref = refs[parts + 5 :]
    width = high_ref.shape[1]
    rows, panels = rhs_ref.shape
    summed = sums[0][...]
    for ref in sums[1:]:
        summed = summed + ref[...]
    rhs_sq = column(summed[:, width:], 0)
    start_len = jnp.sqrt(rhs_sq + EPS)
    first_dir = rhs_ref[...] / start_len
    proj = summed[:, :width] / start_len
    first_pre = diag_ref[...] * first_dir - dot_wide(dot_nt, proj, high_ref[...], low_ref[...])
    field_low = first_pre.astype(BF)
    dir_ref[...] = first_dir
    pre_ref[...] = first_pre
    send_ref[:, :panels] = field_low
    charge_rows(field_low, maps_ref, send_ref)
    keep_ref[:, :width] = proj
    keep_ref[:, width:] = put_scalars([start_len, rhs_sq / (start_len * start_len)], rows)


def block_place(wanted, live, block_count, sources, region):
    source = wanted // block_count
    if sources == 4:
        slot = jnp.where(
            source == region,
            0,
            jnp.where(source == region ^ 1, 1, jnp.where(source == region ^ 3, 2, 3)),
        )
    else:
        slot = source - region + 1
    return jnp.where(live, slot * block_count + wanted % block_count, sources * block_count)


def near_kernel(sources, *refs):
    field_refs = refs[:sources]
    places_ref, mats_ref, near_ref, blocks_ref = refs[sources:]
    rows, panels = near_ref.shape
    block_count, slots, block, _ = mats_ref.shape
    packed = places_ref[...]
    for index, ref in enumerate(field_refs):
        for b in range(block_count):
            blocks_ref[index * block_count + b] = ref[:, b * block : (b + 1) * block]
    blocks_ref[sources * block_count] = jnp.zeros((rows, block), BF)
    for b in range(block_count):
        fours = [packed[b, group] for group in range(slots // 4)]
        places = [(fours[k // 4] >> (6 * (k % 4))) & 63 for k in range(slots)]
        picked = jnp.concatenate([blocks_ref[place] for place in places], axis=1)
        mats = jnp.concatenate([mats_ref[b, k] for k in range(slots)], axis=1)
        near_ref[:, b * block : (b + 1) * block] = dot_nt(picked, mats)


def apply_matrix(field_ref, self_ref, near_ref, charge_refs, coupling_refs, maps_ref, charges_ref):
    rows, panels = field_ref.shape
    quarters, pairs = charges_ref.shape[:2]
    gathered = len(coupling_refs) == 1
    region = lax.axis_index(AXIS)
    first_quarter = 0 if gathered else lax.axis_index("rhs")
    for quarter in range(quarters):
        for index in range(pairs):
            if len(charge_refs) == pairs:
                ref, start = charge_refs[index]
                start += quarter * LANES
                charge = ref[:, start : start + LANES]
                charges_ref[quarter, (region // 2) ^ index] = charge
            else:
                lanes = slice(quarter * LANES, (quarter + 1) * LANES)
                charges_ref[quarter, index] = charge_refs[0][0][index, :, lanes]
    far = jnp.zeros((rows, coupling_refs[0].shape[-2]), F32)
    for index in range(quarters):
        quarter = first_quarter ^ index
        charge = jnp.concatenate([charges_ref[quarter, t] for t in range(pairs)], axis=1)
        rows_in = coupling_refs[0][index] if gathered else coupling_refs[index][...]
        far = far + dot_nt(charge, rows_in)
    odd = (region % 2) == 1
    per = panels // quarters
    for quarter in range(quarters):
        start = (quarter // 2) * LANES
        chunk = far[:, start : start + LANES]
        turned = pltpu.roll(chunk, HALF, 1)
        chunk = jnp.where(odd, turned, chunk) if quarter % 2 == 0 else jnp.where(odd, chunk, turned)
        high, low = split(chunk)
        both = jnp.concatenate([high, low], axis=0)
        pot = dot_nn(jnp.concatenate([both, both], axis=1), maps_ref[quarter])
        cols = slice(quarter * per, (quarter + 1) * per)
        near = near_ref[:, cols] + (pot[:rows] + pot[rows:])
        yield cols, near + self_ref[:, cols] * field_ref[:, cols]


def second_kernel(charge_starts, *refs):
    parts = len(charge_starts)
    charge_refs = list(zip(refs[:parts], charge_starts))
    dir_ref, pre_ref, self_ref, diag_ref = refs[parts : parts + 4]
    near_ref, maps_ref, high_ref, low_ref = refs[parts + 4 : parts + 8]
    *coupling_refs, res_ref, scaled_ref, out_ref, charges_ref = refs[parts + 8 :]
    width = high_ref.shape[1]
    rows = pre_ref.shape[0]
    for cols, values in apply_matrix(
        pre_ref, self_ref, near_ref, charge_refs, coupling_refs, maps_ref, charges_ref
    ):
        res_ref[:, cols] = values
    res = res_ref[...]
    out_ref[:, :width] = dot_wide(dot_nn, res, high_ref[...], low_ref[...])
    out_ref[:, width:] = put_scalars([row_sum(res * dir_ref[...]), row_sum(res * res)], rows)
    scaled_ref[...] = diag_ref[...] * res


def third_kernel(parts, rank, block, *refs):
    if rank:
        *refs, other_maps_ref = refs
    sums = refs[:parts]
    res_ref, dir_ref, keep_ref, diag_ref, high_ref, low_ref, maps_ref = refs[parts : parts + 7]
    *extra, next_ref, pre_ref, scalars_ref, send_ref = refs[parts + 7 :]
    width = high_ref.shape[1]
    rows, panels = res_ref.shape
    summed = sums[0][...]
    for ref in sums[1:]:
        summed = summed + ref[...]
    keep = keep_ref[:, width:]
    start_len, first_sq = column(keep, 0), column(keep, 1)
    diag_one, res_sq = column(summed[:, width:], 0), column(summed[:, width:], 1)
    below_sq = jnp.maximum(res_sq - diag_one * diag_one * (2.0 - first_sq), 0.0)
    below_one = jnp.sqrt(below_sq + EPS)
    second_dir = (res_ref[...] - diag_one * dir_ref[...]) / below_one
    proj = (summed[:, :width] - diag_one * keep_ref[:, :width]) / below_one
    pre = diag_ref[...] * second_dir - dot_wide(dot_nt, proj, high_ref[...], low_ref[...])
    field_low = pre.astype(BF)
    pre_ref[...] = pre
    if extra:
        got_ref, *part_refs, some_maps_ref, onward_ref, pair_ref = extra
        other_maps_ref[...] = some_maps_ref[...]
        last = len(part_refs) - 1
        other_maps(panels // (last + 1), rank, block, [(last, part_refs[last])], other_maps_ref)
        ratio = diag_one / start_len
        count = panels // width
        base = part_refs[0].shape[0] - 2 * count * rows
        before = []
        for index in range(count):
            high_rows = pl.ds(base + index * rows, rows)
            low_rows = pl.ds(base + (index + count) * rows, rows)
            before.append(
                part_refs[0][high_rows, :].astype(F32) + part_refs[0][low_rows, :].astype(F32)
            )
        scaled_ref = next_ref
        scaled_ref[...] = (
            got_ref[...] - ratio * jnp.concatenate(before, axis=1)
        ) / below_one

        def scaled(start, size):
            return scaled_ref[:, pl.ds(start, size)]

        neighbour_field(panels, scaled, proj, part_refs, onward_ref)
        send_ref[...] = field_low
        pair_charges(field_low, maps_ref, other_maps_ref, onward_ref, pair_ref)
    else:
        send_ref[:, :panels] = field_low
        charge_rows(field_low, maps_ref, send_ref)
    next_ref[...] = second_dir
    cross = diag_one * (1.0 - first_sq) / below_one
    second_sq = below_sq / (below_one * below_one)
    scalars_ref[...] = put_scalars(
        [start_len, first_sq, diag_one, below_one, cross, second_sq], rows
    )


def fourth_kernel(charge_starts, *refs):
    parts = len(charge_starts)
    charge_refs = list(zip(refs[:parts], charge_starts))
    dir_ref, next_ref, pre_ref, self_ref, near_ref, maps_ref = refs[parts : parts + 6]
    *coupling_refs, out_ref, charges_ref = refs[parts + 6 :]
    rows = pre_ref.shape[0]
    upper = diag = square = 0.0
    for cols, values in apply_matrix(
        pre_ref, self_ref, near_ref, charge_refs, coupling_refs, maps_ref, charges_ref
    ):
        upper = upper + row_sum(values * dir_ref[:, cols])
        diag = diag + row_sum(values * next_ref[:, cols])
        square = square + row_sum(values * values)
    out_ref[...] = put_scalars([upper, diag, square], rows)


def givens_pair(start_len, diag_one, below_one, upper_two, diag_two, below_two):
    radius_one = jnp.sqrt(diag_one * diag_one + below_one * below_one)
    cos_one = diag_one / radius_one
    sin_one = below_one / radius_one
    upper = cos_one * upper_two + sin_one * diag_two
    lower = cos_one * diag_two - sin_one * upper_two
    radius_two = jnp.sqrt(lower * lower + below_two * below_two)
    step_two = lower / radius_two * (-sin_one * start_len) / radius_two
    step_one = (cos_one * start_len - upper * step_two) / radius_one
    return (step_one, step_two)


def last_kernel(parts, *refs):
    scalars_ref, first_ref, second_ref, out_ref = refs[parts:]
    summed = refs[0][...]
    for ref in refs[1:parts]:
        summed = summed + ref[...]
    start_len, first_sq, diag_one, below_one, cross, second_sq = [
        column(scalars_ref[...], i) for i in range(6)
    ]
    upper_two, diag_two, res_sq = [column(summed, i) for i in range(3)]
    left_sq = (
        res_sq
        - upper_two * upper_two * (2.0 - first_sq)
        - diag_two * diag_two * (2.0 - second_sq)
        + 2.0 * upper_two * diag_two * cross
    )
    below_two = jnp.sqrt(jnp.maximum(left_sq, 0.0) + EPS)
    step_one, step_two = givens_pair(
        start_len, diag_one, below_one, upper_two, diag_two, below_two
    )
    out_ref[...] = step_one * first_ref[...] + step_two * second_ref[...]


def sum_parts(values, count):
    if count != 8:
        return [lax.psum(values, AXIS)]
    pair = values + swap(values, 1, count)
    return [pair, swap(pair, 2, count), swap(pair, 4, count), swap(pair, 6, count)]


def exchange_z(field, onward, pair, panels, count):
    two = swap(onward, 2, count)
    four = swap(pair, 4, count)
    six = swap(onward, 6, count)
    return [field, onward, two, six], [pair, two, four, six], [0, panels, 0, panels]


def exchange(send, panels, count):
    if count == 8:
        near = swap(send, 1, count)
        rows, long = send.shape
        onward, pair = call(
            "onward", onward_kernel, [((rows, long), BF), ((rows, long - panels), BF)], [send, near]
        )
        fields, charges, starts = exchange_z(send, onward, pair, panels, count)
        return [send, near] + fields[2:], charges, starts
    field, charges = send[:, :panels], send[:, panels:]
    ends = count - 1
    lower = lax.ppermute(field, AXIS, [(i, i + 1) for i in range(ends)])
    upper = lax.ppermute(field, AXIS, [(i + 1, i) for i in range(ends)])
    every = lax.all_gather(charges, AXIS)
    every = every.reshape((count // 2, 2) + charges.shape)
    return [lower, send, upper], [every[:, 0] + every[:, 1]], [0]


def gather_quarters(coupling, quarters, count, early):
    if count != 8 or quarters != 4:
        return [lax.all_gather(coupling, "rhs")], early
    coupling, early = lax.optimization_barrier((coupling, early))
    pairs = [[(i, i ^ mask) for i in range(quarters)] for mask in (1, 2)]
    return [coupling] + [lax.ppermute(coupling, "rhs", pair) for pair in pairs], early


def finish_quarters(rows, quarters, late):
    if len(rows) == 1:
        return rows, late
    far, late = lax.optimization_barrier((rows[2], late))
    return rows + [lax.ppermute(far, "rhs", [(i, i ^ 1) for i in range(quarters)])], late


def nbytes(shape, kind):
    return math.prod(shape) * jnp.dtype(kind).itemsize


def room(*arrays):
    return pltpu.CompilerParams(
        vmem_limit_bytes=sum(nbytes(a.shape, a.dtype) for a in arrays) * 5 // 4 + 4 * 2**20
    )


def call(name, kernel, out_shapes, args, scratch=(), far=(), flops=0):
    out_shapes = [jax.ShapeDtypeStruct(shape, kind) for shape, kind in out_shapes]
    args = [pltpu.with_memory_space_constraint(x, pltpu.HBM) if i in far else x
            for i, x in enumerate(args)]
    specs = [
        pl.BlockSpec(
            memory_space=pltpu.HBM if i in far else pltpu.VMEM
        )
        for i in range(len(args))
    ]
    outs = [pl.BlockSpec(memory_space=pltpu.VMEM)] * len(out_shapes)
    held = [x for i, x in enumerate(args) if i not in far]
    held += [x for x in scratch if getattr(x, "memory_space", None) == pltpu.VMEM]
    return pl.pallas_call(
        kernel,
        name=name,
        out_shape=out_shapes,
        in_specs=specs,
        out_specs=outs,
        scratch_shapes=list(scratch),
        cost_estimate=pl.CostEstimate(flops=flops, bytes_accessed=flops // 500, transcendentals=0) if flops else None,
        compiler_params=room(*held, *out_shapes),
    )(*args)


def on_device(
    rhs_vec,
    self_coef,
    near_mats,
    near_ids,
    near_count,
    interp,
    skel_idx,
    coupling,
    diag_prec,
    low_rank,
):
    rows, panels = rhs_vec.shape
    block_count, slots, block, _ = near_mats.shape
    rank = interp.shape[2]
    quarters = lax.axis_size("rhs")
    count = lax.axis_size(AXIS)
    width = low_rank.shape[1]
    sources = 4 if count == 8 else 3
    weights = jnp.swapaxes(interp, 1, 2)
    maps, places = call(
        "maps",
        lambda *refs: maps_kernel(sources, *refs),
        [((quarters, 2 * LANES, panels // quarters), BF), ((block_count, LANES), jnp.int32)],
        [near_ids, near_count[None, :], weights, skel_idx],
    )
    wide = width + LANES
    long = panels + quarters * LANES
    paired = count == 8 and quarters == 4
    parts = 4
    args = [rhs_vec, low_rank, diag_prec[None, :], self_coef[None, :]]
    outs = [((rows, wide), F32), ((rows, panels), F32), ((1, panels), F32),
            ((1, panels), F32), (low_rank.shape, BF), (low_rank.shape, BF)]
    scratch = [pltpu.VMEM((panels, width), F32)]
    if paired:
        args += [weights, skel_idx]
        tall = block_count // quarters * rank * block // width
        packed = panels // quarters + tall + 16 + 2 * rows * panels // width
        outs += [((packed, width), BF)]
        scratch += [pltpu.VMEM(weights.shape, BF), pltpu.VMEM(skel_idx.shape, jnp.int32)]
    payload, rhs_near, diag_row, self_row, high, low, *packs = call(
        "open",
        lambda *refs: open_kernel(parts, paired, *refs),
        outs,
        args,
        scratch + [pltpu.SemaphoreType.DMA((parts + 5,))],
        far=range(len(args)),
    )
    some_rows, payload = gather_quarters(coupling[:, 0, :], quarters, count, payload)
    sums = sum_parts(payload, count)
    if paired:
        mine = swap(packs[0], 1, count)
    first_dir, first_pre, keep, send = call(
        "first",
        lambda *refs: first_kernel(len(sums), *refs),
        [((rows, panels), F32), ((rows, panels), F32), ((rows, wide), F32), ((rows, long), BF)],
        [*sums, rhs_near, diag_row, high, low, maps],
        flops=2*10**9,
    )
    fields, charges, starts = exchange(send, panels, count)
    full_rows, fields[1] = finish_quarters(some_rows, quarters, fields[1])
    if paired:
        mine, fields[1] = lax.optimization_barrier((mine, fields[1]))
        far = lax.ppermute(mine, "rhs", [(i, i ^ 2) for i in range(quarters)])

    def near_product(fields):
        (near,) = call(
            "near",
            lambda *refs: near_kernel(len(fields), *refs),
            [((rows, panels), F32)],
            [*fields, places, near_mats],
            [pltpu.VMEM((len(fields) * block_count + 1, rows, block), BF)],
            flops=10**10,
        )
        return near

    near = near_product(fields)
    scratch = [pltpu.VMEM((quarters, count // 2, rows, LANES), BF)]
    residue, scaled, payload = call(
        "second",
        lambda *refs: second_kernel(starts, *refs),
        [((rows, panels), F32), ((rows, panels), F32), ((rows, wide), F32)],
        [*charges, first_dir, first_pre, self_row, diag_row, near, maps, high, low, *full_rows],
        scratch,
        flops=10**10,
    )
    if paired:
        mine, payload = lax.optimization_barrier((mine, payload))
    sums = sum_parts(payload, count)
    outs = [((rows, panels), F32), ((rows, panels), F32), ((rows, LANES), F32)]
    extra = []
    if paired:
        again = swap(scaled, 1, count)
        far, sums[0] = lax.optimization_barrier((far, sums[0]))
        near_pack, last_pack = [
            lax.ppermute(x, "rhs", [(i, i ^ 1) for i in range(quarters)]) for x in (mine, far)
        ]
        mine = [mine, near_pack, far, last_pack]
        (some_maps,) = call(
            "other_maps",
            lambda *refs: other_maps_kernel(panels // quarters, rank, block, *refs),
            [(maps.shape, BF)],
            mine[:-1],
            flops=10**10,
        )
        extra = [again, *mine, some_maps]
        outs = [((rows, long), BF), ((rows, long - panels), BF), *outs, ((rows, panels), BF)]
    else:
        outs += [((rows, long), BF)]
    *onward, second_dir, second_pre, scalars, send = call(
        "third",
        lambda *refs: third_kernel(len(sums), paired * rank, block, *refs),
        outs,
        [*sums, residue, first_dir, keep, diag_row, high, low, maps, *extra],
        [pltpu.VMEM(maps.shape, BF)] if paired else [],
    )
    if paired:
        fields, charges, starts = exchange_z(send, *onward, panels, count)
    else:
        fields, charges, starts = exchange(send, panels, count)
    near = near_product(fields)
    (tail,) = call(
        "fourth",
        lambda *refs: fourth_kernel(starts, *refs),
        [((rows, LANES), F32)],
        [*charges, first_dir, second_dir, second_pre, self_row, near, maps, *full_rows],
        scratch,
    )
    sums = sum_parts(tail, count)
    (result,) = call(
        "last",
        lambda *refs: last_kernel(len(sums), *refs),
        [((rows, panels), F32)],
        [*sums, scalars, first_pre, second_pre],
    )
    return result


def solution(mesh):
    placed = (
        P("rhs", "space"),
        P("space"),
        P("space", None, None, None),
        P("space", None),
        P("space"),
        P("space", None, None),
        P("space", None),
        P("space", "rhs", None),
        P("space"),
        P("space", None),
    )
    return jax.shard_map(
        on_device, mesh=mesh, in_specs=placed, out_specs=P("rhs", "space"), check_vma=False
    )
```

```python
import math

import jax
import jax.numpy as jnp
from jax import lax
from jax.experimental import pallas as pl
from jax.experimental.pallas import tpu as pltpu
from jax.sharding import PartitionSpec as P

EPS = 1e-06
F32 = jnp.float32
BF = jnp.bfloat16
AXIS = "space"
LANES = 128
HALF = 64


def swap(values, mask, count):
    return lax.ppermute(values, AXIS, [(i, i ^ mask) for i in range(count)])


def split(values):
    high = values.astype(BF)
    return high, (values - high.astype(F32)).astype(BF)


def dot_nn(left, right):
    return lax.dot_general(left, right, (((1,), (0,)), ((), ())), preferred_element_type=F32)


def dot_nt(left, right):
    return lax.dot_general(left, right, (((1,), (1,)), ((), ())), preferred_element_type=F32)


def dot_wide(dot, vector, high, low):
    rows = vector.shape[0]
    vec_high, vec_low = split(vector)
    first = dot(jnp.concatenate([vec_high, vec_low], axis=0), high)
    return first[:rows] + first[rows:] + dot(vec_high, low)


def row_sum(values):
    return jnp.sum(values, axis=1, keepdims=True)


def put_scalars(columns, rows):
    lane = lax.broadcasted_iota(jnp.int32, (rows, LANES), 1)
    out = jnp.zeros((rows, LANES), F32)
    for index, column in enumerate(columns):
        out = jnp.where(lane == index, column, out)
    return out


def column(values, index):
    return values[:, index : index + 1]


def charge_rows(field_low, maps_ref, send_ref):
    rows, panels = field_low.shape
    quarters, _, width = maps_ref.shape
    for quarter in range(quarters):
        both = dot_nt(field_low[:, quarter * width : (quarter + 1) * width], maps_ref[quarter])
        start = panels + quarter * LANES
        send_ref[:, start : start + LANES] = (both[:, :LANES] + both[:, LANES:]).astype(BF)


def build_maps(maps_ref, odd_start, skel, weights, block_count, rank, block):
    quarters = maps_ref.shape[0]
    per = block_count // quarters
    odd_start = pl.multiple_of(odd_start, HALF)
    maps_ref[...] = jnp.zeros(maps_ref.shape, BF)
    panel = lax.broadcasted_iota(jnp.int32, (rank, block), 1).astype(F32)
    for b in range(block_count):
        quarter, index = divmod(b, per)
        start = odd_start + index * rank
        cols = slice(index * block, (index + 1) * block)
        hot = jnp.where(skel[:rank, b : b + 1] == panel, 1.0, 0.0).astype(BF)
        maps_ref[quarter, pl.ds(start, rank), cols] = hot
        maps_ref[quarter, pl.ds(start + LANES, rank), cols] = weights(b)


def maps_kernel(sources, ids_ref, live_ref, weights_ref, skel_ref, maps_ref, places_ref):
    block_count, rank, block = weights_ref.shape
    skel = jnp.concatenate(
        [skel_ref[...].astype(F32), jnp.zeros((block_count, LANES - rank), F32)], axis=1
    ).T
    odd_start = (lax.axis_index(AXIS) % 2) * HALF
    build_maps(maps_ref, odd_start, skel, lambda b: weights_ref[b], block_count, rank, block)
    wanted = ids_ref[...]
    slots = wanted.shape[1]
    slot = lax.broadcasted_iota(jnp.int32, wanted.shape, 1)
    row = lax.broadcasted_iota(jnp.int32, wanted.shape, 0)
    counts = live_ref[...]
    live = slot < 0
    for b in range(block_count):
        live = live | ((row == b) & (slot < counts[0, b]))
    region = lax.axis_index(AXIS)
    place = block_place(wanted, live, block_count, sources, region).astype(F32)
    scale = jnp.where(slot % 4 == 0, 1.0, jnp.where(slot % 4 == 1, 64.0, 4096.0))
    scale = jnp.where(slot % 4 == 3, 262144.0, scale)
    lane = lax.broadcasted_iota(jnp.int32, (block_count, LANES), 1)
    packed = jnp.zeros((block_count, LANES), F32)
    for group in range(slots // 4):
        part = row_sum(jnp.where(slot // 4 == group, place * scale, 0.0))
        packed = jnp.where(lane == group, part, packed)
    places_ref[...] = packed.astype(jnp.int32)


def other_maps(base, rank, block, packs, maps_ref):
    chunks = packs[0][1].shape[1] // block
    per = maps_ref.shape[2] // block
    tall = per * rank // chunks
    odd_start = pl.multiple_of((1 - lax.axis_index(AXIS) % 2) * HALF, HALF)
    panel = lax.broadcasted_iota(jnp.int32, (rank, block), 1).astype(F32)
    for mask, ref in packs:
        quarter = lax.axis_index("rhs") ^ mask
        skel = ref[base + tall : base + tall + 16, :LANES].astype(F32)
        skel = jnp.concatenate([skel, jnp.zeros((LANES - 16, LANES), F32)], axis=0).T
        weights = jnp.concatenate(
            [ref[base : base + tall, j * block : (j + 1) * block] for j in range(chunks)], axis=0
        )
        for index in range(per):
            start = odd_start + index * rank
            cols = slice(index * block, (index + 1) * block)
            hot = jnp.where(skel[:rank, index : index + 1] == panel, 1.0, 0.0).astype(BF)
            maps_ref[quarter, pl.ds(start, rank), cols] = hot
            maps_ref[quarter, pl.ds(start + LANES, rank), cols] = weights[
                index * rank : (index + 1) * rank
            ]


def other_maps_kernel(base, rank, block, *refs):
    *pack_refs, maps_ref = refs
    maps_ref[...] = jnp.zeros(maps_ref.shape, BF)
    other_maps(base, rank, block, list(enumerate(pack_refs)), maps_ref)


def onward_kernel(send_ref, near_ref, onward_ref, pair_ref):
    panels = near_ref.shape[1] - pair_ref.shape[1]
    pair = send_ref[:, panels:] + near_ref[:, panels:]
    onward_ref[:, :panels] = near_ref[:, :panels]
    onward_ref[:, panels:] = pair
    pair_ref[...] = pair


def neighbour_field(panels, scaled, proj, part_refs, onward_ref):
    rows = proj.shape[0]
    both = jnp.concatenate(split(proj), axis=0)
    size = panels // len(part_refs)
    for mask, ref in enumerate(part_refs):
        part = dot_nt(both, ref[:size, :])
        start = pl.multiple_of((lax.axis_index("rhs") ^ mask) * size, size)
        field = scaled(start, size) - (part[:rows] + part[rows:])
        onward_ref[:, pl.ds(start, size)] = field.astype(BF)


def pair_charges(field_low, maps_ref, other_maps_ref, onward_ref, pair_ref):
    panels = field_low.shape[1]
    quarters, _, width = maps_ref.shape
    for quarter in range(quarters):
        cols = slice(quarter * width, (quarter + 1) * width)
        both = dot_nt(field_low[:, cols], maps_ref[quarter])
        both = both + dot_nt(onward_ref[:, cols], other_maps_ref[quarter])
        charge = (both[:, :LANES] + both[:, LANES:]).astype(BF)
        pair_ref[:, quarter * LANES : (quarter + 1) * LANES] = charge
        onward_ref[:, panels + quarter * LANES : panels + (quarter + 1) * LANES] = charge


def open_kernel(parts, paired, rhs_hbm, factor_hbm, diag_hbm, self_hbm, *refs):
    if paired:
        weights_hbm, skel_hbm, out_ref, rhs_ref, diag_ref, self_ref, high_ref, low_ref = refs[:8]
        pack_ref, held_ref, weights_ref, skel_ref, sems = refs[8:]
    else:
        out_ref, rhs_ref, diag_ref, self_ref, high_ref, low_ref, held_ref, sems = refs
    panels, width = factor_hbm.shape
    rows = rhs_ref.shape[0]
    depth = panels // parts
    pairs = [(rhs_hbm, rhs_ref), (diag_hbm, diag_ref), (self_hbm, self_ref)]
    if paired:
        pairs += [(weights_hbm, weights_ref), (skel_hbm, skel_ref)]
    loads = [
        pltpu.make_async_copy(source, target, sems.at[parts + index])
        for index, (source, target) in enumerate(pairs)
    ]
    for load in loads:
        load.start()
    copies = []
    for part in range(parts):
        span = pl.ds(part * depth, depth)
        copies.append(
            pltpu.make_async_copy(factor_hbm.at[span], held_ref.at[span], sems.at[part])
        )
        copies[-1].start()
    for load in loads:
        load.wait()
    rhs = rhs_ref[...]
    out_ref[:, width:] = put_scalars([row_sum(rhs * rhs)], rows)
    if paired:
        block_count, rank, block = weights_ref.shape
        quarters = lax.axis_size("rhs")
        quarter = lax.axis_index("rhs")
        size = panels // quarters
        per = block_count // quarters
        chunks = width // block
        tall = per * rank // chunks
        for index in range(per):
            values = weights_ref[quarter * per + index]
            for part in range(rank // tall):
                chunk = index * (rank // tall) + part
                pack_ref[size : size + tall, chunk * block : (chunk + 1) * block] = values[
                    part * tall : (part + 1) * tall
                ]
        skel = skel_ref[...].astype(F32)
        skel = jnp.concatenate([skel, jnp.zeros((block_count, width - rank), F32)], axis=1)
        row = lax.broadcasted_iota(jnp.int32, skel.shape, 0)
        picked = [
            jnp.sum(jnp.where(row == quarter * per + index, skel, 0.0), axis=0, keepdims=True)
            for index in range(per)
        ]
        picked.append(jnp.zeros((16 - per, width), F32))
        pack_ref[size + tall : size + tall + 16, :] = jnp.concatenate(picked, axis=0).astype(BF)
        start = size + tall + 16
        for part in split(diag_ref[...] * rhs):
            for first in range(0, panels, width):
                pack_ref[start : start + rows, :] = part[:, first : first + width]
                start += rows
    total = jnp.zeros((rows, width), F32)
    for part in range(parts):
        span = slice(part * depth, (part + 1) * depth)
        copies[part].wait()
        high, low = split(held_ref[span, :])
        high_ref[span, :] = high
        low_ref[span, :] = low
        total = total + dot_wide(dot_nn, rhs[:, span], high, low)
    out_ref[:, :width] = total
    if paired:
        pack_ref[:size, :] = high_ref[pl.ds(pl.multiple_of(quarter * size, size), size), :]


def turn_kernel(high_ref, low_ref, high_turned_ref, low_turned_ref):
    high_turned_ref[...] = high_ref[...].T
    low_turned_ref[...] = low_ref[...].T


def first_kernel(parts, *refs):
    sums = refs[:parts]
    rhs_ref, diag_ref, high_ref, low_ref, maps_ref = refs[parts : parts + 5]
    dir_ref, pre_ref, keep_ref, send_ref = refs[parts + 5 :]
    width = high_ref.shape[0]
    rows, panels = rhs_ref.shape
    summed = sums[0][...]
    for ref in sums[1:]:
        summed = summed + ref[...]
    rhs_sq = column(summed[:, width:], 0)
    start_len = jnp.sqrt(rhs_sq + EPS)
    first_dir = rhs_ref[...] / start_len
    proj = summed[:, :width] / start_len
    first_pre = diag_ref[...] * first_dir - dot_wide(dot_nn, proj, high_ref[...], low_ref[...])
    field_low = first_pre.astype(BF)
    dir_ref[...] = first_dir
    pre_ref[...] = first_pre
    send_ref[:, :panels] = field_low
    charge_rows(field_low, maps_ref, send_ref)
    keep_ref[:, :width] = proj
    keep_ref[:, width:] = put_scalars([start_len, rhs_sq / (start_len * start_len)], rows)


def block_place(wanted, live, block_count, sources, region):
    source = wanted // block_count
    if sources == 4:
        slot = jnp.where(
            source == region,
            0,
            jnp.where(source == region ^ 1, 1, jnp.where(source == region ^ 3, 2, 3)),
        )
    else:
        slot = source - region + 1
    return jnp.where(live, slot * block_count + wanted % block_count, sources * block_count)


def near_kernel(sources, *refs):
    field_refs = refs[:sources]
    places_ref, mats_ref, near_ref, blocks_ref = refs[sources:]
    rows, panels = near_ref.shape
    block_count, slots, block, _ = mats_ref.shape
    packed = places_ref[...]
    for index, ref in enumerate(field_refs):
        for b in range(block_count):
            blocks_ref[index * block_count + b] = ref[:, b * block : (b + 1) * block]
    blocks_ref[sources * block_count] = jnp.zeros((rows, block), BF)
    for b in range(block_count):
        fours = [packed[b, group] for group in range(slots // 4)]
        places = [(fours[k // 4] >> (6 * (k % 4))) & 63 for k in range(slots)]
        picked = jnp.concatenate([blocks_ref[place] for place in places], axis=1)
        mats = jnp.concatenate([mats_ref[b, k] for k in range(slots)], axis=1)
        near_ref[:, b * block : (b + 1) * block] = dot_nt(picked, mats)


def apply_matrix(field_ref, self_ref, near_ref, charge_refs, coupling_refs, maps_ref, charges_ref):
    rows, panels = field_ref.shape
    quarters, pairs = charges_ref.shape[:2]
    gathered = len(coupling_refs) == 1
    region = lax.axis_index(AXIS)
    first_quarter = 0 if gathered else lax.axis_index("rhs")
    for quarter in range(quarters):
        for index in range(pairs):
            if len(charge_refs) == pairs:
                ref, start = charge_refs[index]
                start += quarter * LANES
                charge = ref[:, start : start + LANES]
                charges_ref[quarter, (region // 2) ^ index] = charge
            else:
                lanes = slice(quarter * LANES, (quarter + 1) * LANES)
                charges_ref[quarter, index] = charge_refs[0][0][index, :, lanes]
    far = jnp.zeros((rows, coupling_refs[0].shape[-2]), F32)
    for index in range(quarters):
        quarter = first_quarter ^ index
        charge = jnp.concatenate([charges_ref[quarter, t] for t in range(pairs)], axis=1)
        rows_in = coupling_refs[0][index] if gathered else coupling_refs[index][...]
        far = far + dot_nt(charge, rows_in)
    odd = (region % 2) == 1
    per = panels // quarters
    for quarter in range(quarters):
        start = (quarter // 2) * LANES
        chunk = far[:, start : start + LANES]
        turned = pltpu.roll(chunk, HALF, 1)
        chunk = jnp.where(odd, turned, chunk) if quarter % 2 == 0 else jnp.where(odd, chunk, turned)
        high, low = split(chunk)
        both = jnp.concatenate([high, low], axis=0)
        pot = dot_nn(jnp.concatenate([both, both], axis=1), maps_ref[quarter])
        cols = slice(quarter * per, (quarter + 1) * per)
        near = near_ref[:, cols] + (pot[:rows] + pot[rows:])
        yield cols, near + self_ref[:, cols] * field_ref[:, cols]


def second_kernel(charge_starts, *refs):
    parts = len(charge_starts)
    charge_refs = list(zip(refs[:parts], charge_starts))
    dir_ref, pre_ref, self_ref, diag_ref = refs[parts : parts + 4]
    near_ref, maps_ref, high_ref, low_ref = refs[parts + 4 : parts + 8]
    *coupling_refs, res_ref, scaled_ref, out_ref, charges_ref = refs[parts + 8 :]
    width = high_ref.shape[1]
    rows = pre_ref.shape[0]
    for cols, values in apply_matrix(
        pre_ref, self_ref, near_ref, charge_refs, coupling_refs, maps_ref, charges_ref
    ):
        res_ref[:, cols] = values
    res = res_ref[...]
    out_ref[:, :width] = dot_wide(dot_nn, res, high_ref[...], low_ref[...])
    out_ref[:, width:] = put_scalars([row_sum(res * dir_ref[...]), row_sum(res * res)], rows)
    scaled_ref[...] = diag_ref[...] * res


def third_kernel(parts, rank, block, *refs):
    if rank:
        *refs, other_maps_ref = refs
    sums = refs[:parts]
    res_ref, dir_ref, keep_ref, diag_ref, high_ref, low_ref, maps_ref = refs[parts : parts + 7]
    *extra, next_ref, pre_ref, scalars_ref, send_ref = refs[parts + 7 :]
    width = high_ref.shape[0]
    rows, panels = res_ref.shape
    summed = sums[0][...]
    for ref in sums[1:]:
        summed = summed + ref[...]
    keep = keep_ref[:, width:]
    start_len, first_sq = column(keep, 0), column(keep, 1)
    diag_one, res_sq = column(summed[:, width:], 0), column(summed[:, width:], 1)
    below_sq = jnp.maximum(res_sq - diag_one * diag_one * (2.0 - first_sq), 0.0)
    below_one = jnp.sqrt(below_sq + EPS)
    second_dir = (res_ref[...] - diag_one * dir_ref[...]) / below_one
    proj = (summed[:, :width] - diag_one * keep_ref[:, :width]) / below_one
    pre = diag_ref[...] * second_dir - dot_wide(dot_nn, proj, high_ref[...], low_ref[...])
    field_low = pre.astype(BF)
    pre_ref[...] = pre
    if extra:
        got_ref, *part_refs, some_maps_ref, onward_ref, pair_ref = extra
        other_maps_ref[...] = some_maps_ref[...]
        last = len(part_refs) - 1
        other_maps(panels // (last + 1), rank, block, [(last, part_refs[last])], other_maps_ref)
        ratio = diag_one / start_len
        count = panels // width
        base = part_refs[0].shape[0] - 2 * count * rows
        before = []
        for index in range(count):
            high_rows = pl.ds(base + index * rows, rows)
            low_rows = pl.ds(base + (index + count) * rows, rows)
            before.append(
                part_refs[0][high_rows, :].astype(F32) + part_refs[0][low_rows, :].astype(F32)
            )
        scaled_ref = next_ref
        scaled_ref[...] = (
            got_ref[...] - ratio * jnp.concatenate(before, axis=1)
        ) / below_one

        def scaled(start, size):
            return scaled_ref[:, pl.ds(start, size)]

        neighbour_field(panels, scaled, proj, part_refs, onward_ref)
        send_ref[...] = field_low
        pair_charges(field_low, maps_ref, other_maps_ref, onward_ref, pair_ref)
    else:
        send_ref[:, :panels] = field_low
        charge_rows(field_low, maps_ref, send_ref)
    next_ref[...] = second_dir
    cross = diag_one * (1.0 - first_sq) / below_one
    second_sq = below_sq / (below_one * below_one)
    scalars_ref[...] = put_scalars(
        [start_len, first_sq, diag_one, below_one, cross, second_sq], rows
    )


def fourth_kernel(charge_starts, *refs):
    parts = len(charge_starts)
    charge_refs = list(zip(refs[:parts], charge_starts))
    dir_ref, next_ref, pre_ref, self_ref, near_ref, maps_ref = refs[parts : parts + 6]
    *coupling_refs, out_ref, charges_ref = refs[parts + 6 :]
    rows = pre_ref.shape[0]
    upper = diag = square = 0.0
    for cols, values in apply_matrix(
        pre_ref, self_ref, near_ref, charge_refs, coupling_refs, maps_ref, charges_ref
    ):
        upper = upper + row_sum(values * dir_ref[:, cols])
        diag = diag + row_sum(values * next_ref[:, cols])
        square = square + row_sum(values * values)
    out_ref[...] = put_scalars([upper, diag, square], rows)


def givens_pair(start_len, diag_one, below_one, upper_two, diag_two, below_two):
    radius_one = jnp.sqrt(diag_one * diag_one + below_one * below_one)
    cos_one = diag_one / radius_one
    sin_one = below_one / radius_one
    upper = cos_one * upper_two + sin_one * diag_two
    lower = cos_one * diag_two - sin_one * upper_two
    radius_two = jnp.sqrt(lower * lower + below_two * below_two)
    step_two = lower / radius_two * (-sin_one * start_len) / radius_two
    step_one = (cos_one * start_len - upper * step_two) / radius_one
    return (step_one, step_two)


def last_kernel(parts, *refs):
    scalars_ref, first_ref, second_ref, out_ref = refs[parts:]
    summed = refs[0][...]
    for ref in refs[1:parts]:
        summed = summed + ref[...]
    start_len, first_sq, diag_one, below_one, cross, second_sq = [
        column(scalars_ref[...], i) for i in range(6)
    ]
    upper_two, diag_two, res_sq = [column(summed, i) for i in range(3)]
    left_sq = (
        res_sq
        - upper_two * upper_two * (2.0 - first_sq)
        - diag_two * diag_two * (2.0 - second_sq)
        + 2.0 * upper_two * diag_two * cross
    )
    below_two = jnp.sqrt(jnp.maximum(left_sq, 0.0) + EPS)
    step_one, step_two = givens_pair(
        start_len, diag_one, below_one, upper_two, diag_two, below_two
    )
    out_ref[...] = step_one * first_ref[...] + step_two * second_ref[...]


def sum_parts(values, count, beside=()):
    if count != 8:
        return [lax.psum(values, AXIS)], beside
    pair = values + swap(values, 1, count)
    pair, *beside = lax.optimization_barrier((pair, *beside))
    return [pair, swap(pair, 2, count), swap(pair, 4, count), swap(pair, 6, count)], beside


def exchange_z(field, onward, pair, panels, count):
    two = swap(onward, 2, count)
    four = swap(pair, 4, count)
    six = swap(onward, 6, count)
    return [field, onward, two, six], [pair, two, four, six], [0, panels, 0, panels]


def exchange(send, panels, count):
    if count == 8:
        near = swap(send, 1, count)
        rows, long = send.shape
        onward, pair = call(
            "onward", onward_kernel, [((rows, long), BF), ((rows, long - panels), BF)], [send, near]
        )
        fields, charges, starts = exchange_z(send, onward, pair, panels, count)
        return [send, near] + fields[2:], charges, starts
    field, charges = send[:, :panels], send[:, panels:]
    ends = count - 1
    lower = lax.ppermute(field, AXIS, [(i, i + 1) for i in range(ends)])
    upper = lax.ppermute(field, AXIS, [(i + 1, i) for i in range(ends)])
    every = lax.all_gather(charges, AXIS)
    every = every.reshape((count // 2, 2) + charges.shape)
    return [lower, send, upper], [every[:, 0] + every[:, 1]], [0]


def gather_quarters(coupling, quarters, count, early):
    if count != 8 or quarters != 4:
        return [lax.all_gather(coupling, "rhs")], early
    coupling, early = lax.optimization_barrier((coupling, early))
    pairs = [[(i, i ^ mask) for i in range(quarters)] for mask in (1, 2)]
    return [coupling] + [lax.ppermute(coupling, "rhs", pair) for pair in pairs], early


def finish_quarters(rows, quarters, late):
    if len(rows) == 1:
        return rows, late
    far, late = lax.optimization_barrier((rows[2], late))
    return rows + [lax.ppermute(far, "rhs", [(i, i ^ 1) for i in range(quarters)])], late


def nbytes(shape, kind):
    return math.prod(shape) * jnp.dtype(kind).itemsize


def room(*arrays):
    return pltpu.CompilerParams(
        vmem_limit_bytes=sum(nbytes(a.shape, a.dtype) for a in arrays) * 5 // 4 + 4 * 2**20
    )


def call(name, kernel, out_shapes, args, scratch=(), far=(), flops=0):
    out_shapes = [jax.ShapeDtypeStruct(shape, kind) for shape, kind in out_shapes]
    args = [pltpu.with_memory_space_constraint(x, pltpu.HBM) if i in far else x
            for i, x in enumerate(args)]
    specs = [
        pl.BlockSpec(
            memory_space=pltpu.HBM if i in far else pltpu.VMEM
        )
        for i in range(len(args))
    ]
    outs = [pl.BlockSpec(memory_space=pltpu.VMEM)] * len(out_shapes)
    held = [x for i, x in enumerate(args) if i not in far]
    held += [x for x in scratch if getattr(x, "memory_space", None) == pltpu.VMEM]
    return pl.pallas_call(
        kernel,
        name=name,
        out_shape=out_shapes,
        in_specs=specs,
        out_specs=outs,
        scratch_shapes=list(scratch),
        cost_estimate=pl.CostEstimate(flops=flops, bytes_accessed=flops // 500, transcendentals=0) if flops else None,
        compiler_params=room(*held, *out_shapes),
    )(*args)


def on_device(
    rhs_vec,
    self_coef,
    near_mats,
    near_ids,
    near_count,
    interp,
    skel_idx,
    coupling,
    diag_prec,
    low_rank,
):
    rows, panels = rhs_vec.shape
    block_count, slots, block, _ = near_mats.shape
    rank = interp.shape[2]
    quarters = lax.axis_size("rhs")
    count = lax.axis_size(AXIS)
    width = low_rank.shape[1]
    sources = 4 if count == 8 else 3
    weights = jnp.swapaxes(interp, 1, 2)
    maps, places = call(
        "maps",
        lambda *refs: maps_kernel(sources, *refs),
        [((quarters, 2 * LANES, panels // quarters), BF), ((block_count, LANES), jnp.int32)],
        [near_ids, near_count[None, :], weights, skel_idx],
    )
    wide = width + LANES
    long = panels + quarters * LANES
    paired = count == 8 and quarters == 4
    parts = 4
    args = [rhs_vec, low_rank, diag_prec[None, :], self_coef[None, :]]
    outs = [((rows, wide), F32), ((rows, panels), F32), ((1, panels), F32),
            ((1, panels), F32), (low_rank.shape, BF), (low_rank.shape, BF)]
    scratch = [pltpu.VMEM((panels, width), F32)]
    if paired:
        args += [weights, skel_idx]
        tall = block_count // quarters * rank * block // width
        packed = panels // quarters + tall + 16 + 2 * rows * panels // width
        outs += [((packed, width), BF)]
        scratch += [pltpu.VMEM(weights.shape, BF), pltpu.VMEM(skel_idx.shape, jnp.int32)]
    payload, rhs_near, diag_row, self_row, high, low, *packs = call(
        "open",
        lambda *refs: open_kernel(parts, paired, *refs),
        outs,
        args,
        scratch + [pltpu.SemaphoreType.DMA((parts + 5,))],
        far=range(len(args)),
    )
    turned = call("turn", turn_kernel, [((width, panels), BF)] * 2, [high, low])
    some_rows, payload = gather_quarters(coupling[:, 0, :], quarters, count, payload)
    sums, turned = sum_parts(payload, count, turned)
    if paired:
        mine = swap(packs[0], 1, count)
    first_dir, first_pre, keep, send = call(
        "first",
        lambda *refs: first_kernel(len(sums), *refs),
        [((rows, panels), F32), ((rows, panels), F32), ((rows, wide), F32), ((rows, long), BF)],
        [*sums, rhs_near, diag_row, *turned, maps],
        flops=2*10**9,
    )
    fields, charges, starts = exchange(send, panels, count)
    full_rows, fields[1] = finish_quarters(some_rows, quarters, fields[1])
    if paired:
        mine, fields[1] = lax.optimization_barrier((mine, fields[1]))
        far = lax.ppermute(mine, "rhs", [(i, i ^ 2) for i in range(quarters)])

    def near_product(fields):
        (near,) = call(
            "near",
            lambda *refs: near_kernel(len(fields), *refs),
            [((rows, panels), F32)],
            [*fields, places, near_mats],
            [pltpu.VMEM((len(fields) * block_count + 1, rows, block), BF)],
            flops=10**10,
        )
        return near

    near = near_product(fields)
    scratch = [pltpu.VMEM((quarters, count // 2, rows, LANES), BF)]
    residue, scaled, payload = call(
        "second",
        lambda *refs: second_kernel(starts, *refs),
        [((rows, panels), F32), ((rows, panels), F32), ((rows, wide), F32)],
        [*charges, first_dir, first_pre, self_row, diag_row, near, maps, high, low, *full_rows],
        scratch,
        flops=10**10,
    )
    if paired:
        mine, payload = lax.optimization_barrier((mine, payload))
    sums, _ = sum_parts(payload, count)
    outs = [((rows, panels), F32), ((rows, panels), F32), ((rows, LANES), F32)]
    extra = []
    if paired:
        again = swap(scaled, 1, count)
        far, sums[0] = lax.optimization_barrier((far, sums[0]))
        near_pack, last_pack = [
            lax.ppermute(x, "rhs", [(i, i ^ 1) for i in range(quarters)]) for x in (mine, far)
        ]
        mine = [mine, near_pack, far, last_pack]
        (some_maps,) = call(
            "other_maps",
            lambda *refs: other_maps_kernel(panels // quarters, rank, block, *refs),
            [(maps.shape, BF)],
            mine[:-1],
            flops=10**10,
        )
        extra = [again, *mine, some_maps]
        outs = [((rows, long), BF), ((rows, long - panels), BF), *outs, ((rows, panels), BF)]
    else:
        outs += [((rows, long), BF)]
    *onward, second_dir, second_pre, scalars, send = call(
        "third",
        lambda *refs: third_kernel(len(sums), paired * rank, block, *refs),
        outs,
        [*sums, residue, first_dir, keep, diag_row, *turned, maps, *extra],
        [pltpu.VMEM(maps.shape, BF)] if paired else [],
    )
    if paired:
        fields, charges, starts = exchange_z(send, *onward, panels, count)
    else:
        fields, charges, starts = exchange(send, panels, count)
    near = near_product(fields)
    (tail,) = call(
        "fourth",
        lambda *refs: fourth_kernel(starts, *refs),
        [((rows, LANES), F32)],
        [*charges, first_dir, second_dir, second_pre, self_row, near, maps, *full_rows],
        scratch,
    )
    sums, _ = sum_parts(tail, count)
    (result,) = call(
        "last",
        lambda *refs: last_kernel(len(sums), *refs),
        [((rows, panels), F32)],
        [*sums, scalars, first_pre, second_pre],
    )
    return result


def solution(mesh):
    placed = (
        P("rhs", "space"),
        P("space"),
        P("space", None, None, None),
        P("space", None),
        P("space"),
        P("space", None, None),
        P("space", None),
        P("space", "rhs", None),
        P("space"),
        P("space", None),
    )
    return jax.shard_map(
        on_device, mesh=mesh, in_specs=placed, out_specs=P("rhs", "space"), check_vma=False
    )
```

```python
import math

import jax
import jax.numpy as jnp
from jax import lax
from jax.experimental import pallas as pl
from jax.experimental.pallas import tpu as pltpu
from jax.sharding import PartitionSpec as P

EPS = 1e-06
F32 = jnp.float32
BF = jnp.bfloat16
AXIS = "space"
LANES = 128
HALF = 64


def swap(values, mask, count):
    return lax.ppermute(values, AXIS, [(i, i ^ mask) for i in range(count)])


def split(values):
    high = values.astype(BF)
    return high, (values - high.astype(F32)).astype(BF)


def dot_nn(left, right):
    return lax.dot_general(left, right, (((1,), (0,)), ((), ())), preferred_element_type=F32)


def dot_nt(left, right):
    return lax.dot_general(left, right, (((1,), (1,)), ((), ())), preferred_element_type=F32)


def dot_wide(dot, vector, high, low):
    rows = vector.shape[0]
    vec_high, vec_low = split(vector)
    first = dot(jnp.concatenate([vec_high, vec_low], axis=0), high)
    return first[:rows] + first[rows:] + dot(vec_high, low)


def row_sum(values):
    return jnp.sum(values, axis=1, keepdims=True)


def put_scalars(columns, rows):
    lane = lax.broadcasted_iota(jnp.int32, (rows, LANES), 1)
    out = jnp.zeros((rows, LANES), F32)
    for index, column in enumerate(columns):
        out = jnp.where(lane == index, column, out)
    return out


def column(values, index):
    return values[:, index : index + 1]


def charge_rows(field_low, maps_ref, send_ref):
    rows, panels = field_low.shape
    quarters, _, width = maps_ref.shape
    for quarter in range(quarters):
        both = dot_nt(field_low[:, quarter * width : (quarter + 1) * width], maps_ref[quarter])
        start = panels + quarter * LANES
        send_ref[:, start : start + LANES] = (both[:, :LANES] + both[:, LANES:]).astype(BF)


def build_maps(maps_ref, odd_start, skel, weights, block_count, rank, block):
    quarters = maps_ref.shape[0]
    per = block_count // quarters
    odd_start = pl.multiple_of(odd_start, HALF)
    maps_ref[...] = jnp.zeros(maps_ref.shape, BF)
    panel = lax.broadcasted_iota(jnp.int32, (rank, block), 1).astype(F32)
    for b in range(block_count):
        quarter, index = divmod(b, per)
        start = odd_start + index * rank
        cols = slice(index * block, (index + 1) * block)
        hot = jnp.where(skel[:rank, b : b + 1] == panel, 1.0, 0.0).astype(BF)
        maps_ref[quarter, pl.ds(start, rank), cols] = hot
        maps_ref[quarter, pl.ds(start + LANES, rank), cols] = weights(b)


def maps_kernel(sources, ids_ref, live_ref, weights_ref, skel_ref, maps_ref, places_ref):
    block_count, rank, block = weights_ref.shape
    skel = jnp.concatenate(
        [skel_ref[...].astype(F32), jnp.zeros((block_count, LANES - rank), F32)], axis=1
    ).T
    odd_start = (lax.axis_index(AXIS) % 2) * HALF
    build_maps(maps_ref, odd_start, skel, lambda b: weights_ref[b], block_count, rank, block)
    wanted = ids_ref[...]
    slots = wanted.shape[1]
    slot = lax.broadcasted_iota(jnp.int32, wanted.shape, 1)
    row = lax.broadcasted_iota(jnp.int32, wanted.shape, 0)
    counts = live_ref[...]
    live = slot < 0
    for b in range(block_count):
        live = live | ((row == b) & (slot < counts[0, b]))
    region = lax.axis_index(AXIS)
    place = block_place(wanted, live, block_count, sources, region).astype(F32)
    scale = jnp.where(slot % 4 == 0, 1.0, jnp.where(slot % 4 == 1, 64.0, 4096.0))
    scale = jnp.where(slot % 4 == 3, 262144.0, scale)
    lane = lax.broadcasted_iota(jnp.int32, (block_count, LANES), 1)
    packed = jnp.zeros((block_count, LANES), F32)
    for group in range(slots // 4):
        part = row_sum(jnp.where(slot // 4 == group, place * scale, 0.0))
        packed = jnp.where(lane == group, part, packed)
    places_ref[...] = packed.astype(jnp.int32)


def other_maps(base, rank, block, packs, maps_ref):
    chunks = packs[0][1].shape[1] // block
    per = maps_ref.shape[2] // block
    tall = per * rank // chunks
    odd_start = pl.multiple_of((1 - lax.axis_index(AXIS) % 2) * HALF, HALF)
    panel = lax.broadcasted_iota(jnp.int32, (rank, block), 1).astype(F32)
    for mask, ref in packs:
        quarter = lax.axis_index("rhs") ^ mask
        skel = ref[base + tall : base + tall + 16, :LANES].astype(F32)
        skel = jnp.concatenate([skel, jnp.zeros((LANES - 16, LANES), F32)], axis=0).T
        weights = jnp.concatenate(
            [ref[base : base + tall, j * block : (j + 1) * block] for j in range(chunks)], axis=0
        )
        for index in range(per):
            start = odd_start + index * rank
            cols = slice(index * block, (index + 1) * block)
            hot = jnp.where(skel[:rank, index : index + 1] == panel, 1.0, 0.0).astype(BF)
            maps_ref[quarter, pl.ds(start, rank), cols] = hot
            maps_ref[quarter, pl.ds(start + LANES, rank), cols] = weights[
                index * rank : (index + 1) * rank
            ]


def other_maps_kernel(base, rank, block, *refs):
    *pack_refs, maps_ref, turned_ref = refs
    for place, ref in enumerate(pack_refs):
        turned_ref[place] = ref[:base, :].T
    maps_ref[...] = jnp.zeros(maps_ref.shape, BF)
    other_maps(base, rank, block, list(enumerate(pack_refs)), maps_ref)


def onward_kernel(send_ref, near_ref, onward_ref, pair_ref):
    panels = near_ref.shape[1] - pair_ref.shape[1]
    pair = send_ref[:, panels:] + near_ref[:, panels:]
    onward_ref[:, :panels] = near_ref[:, :panels]
    onward_ref[:, panels:] = pair
    pair_ref[...] = pair


def neighbour_field(panels, scaled, proj, turned_ref, part_refs, onward_ref):
    rows = proj.shape[0]
    both = jnp.concatenate(split(proj), axis=0)
    size = panels // len(part_refs)
    for mask, ref in enumerate(part_refs):
        if mask < turned_ref.shape[0]:
            part = dot_nn(both, turned_ref[mask])
        else:
            part = dot_nt(both, ref[:size, :])
        start = pl.multiple_of((lax.axis_index("rhs") ^ mask) * size, size)
        field = scaled(start, size) - (part[:rows] + part[rows:])
        onward_ref[:, pl.ds(start, size)] = field.astype(BF)


def pair_charges(field_low, maps_ref, other_maps_ref, onward_ref, pair_ref):
    panels = field_low.shape[1]
    quarters, _, width = maps_ref.shape
    for quarter in range(quarters):
        cols = slice(quarter * width, (quarter + 1) * width)
        both = dot_nt(field_low[:, cols], maps_ref[quarter])
        both = both + dot_nt(onward_ref[:, cols], other_maps_ref[quarter])
        charge = (both[:, :LANES] + both[:, LANES:]).astype(BF)
        pair_ref[:, quarter * LANES : (quarter + 1) * LANES] = charge
        onward_ref[:, panels + quarter * LANES : panels + (quarter + 1) * LANES] = charge


def open_kernel(parts, paired, rhs_hbm, factor_hbm, diag_hbm, self_hbm, *refs):
    if paired:
        weights_hbm, skel_hbm, out_ref, rhs_ref, diag_ref, self_ref, high_ref, low_ref = refs[:8]
        pack_ref, held_ref, weights_ref, skel_ref, sems = refs[8:]
    else:
        out_ref, rhs_ref, diag_ref, self_ref, high_ref, low_ref, held_ref, sems = refs
    panels, width = factor_hbm.shape
    rows = rhs_ref.shape[0]
    depth = panels // parts
    pairs = [(rhs_hbm, rhs_ref), (diag_hbm, diag_ref), (self_hbm, self_ref)]
    if paired:
        pairs += [(weights_hbm, weights_ref), (skel_hbm, skel_ref)]
    loads = [
        pltpu.make_async_copy(source, target, sems.at[parts + index])
        for index, (source, target) in enumerate(pairs)
    ]
    for load in loads:
        load.start()
    copies = []
    for part in range(parts):
        span = pl.ds(part * depth, depth)
        copies.append(
            pltpu.make_async_copy(factor_hbm.at[span], held_ref.at[span], sems.at[part])
        )
        copies[-1].start()
    for load in loads:
        load.wait()
    rhs = rhs_ref[...]
    out_ref[:, width:] = put_scalars([row_sum(rhs * rhs)], rows)
    if paired:
        block_count, rank, block = weights_ref.shape
        quarters = lax.axis_size("rhs")
        quarter = lax.axis_index("rhs")
        size = panels // quarters
        per = block_count // quarters
        chunks = width // block
        tall = per * rank // chunks
        for index in range(per):
            values = weights_ref[quarter * per + index]
            for part in range(rank // tall):
                chunk = index * (rank // tall) + part
                pack_ref[size : size + tall, chunk * block : (chunk + 1) * block] = values[
                    part * tall : (part + 1) * tall
                ]
        skel = skel_ref[...].astype(F32)
        skel = jnp.concatenate([skel, jnp.zeros((block_count, width - rank), F32)], axis=1)
        row = lax.broadcasted_iota(jnp.int32, skel.shape, 0)
        picked = [
            jnp.sum(jnp.where(row == quarter * per + index, skel, 0.0), axis=0, keepdims=True)
            for index in range(per)
        ]
        picked.append(jnp.zeros((16 - per, width), F32))
        pack_ref[size + tall : size + tall + 16, :] = jnp.concatenate(picked, axis=0).astype(BF)
        start = size + tall + 16
        for part in split(diag_ref[...] * rhs):
            for first in range(0, panels, width):
                pack_ref[start : start + rows, :] = part[:, first : first + width]
                start += rows
    total = jnp.zeros((rows, width), F32)
    for part in range(parts):
        span = slice(part * depth, (part + 1) * depth)
        copies[part].wait()
        high, low = split(held_ref[span, :])
        high_ref[span, :] = high
        low_ref[span, :] = low
        total = total + dot_wide(dot_nn, rhs[:, span], high, low)
    out_ref[:, :width] = total
    if paired:
        pack_ref[:size, :] = high_ref[pl.ds(pl.multiple_of(quarter * size, size), size), :]


def turn_kernel(high_ref, low_ref, high_turned_ref, low_turned_ref):
    high_turned_ref[...] = high_ref[...].T
    low_turned_ref[...] = low_ref[...].T


def first_kernel(parts, *refs):
    sums = refs[:parts]
    rhs_ref, diag_ref, high_ref, low_ref, maps_ref = refs[parts : parts + 5]
    dir_ref, pre_ref, keep_ref, send_ref = refs[parts + 5 :]
    width = high_ref.shape[0]
    rows, panels = rhs_ref.shape
    summed = sums[0][...]
    for ref in sums[1:]:
        summed = summed + ref[...]
    rhs_sq = column(summed[:, width:], 0)
    start_len = jnp.sqrt(rhs_sq + EPS)
    first_dir = rhs_ref[...] / start_len
    proj = summed[:, :width] / start_len
    first_pre = diag_ref[...] * first_dir - dot_wide(dot_nn, proj, high_ref[...], low_ref[...])
    field_low = first_pre.astype(BF)
    dir_ref[...] = first_dir
    pre_ref[...] = first_pre
    send_ref[:, :panels] = field_low
    charge_rows(field_low, maps_ref, send_ref)
    keep_ref[:, :width] = proj
    keep_ref[:, width:] = put_scalars([start_len, rhs_sq / (start_len * start_len)], rows)


def block_place(wanted, live, block_count, sources, region):
    source = wanted // block_count
    if sources == 4:
        slot = jnp.where(
            source == region,
            0,
            jnp.where(source == region ^ 1, 1, jnp.where(source == region ^ 3, 2, 3)),
        )
    else:
        slot = source - region + 1
    return jnp.where(live, slot * block_count + wanted % block_count, sources * block_count)


def near_kernel(sources, *refs):
    field_refs = refs[:sources]
    places_ref, mats_ref, near_ref, blocks_ref = refs[sources:]
    rows, panels = near_ref.shape
    block_count, slots, block, _ = mats_ref.shape
    packed = places_ref[...]
    for index, ref in enumerate(field_refs):
        for b in range(block_count):
            blocks_ref[index * block_count + b] = ref[:, b * block : (b + 1) * block]
    blocks_ref[sources * block_count] = jnp.zeros((rows, block), BF)
    for b in range(block_count):
        fours = [packed[b, group] for group in range(slots // 4)]
        places = [(fours[k // 4] >> (6 * (k % 4))) & 63 for k in range(slots)]
        picked = jnp.concatenate([blocks_ref[place] for place in places], axis=1)
        mats = jnp.concatenate([mats_ref[b, k] for k in range(slots)], axis=1)
        near_ref[:, b * block : (b + 1) * block] = dot_nt(picked, mats)


def apply_matrix(field_ref, self_ref, near_ref, charge_refs, coupling_refs, maps_ref, charges_ref):
    rows, panels = field_ref.shape
    quarters, pairs = charges_ref.shape[:2]
    gathered = len(coupling_refs) == 1
    region = lax.axis_index(AXIS)
    first_quarter = 0 if gathered else lax.axis_index("rhs")
    for quarter in range(quarters):
        for index in range(pairs):
            if len(charge_refs) == pairs:
                ref, start = charge_refs[index]
                start += quarter * LANES
                charge = ref[:, start : start + LANES]
                charges_ref[quarter, (region // 2) ^ index] = charge
            else:
                lanes = slice(quarter * LANES, (quarter + 1) * LANES)
                charges_ref[quarter, index] = charge_refs[0][0][index, :, lanes]
    far = jnp.zeros((rows, coupling_refs[0].shape[-2]), F32)
    for index in range(quarters):
        quarter = first_quarter ^ index
        charge = jnp.concatenate([charges_ref[quarter, t] for t in range(pairs)], axis=1)
        rows_in = coupling_refs[0][index] if gathered else coupling_refs[index][...]
        far = far + dot_nt(charge, rows_in)
    odd = (region % 2) == 1
    per = panels // quarters
    for quarter in range(quarters):
        start = (quarter // 2) * LANES
        chunk = far[:, start : start + LANES]
        turned = pltpu.roll(chunk, HALF, 1)
        chunk = jnp.where(odd, turned, chunk) if quarter % 2 == 0 else jnp.where(odd, chunk, turned)
        high, low = split(chunk)
        both = jnp.concatenate([high, low], axis=0)
        pot = dot_nn(jnp.concatenate([both, both], axis=1), maps_ref[quarter])
        cols = slice(quarter * per, (quarter + 1) * per)
        near = near_ref[:, cols] + (pot[:rows] + pot[rows:])
        yield cols, near + self_ref[:, cols] * field_ref[:, cols]


def second_kernel(charge_starts, *refs):
    parts = len(charge_starts)
    charge_refs = list(zip(refs[:parts], charge_starts))
    dir_ref, pre_ref, self_ref, diag_ref = refs[parts : parts + 4]
    near_ref, maps_ref, high_ref, low_ref = refs[parts + 4 : parts + 8]
    *coupling_refs, res_ref, scaled_ref, out_ref, charges_ref = refs[parts + 8 :]
    width = high_ref.shape[1]
    rows = pre_ref.shape[0]
    for cols, values in apply_matrix(
        pre_ref, self_ref, near_ref, charge_refs, coupling_refs, maps_ref, charges_ref
    ):
        res_ref[:, cols] = values
    res = res_ref[...]
    out_ref[:, :width] = dot_wide(dot_nn, res, high_ref[...], low_ref[...])
    out_ref[:, width:] = put_scalars([row_sum(res * dir_ref[...]), row_sum(res * res)], rows)
    scaled_ref[...] = diag_ref[...] * res


def third_kernel(parts, rank, block, *refs):
    if rank:
        *refs, other_maps_ref = refs
    sums = refs[:parts]
    res_ref, dir_ref, keep_ref, diag_ref, high_ref, low_ref, maps_ref = refs[parts : parts + 7]
    *extra, next_ref, pre_ref, scalars_ref, send_ref = refs[parts + 7 :]
    width = high_ref.shape[0]
    rows, panels = res_ref.shape
    summed = sums[0][...]
    for ref in sums[1:]:
        summed = summed + ref[...]
    keep = keep_ref[:, width:]
    start_len, first_sq = column(keep, 0), column(keep, 1)
    diag_one, res_sq = column(summed[:, width:], 0), column(summed[:, width:], 1)
    below_sq = jnp.maximum(res_sq - diag_one * diag_one * (2.0 - first_sq), 0.0)
    below_one = jnp.sqrt(below_sq + EPS)
    second_dir = (res_ref[...] - diag_one * dir_ref[...]) / below_one
    proj = (summed[:, :width] - diag_one * keep_ref[:, :width]) / below_one
    pre = diag_ref[...] * second_dir - dot_wide(dot_nn, proj, high_ref[...], low_ref[...])
    field_low = pre.astype(BF)
    pre_ref[...] = pre
    if extra:
        got_ref, *part_refs, some_maps_ref, turned_ref, onward_ref, pair_ref = extra
        other_maps_ref[...] = some_maps_ref[...]
        last = len(part_refs) - 1
        other_maps(panels // (last + 1), rank, block, [(last, part_refs[last])], other_maps_ref)
        ratio = diag_one / start_len
        count = panels // width
        base = part_refs[0].shape[0] - 2 * count * rows
        before = []
        for index in range(count):
            high_rows = pl.ds(base + index * rows, rows)
            low_rows = pl.ds(base + (index + count) * rows, rows)
            before.append(
                part_refs[0][high_rows, :].astype(F32) + part_refs[0][low_rows, :].astype(F32)
            )
        scaled_ref = next_ref
        scaled_ref[...] = (
            got_ref[...] - ratio * jnp.concatenate(before, axis=1)
        ) / below_one

        def scaled(start, size):
            return scaled_ref[:, pl.ds(start, size)]

        neighbour_field(panels, scaled, proj, turned_ref, part_refs, onward_ref)
        send_ref[...] = field_low
        pair_charges(field_low, maps_ref, other_maps_ref, onward_ref, pair_ref)
    else:
        send_ref[:, :panels] = field_low
        charge_rows(field_low, maps_ref, send_ref)
    next_ref[...] = second_dir
    cross = diag_one * (1.0 - first_sq) / below_one
    second_sq = below_sq / (below_one * below_one)
    scalars_ref[...] = put_scalars(
        [start_len, first_sq, diag_one, below_one, cross, second_sq], rows
    )


def fourth_kernel(charge_starts, *refs):
    parts = len(charge_starts)
    charge_refs = list(zip(refs[:parts], charge_starts))
    dir_ref, next_ref, pre_ref, self_ref, near_ref, maps_ref = refs[parts : parts + 6]
    *coupling_refs, out_ref, charges_ref = refs[parts + 6 :]
    rows = pre_ref.shape[0]
    upper = diag = square = 0.0
    for cols, values in apply_matrix(
        pre_ref, self_ref, near_ref, charge_refs, coupling_refs, maps_ref, charges_ref
    ):
        upper = upper + row_sum(values * dir_ref[:, cols])
        diag = diag + row_sum(values * next_ref[:, cols])
        square = square + row_sum(values * values)
    out_ref[...] = put_scalars([upper, diag, square], rows)


def givens_pair(start_len, diag_one, below_one, upper_two, diag_two, below_two):
    radius_one = jnp.sqrt(diag_one * diag_one + below_one * below_one)
    cos_one = diag_one / radius_one
    sin_one = below_one / radius_one
    upper = cos_one * upper_two + sin_one * diag_two
    lower = cos_one * diag_two - sin_one * upper_two
    radius_two = jnp.sqrt(lower * lower + below_two * below_two)
    step_two = lower / radius_two * (-sin_one * start_len) / radius_two
    step_one = (cos_one * start_len - upper * step_two) / radius_one
    return (step_one, step_two)


def last_kernel(parts, *refs):
    scalars_ref, first_ref, second_ref, out_ref = refs[parts:]
    summed = refs[0][...]
    for ref in refs[1:parts]:
        summed = summed + ref[...]
    start_len, first_sq, diag_one, below_one, cross, second_sq = [
        column(scalars_ref[...], i) for i in range(6)
    ]
    upper_two, diag_two, res_sq = [column(summed, i) for i in range(3)]
    left_sq = (
        res_sq
        - upper_two * upper_two * (2.0 - first_sq)
        - diag_two * diag_two * (2.0 - second_sq)
        + 2.0 * upper_two * diag_two * cross
    )
    below_two = jnp.sqrt(jnp.maximum(left_sq, 0.0) + EPS)
    step_one, step_two = givens_pair(
        start_len, diag_one, below_one, upper_two, diag_two, below_two
    )
    out_ref[...] = step_one * first_ref[...] + step_two * second_ref[...]


def sum_parts(values, count, beside=()):
    if count != 8:
        return [lax.psum(values, AXIS)], beside
    pair = values + swap(values, 1, count)
    pair, *beside = lax.optimization_barrier((pair, *beside))
    return [pair, swap(pair, 2, count), swap(pair, 4, count), swap(pair, 6, count)], beside


def exchange_z(field, onward, pair, panels, count):
    two = swap(onward, 2, count)
    four = swap(pair, 4, count)
    six = swap(onward, 6, count)
    return [field, onward, two, six], [pair, two, four, six], [0, panels, 0, panels]


def exchange(send, panels, count):
    if count == 8:
        near = swap(send, 1, count)
        rows, long = send.shape
        onward, pair = call(
            "onward", onward_kernel, [((rows, long), BF), ((rows, long - panels), BF)], [send, near]
        )
        fields, charges, starts = exchange_z(send, onward, pair, panels, count)
        return [send, near] + fields[2:], charges, starts
    field, charges = send[:, :panels], send[:, panels:]
    ends = count - 1
    lower = lax.ppermute(field, AXIS, [(i, i + 1) for i in range(ends)])
    upper = lax.ppermute(field, AXIS, [(i + 1, i) for i in range(ends)])
    every = lax.all_gather(charges, AXIS)
    every = every.reshape((count // 2, 2) + charges.shape)
    return [lower, send, upper], [every[:, 0] + every[:, 1]], [0]


def gather_quarters(coupling, quarters, count, early):
    if count != 8 or quarters != 4:
        return [lax.all_gather(coupling, "rhs")], early
    coupling, early = lax.optimization_barrier((coupling, early))
    pairs = [[(i, i ^ mask) for i in range(quarters)] for mask in (1, 2)]
    return [coupling] + [lax.ppermute(coupling, "rhs", pair) for pair in pairs], early


def finish_quarters(rows, quarters, late):
    if len(rows) == 1:
        return rows, late
    far, late = lax.optimization_barrier((rows[2], late))
    return rows + [lax.ppermute(far, "rhs", [(i, i ^ 1) for i in range(quarters)])], late


def nbytes(shape, kind):
    return math.prod(shape) * jnp.dtype(kind).itemsize


def room(*arrays):
    return pltpu.CompilerParams(
        vmem_limit_bytes=sum(nbytes(a.shape, a.dtype) for a in arrays) * 5 // 4 + 4 * 2**20
    )


def call(name, kernel, out_shapes, args, scratch=(), far=(), flops=0):
    out_shapes = [jax.ShapeDtypeStruct(shape, kind) for shape, kind in out_shapes]
    args = [pltpu.with_memory_space_constraint(x, pltpu.HBM) if i in far else x
            for i, x in enumerate(args)]
    specs = [
        pl.BlockSpec(
            memory_space=pltpu.HBM if i in far else pltpu.VMEM
        )
        for i in range(len(args))
    ]
    outs = [pl.BlockSpec(memory_space=pltpu.VMEM)] * len(out_shapes)
    held = [x for i, x in enumerate(args) if i not in far]
    held += [x for x in scratch if getattr(x, "memory_space", None) == pltpu.VMEM]
    return pl.pallas_call(
        kernel,
        name=name,
        out_shape=out_shapes,
        in_specs=specs,
        out_specs=outs,
        scratch_shapes=list(scratch),
        cost_estimate=pl.CostEstimate(flops=flops, bytes_accessed=flops // 500, transcendentals=0) if flops else None,
        compiler_params=room(*held, *out_shapes),
    )(*args)


def on_device(
    rhs_vec,
    self_coef,
    near_mats,
    near_ids,
    near_count,
    interp,
    skel_idx,
    coupling,
    diag_prec,
    low_rank,
):
    rows, panels = rhs_vec.shape
    block_count, slots, block, _ = near_mats.shape
    rank = interp.shape[2]
    quarters = lax.axis_size("rhs")
    count = lax.axis_size(AXIS)
    width = low_rank.shape[1]
    sources = 4 if count == 8 else 3
    weights = jnp.swapaxes(interp, 1, 2)
    maps, places = call(
        "maps",
        lambda *refs: maps_kernel(sources, *refs),
        [((quarters, 2 * LANES, panels // quarters), BF), ((block_count, LANES), jnp.int32)],
        [near_ids, near_count[None, :], weights, skel_idx],
    )
    wide = width + LANES
    long = panels + quarters * LANES
    paired = count == 8 and quarters == 4
    parts = 4
    args = [rhs_vec, low_rank, diag_prec[None, :], self_coef[None, :]]
    outs = [((rows, wide), F32), ((rows, panels), F32), ((1, panels), F32),
            ((1, panels), F32), (low_rank.shape, BF), (low_rank.shape, BF)]
    scratch = [pltpu.VMEM((panels, width), F32)]
    if paired:
        args += [weights, skel_idx]
        tall = block_count // quarters * rank * block // width
        packed = panels // quarters + tall + 16 + 2 * rows * panels // width
        outs += [((packed, width), BF)]
        scratch += [pltpu.VMEM(weights.shape, BF), pltpu.VMEM(skel_idx.shape, jnp.int32)]
    payload, rhs_near, diag_row, self_row, high, low, *packs = call(
        "open",
        lambda *refs: open_kernel(parts, paired, *refs),
        outs,
        args,
        scratch + [pltpu.SemaphoreType.DMA((parts + 5,))],
        far=range(len(args)),
    )
    turned = call("turn", turn_kernel, [((width, panels), BF)] * 2, [high, low])
    some_rows, payload = gather_quarters(coupling[:, 0, :], quarters, count, payload)
    sums, turned = sum_parts(payload, count, turned)
    if paired:
        mine = swap(packs[0], 1, count)
    first_dir, first_pre, keep, send = call(
        "first",
        lambda *refs: first_kernel(len(sums), *refs),
        [((rows, panels), F32), ((rows, panels), F32), ((rows, wide), F32), ((rows, long), BF)],
        [*sums, rhs_near, diag_row, *turned, maps],
        flops=2*10**9,
    )
    fields, charges, starts = exchange(send, panels, count)
    full_rows, fields[1] = finish_quarters(some_rows, quarters, fields[1])
    if paired:
        mine, fields[1] = lax.optimization_barrier((mine, fields[1]))
        far = lax.ppermute(mine, "rhs", [(i, i ^ 2) for i in range(quarters)])

    def near_product(fields):
        (near,) = call(
            "near",
            lambda *refs: near_kernel(len(fields), *refs),
            [((rows, panels), F32)],
            [*fields, places, near_mats],
            [pltpu.VMEM((len(fields) * block_count + 1, rows, block), BF)],
            flops=10**10,
        )
        return near

    near = near_product(fields)
    scratch = [pltpu.VMEM((quarters, count // 2, rows, LANES), BF)]
    residue, scaled, payload = call(
        "second",
        lambda *refs: second_kernel(starts, *refs),
        [((rows, panels), F32), ((rows, panels), F32), ((rows, wide), F32)],
        [*charges, first_dir, first_pre, self_row, diag_row, near, maps, high, low, *full_rows],
        scratch,
        flops=10**10,
    )
    if paired:
        mine, payload = lax.optimization_barrier((mine, payload))
    sums, _ = sum_parts(payload, count)
    outs = [((rows, panels), F32), ((rows, panels), F32), ((rows, LANES), F32)]
    extra = []
    if paired:
        again = swap(scaled, 1, count)
        far, sums[0] = lax.optimization_barrier((far, sums[0]))
        near_pack, last_pack = [
            lax.ppermute(x, "rhs", [(i, i ^ 1) for i in range(quarters)]) for x in (mine, far)
        ]
        mine = [mine, near_pack, far, last_pack]
        extra = call(
            "other_maps",
            lambda *refs: other_maps_kernel(panels // quarters, rank, block, *refs),
            [(maps.shape, BF), ((quarters - 1, width, panels // quarters), BF)],
            mine[:-1],
            flops=10**10,
        )
        extra = [again, *mine, *extra]
        outs = [((rows, long), BF), ((rows, long - panels), BF), *outs, ((rows, panels), BF)]
    else:
        outs += [((rows, long), BF)]
    *onward, second_dir, second_pre, scalars, send = call(
        "third",
        lambda *refs: third_kernel(len(sums), paired * rank, block, *refs),
        outs,
        [*sums, residue, first_dir, keep, diag_row, *turned, maps, *extra],
        [pltpu.VMEM(maps.shape, BF)] if paired else [],
    )
    if paired:
        fields, charges, starts = exchange_z(send, *onward, panels, count)
    else:
        fields, charges, starts = exchange(send, panels, count)
    near = near_product(fields)
    (tail,) = call(
        "fourth",
        lambda *refs: fourth_kernel(starts, *refs),
        [((rows, LANES), F32)],
        [*charges, first_dir, second_dir, second_pre, self_row, near, maps, *full_rows],
        scratch,
    )
    sums, _ = sum_parts(tail, count)
    (result,) = call(
        "last",
        lambda *refs: last_kernel(len(sums), *refs),
        [((rows, panels), F32)],
        [*sums, scalars, first_pre, second_pre],
    )
    return result


def solution(mesh):
    placed = (
        P("rhs", "space"),
        P("space"),
        P("space", None, None, None),
        P("space", None),
        P("space"),
        P("space", None, None),
        P("space", None),
        P("space", "rhs", None),
        P("space"),
        P("space", None),
    )
    return jax.shard_map(
        on_device, mesh=mesh, in_specs=placed, out_specs=P("rhs", "space"), check_vma=False
    )
```

```python
import math

import jax
import jax.numpy as jnp
from jax import lax
from jax.experimental import pallas as pl
from jax.experimental.pallas import tpu as pltpu
from jax.sharding import PartitionSpec as P

EPS = 1e-06
F32 = jnp.float32
BF = jnp.bfloat16
AXIS = "space"
LANES = 128
HALF = 64


def swap(values, mask, count):
    return lax.ppermute(values, AXIS, [(i, i ^ mask) for i in range(count)])


def split(values):
    high = values.astype(BF)
    return high, (values - high.astype(F32)).astype(BF)


def dot_nn(left, right):
    return lax.dot_general(left, right, (((1,), (0,)), ((), ())), preferred_element_type=F32)


def dot_nt(left, right):
    return lax.dot_general(left, right, (((1,), (1,)), ((), ())), preferred_element_type=F32)


def dot_wide(dot, vector, high, low):
    rows = vector.shape[0]
    vec_high, vec_low = split(vector)
    first = dot(jnp.concatenate([vec_high, vec_low], axis=0), high)
    return first[:rows] + first[rows:] + dot(vec_high, low)


def row_sum(values):
    return jnp.sum(values, axis=1, keepdims=True)


def put_scalars(columns, rows):
    lane = lax.broadcasted_iota(jnp.int32, (rows, LANES), 1)
    out = jnp.zeros((rows, LANES), F32)
    for index, column in enumerate(columns):
        out = jnp.where(lane == index, column, out)
    return out


def column(values, index):
    return values[:, index : index + 1]


def charge_rows(field_low, maps_ref, send_ref):
    rows, panels = field_low.shape
    quarters, _, width = maps_ref.shape
    for quarter in range(quarters):
        both = dot_nt(field_low[:, quarter * width : (quarter + 1) * width], maps_ref[quarter])
        start = panels + quarter * LANES
        send_ref[:, start : start + LANES] = (both[:, :LANES] + both[:, LANES:]).astype(BF)


def build_maps(maps_ref, odd_start, skel, weights, block_count, rank, block):
    quarters = maps_ref.shape[0]
    per = block_count // quarters
    odd_start = pl.multiple_of(odd_start, HALF)
    maps_ref[...] = jnp.zeros(maps_ref.shape, BF)
    panel = lax.broadcasted_iota(jnp.int32, (rank, block), 1).astype(F32)
    for b in range(block_count):
        quarter, index = divmod(b, per)
        start = odd_start + index * rank
        cols = slice(index * block, (index + 1) * block)
        hot = jnp.where(skel[:rank, b : b + 1] == panel, 1.0, 0.0).astype(BF)
        maps_ref[quarter, pl.ds(start, rank), cols] = hot
        maps_ref[quarter, pl.ds(start + LANES, rank), cols] = weights(b)


def maps_kernel(sources, ids_ref, live_ref, weights_ref, skel_ref, maps_ref, places_ref):
    block_count, rank, block = weights_ref.shape
    skel = jnp.concatenate(
        [skel_ref[...].astype(F32), jnp.zeros((block_count, LANES - rank), F32)], axis=1
    ).T
    odd_start = (lax.axis_index(AXIS) % 2) * HALF
    build_maps(maps_ref, odd_start, skel, lambda b: weights_ref[b], block_count, rank, block)
    wanted = ids_ref[...]
    slots = wanted.shape[1]
    slot = lax.broadcasted_iota(jnp.int32, wanted.shape, 1)
    row = lax.broadcasted_iota(jnp.int32, wanted.shape, 0)
    counts = live_ref[...]
    live = slot < 0
    for b in range(block_count):
        live = live | ((row == b) & (slot < counts[0, b]))
    region = lax.axis_index(AXIS)
    place = block_place(wanted, live, block_count, sources, region).astype(F32)
    scale = jnp.where(slot % 4 == 0, 1.0, jnp.where(slot % 4 == 1, 64.0, 4096.0))
    scale = jnp.where(slot % 4 == 3, 262144.0, scale)
    lane = lax.broadcasted_iota(jnp.int32, (block_count, LANES), 1)
    packed = jnp.zeros((block_count, LANES), F32)
    for group in range(slots // 4):
        part = row_sum(jnp.where(slot // 4 == group, place * scale, 0.0))
        packed = jnp.where(lane == group, part, packed)
    places_ref[...] = packed.astype(jnp.int32)


def other_maps(base, rank, block, packs, maps_ref):
    chunks = packs[0][1].shape[1] // block
    per = maps_ref.shape[2] // block
    tall = per * rank // chunks
    odd_start = pl.multiple_of((1 - lax.axis_index(AXIS) % 2) * HALF, HALF)
    panel = lax.broadcasted_iota(jnp.int32, (rank, block), 1).astype(F32)
    for mask, ref in packs:
        quarter = lax.axis_index("rhs") ^ mask
        skel = ref[base + tall : base + tall + 16, :LANES].astype(F32)
        skel = jnp.concatenate([skel, jnp.zeros((LANES - 16, LANES), F32)], axis=0).T
        weights = jnp.concatenate(
            [ref[base : base + tall, j * block : (j + 1) * block] for j in range(chunks)], axis=0
        )
        for index in range(per):
            start = odd_start + index * rank
            cols = slice(index * block, (index + 1) * block)
            hot = jnp.where(skel[:rank, index : index + 1] == panel, 1.0, 0.0).astype(BF)
            maps_ref[quarter, pl.ds(start, rank), cols] = hot
            maps_ref[quarter, pl.ds(start + LANES, rank), cols] = weights[
                index * rank : (index + 1) * rank
            ]


def other_maps_kernel(base, rank, block, *refs):
    *pack_refs, maps_ref, turned_ref = refs
    for place, ref in enumerate(pack_refs):
        turned_ref[place] = ref[:base, :].T
    maps_ref[...] = jnp.zeros(maps_ref.shape, BF)
    other_maps(base, rank, block, list(enumerate(pack_refs)), maps_ref)


def onward_kernel(send_ref, near_ref, onward_ref, pair_ref):
    panels = near_ref.shape[1] - pair_ref.shape[1]
    pair = send_ref[:, panels:] + near_ref[:, panels:]
    onward_ref[:, :panels] = near_ref[:, :panels]
    onward_ref[:, panels:] = pair
    pair_ref[...] = pair


def neighbour_field(panels, scaled, proj, turned_ref, part_refs, onward_ref):
    rows = proj.shape[0]
    both = jnp.concatenate(split(proj), axis=0)
    size = panels // len(part_refs)
    for mask, ref in enumerate(part_refs):
        if mask < turned_ref.shape[0]:
            part = dot_nn(both, turned_ref[mask])
        else:
            part = dot_nt(both, ref[:size, :])
        start = pl.multiple_of((lax.axis_index("rhs") ^ mask) * size, size)
        field = scaled(start, size) - (part[:rows] + part[rows:])
        onward_ref[:, pl.ds(start, size)] = field.astype(BF)


def pair_charges(field_low, maps_ref, other_maps_ref, onward_ref, pair_ref):
    panels = field_low.shape[1]
    quarters, _, width = maps_ref.shape
    for quarter in range(quarters):
        cols = slice(quarter * width, (quarter + 1) * width)
        both = dot_nt(field_low[:, cols], maps_ref[quarter])
        both = both + dot_nt(onward_ref[:, cols], other_maps_ref[quarter])
        charge = (both[:, :LANES] + both[:, LANES:]).astype(BF)
        pair_ref[:, quarter * LANES : (quarter + 1) * LANES] = charge
        onward_ref[:, panels + quarter * LANES : panels + (quarter + 1) * LANES] = charge


def open_kernel(parts, paired, rhs_hbm, factor_hbm, diag_hbm, self_hbm, *refs):
    if paired:
        weights_hbm, skel_hbm, out_ref, rhs_ref, diag_ref, self_ref, high_ref, low_ref = refs[:8]
        pack_ref, held_ref, weights_ref, skel_ref, sems = refs[8:]
    else:
        out_ref, rhs_ref, diag_ref, self_ref, high_ref, low_ref, held_ref, sems = refs
    panels, width = factor_hbm.shape
    rows = rhs_ref.shape[0]
    depth = panels // parts
    pairs = [(rhs_hbm, rhs_ref), (diag_hbm, diag_ref), (self_hbm, self_ref)]
    if paired:
        pairs += [(weights_hbm, weights_ref), (skel_hbm, skel_ref)]
    loads = [
        pltpu.make_async_copy(source, target, sems.at[parts + index])
        for index, (source, target) in enumerate(pairs)
    ]
    for load in loads:
        load.start()
    copies = []
    for part in range(parts):
        span = pl.ds(part * depth, depth)
        copies.append(
            pltpu.make_async_copy(factor_hbm.at[span], held_ref.at[span], sems.at[part])
        )
        copies[-1].start()
    for load in loads:
        load.wait()
    rhs = rhs_ref[...]
    out_ref[:, width:] = put_scalars([row_sum(rhs * rhs)], rows)
    if paired:
        block_count, rank, block = weights_ref.shape
        quarters = lax.axis_size("rhs")
        quarter = lax.axis_index("rhs")
        size = panels // quarters
        per = block_count // quarters
        chunks = width // block
        tall = per * rank // chunks
        for index in range(per):
            values = weights_ref[quarter * per + index]
            for part in range(rank // tall):
                chunk = index * (rank // tall) + part
                pack_ref[size : size + tall, chunk * block : (chunk + 1) * block] = values[
                    part * tall : (part + 1) * tall
                ]
        skel = skel_ref[...].astype(F32)
        skel = jnp.concatenate([skel, jnp.zeros((block_count, width - rank), F32)], axis=1)
        row = lax.broadcasted_iota(jnp.int32, skel.shape, 0)
        picked = [
            jnp.sum(jnp.where(row == quarter * per + index, skel, 0.0), axis=0, keepdims=True)
            for index in range(per)
        ]
        picked.append(jnp.zeros((16 - per, width), F32))
        pack_ref[size + tall : size + tall + 16, :] = jnp.concatenate(picked, axis=0).astype(BF)
        start = size + tall + 16
        for part in split(diag_ref[...] * rhs):
            for first in range(0, panels, width):
                pack_ref[start : start + rows, :] = part[:, first : first + width]
                start += rows
    total = jnp.zeros((rows, width), F32)
    for part in range(parts):
        span = slice(part * depth, (part + 1) * depth)
        copies[part].wait()
        high, low = split(held_ref[span, :])
        high_ref[span, :] = high
        low_ref[span, :] = low
        total = total + dot_wide(dot_nn, rhs[:, span], high, low)
    out_ref[:, :width] = total
    if paired:
        pack_ref[:size, :] = high_ref[pl.ds(pl.multiple_of(quarter * size, size), size), :]


def turn_kernel(high_ref, low_ref, high_turned_ref, low_turned_ref):
    high_turned_ref[...] = high_ref[...].T
    low_turned_ref[...] = low_ref[...].T


def turn_blocks_kernel(mats_ref, turned_ref):
    block_count, slots, block, _ = mats_ref.shape
    for b in range(block_count):
        for k in range(slots):
            turned_ref[b, k * block : (k + 1) * block, :] = mats_ref[b, k].T


def first_kernel(parts, *refs):
    sums = refs[:parts]
    rhs_ref, diag_ref, high_ref, low_ref, maps_ref = refs[parts : parts + 5]
    dir_ref, pre_ref, keep_ref, send_ref = refs[parts + 5 :]
    width = high_ref.shape[0]
    rows, panels = rhs_ref.shape
    summed = sums[0][...]
    for ref in sums[1:]:
        summed = summed + ref[...]
    rhs_sq = column(summed[:, width:], 0)
    start_len = jnp.sqrt(rhs_sq + EPS)
    first_dir = rhs_ref[...] / start_len
    proj = summed[:, :width] / start_len
    first_pre = diag_ref[...] * first_dir - dot_wide(dot_nn, proj, high_ref[...], low_ref[...])
    field_low = first_pre.astype(BF)
    dir_ref[...] = first_dir
    pre_ref[...] = first_pre
    send_ref[:, :panels] = field_low
    charge_rows(field_low, maps_ref, send_ref)
    keep_ref[:, :width] = proj
    keep_ref[:, width:] = put_scalars([start_len, rhs_sq / (start_len * start_len)], rows)


def block_place(wanted, live, block_count, sources, region):
    source = wanted // block_count
    if sources == 4:
        slot = jnp.where(
            source == region,
            0,
            jnp.where(source == region ^ 1, 1, jnp.where(source == region ^ 3, 2, 3)),
        )
    else:
        slot = source - region + 1
    return jnp.where(live, slot * block_count + wanted % block_count, sources * block_count)


def near_kernel(sources, *refs):
    field_refs = refs[:sources]
    places_ref, mats_ref, near_ref, blocks_ref = refs[sources:]
    rows, panels = near_ref.shape
    block_count, deep, block = mats_ref.shape
    slots = deep // block
    packed = places_ref[...]
    for index, ref in enumerate(field_refs):
        for b in range(block_count):
            blocks_ref[index * block_count + b] = ref[:, b * block : (b + 1) * block]
    blocks_ref[sources * block_count] = jnp.zeros((rows, block), BF)
    for b in range(block_count):
        fours = [packed[b, group] for group in range(slots // 4)]
        places = [(fours[k // 4] >> (6 * (k % 4))) & 63 for k in range(slots)]
        picked = jnp.concatenate([blocks_ref[place] for place in places], axis=1)
        near_ref[:, b * block : (b + 1) * block] = dot_nn(picked, mats_ref[b])


def apply_matrix(field_ref, self_ref, near_ref, charge_refs, coupling_refs, maps_ref, charges_ref):
    rows, panels = field_ref.shape
    quarters, pairs = charges_ref.shape[:2]
    gathered = len(coupling_refs) == 1
    region = lax.axis_index(AXIS)
    first_quarter = 0 if gathered else lax.axis_index("rhs")
    for quarter in range(quarters):
        for index in range(pairs):
            if len(charge_refs) == pairs:
                ref, start = charge_refs[index]
                start += quarter * LANES
                charge = ref[:, start : start + LANES]
                charges_ref[quarter, (region // 2) ^ index] = charge
            else:
                lanes = slice(quarter * LANES, (quarter + 1) * LANES)
                charges_ref[quarter, index] = charge_refs[0][0][index, :, lanes]
    far = jnp.zeros((rows, coupling_refs[0].shape[-2]), F32)
    for index in range(quarters):
        quarter = first_quarter ^ index
        charge = jnp.concatenate([charges_ref[quarter, t] for t in range(pairs)], axis=1)
        rows_in = coupling_refs[0][index] if gathered else coupling_refs[index][...]
        far = far + dot_nt(charge, rows_in)
    odd = (region % 2) == 1
    per = panels // quarters
    for quarter in range(quarters):
        start = (quarter // 2) * LANES
        chunk = far[:, start : start + LANES]
        turned = pltpu.roll(chunk, HALF, 1)
        chunk = jnp.where(odd, turned, chunk) if quarter % 2 == 0 else jnp.where(odd, chunk, turned)
        high, low = split(chunk)
        both = jnp.concatenate([high, low], axis=0)
        pot = dot_nn(jnp.concatenate([both, both], axis=1), maps_ref[quarter])
        cols = slice(quarter * per, (quarter + 1) * per)
        near = near_ref[:, cols] + (pot[:rows] + pot[rows:])
        yield cols, near + self_ref[:, cols] * field_ref[:, cols]


def second_kernel(charge_starts, *refs):
    parts = len(charge_starts)
    charge_refs = list(zip(refs[:parts], charge_starts))
    dir_ref, pre_ref, self_ref, diag_ref = refs[parts : parts + 4]
    near_ref, maps_ref, high_ref, low_ref = refs[parts + 4 : parts + 8]
    *coupling_refs, res_ref, scaled_ref, out_ref, charges_ref = refs[parts + 8 :]
    width = high_ref.shape[1]
    rows = pre_ref.shape[0]
    for cols, values in apply_matrix(
        pre_ref, self_ref, near_ref, charge_refs, coupling_refs, maps_ref, charges_ref
    ):
        res_ref[:, cols] = values
    res = res_ref[...]
    out_ref[:, :width] = dot_wide(dot_nn, res, high_ref[...], low_ref[...])
    out_ref[:, width:] = put_scalars([row_sum(res * dir_ref[...]), row_sum(res * res)], rows)
    scaled_ref[...] = diag_ref[...] * res


def third_kernel(parts, rank, block, *refs):
    if rank:
        *refs, other_maps_ref = refs
    sums = refs[:parts]
    res_ref, dir_ref, keep_ref, diag_ref, high_ref, low_ref, maps_ref = refs[parts : parts + 7]
    *extra, next_ref, pre_ref, scalars_ref, send_ref = refs[parts + 7 :]
    width = high_ref.shape[0]
    rows, panels = res_ref.shape
    summed = sums[0][...]
    for ref in sums[1:]:
        summed = summed + ref[...]
    keep = keep_ref[:, width:]
    start_len, first_sq = column(keep, 0), column(keep, 1)
    diag_one, res_sq = column(summed[:, width:], 0), column(summed[:, width:], 1)
    below_sq = jnp.maximum(res_sq - diag_one * diag_one * (2.0 - first_sq), 0.0)
    below_one = jnp.sqrt(below_sq + EPS)
    second_dir = (res_ref[...] - diag_one * dir_ref[...]) / below_one
    proj = (summed[:, :width] - diag_one * keep_ref[:, :width]) / below_one
    pre = diag_ref[...] * second_dir - dot_wide(dot_nn, proj, high_ref[...], low_ref[...])
    field_low = pre.astype(BF)
    pre_ref[...] = pre
    if extra:
        got_ref, *part_refs, some_maps_ref, turned_ref, onward_ref, pair_ref = extra
        other_maps_ref[...] = some_maps_ref[...]
        last = len(part_refs) - 1
        other_maps(panels // (last + 1), rank, block, [(last, part_refs[last])], other_maps_ref)
        ratio = diag_one / start_len
        count = panels // width
        base = part_refs[0].shape[0] - 2 * count * rows
        before = []
        for index in range(count):
            high_rows = pl.ds(base + index * rows, rows)
            low_rows = pl.ds(base + (index + count) * rows, rows)
            before.append(
                part_refs[0][high_rows, :].astype(F32) + part_refs[0][low_rows, :].astype(F32)
            )
        scaled_ref = next_ref
        scaled_ref[...] = (
            got_ref[...] - ratio * jnp.concatenate(before, axis=1)
        ) / below_one

        def scaled(start, size):
            return scaled_ref[:, pl.ds(start, size)]

        neighbour_field(panels, scaled, proj, turned_ref, part_refs, onward_ref)
        send_ref[...] = field_low
        pair_charges(field_low, maps_ref, other_maps_ref, onward_ref, pair_ref)
    else:
        send_ref[:, :panels] = field_low
        charge_rows(field_low, maps_ref, send_ref)
    next_ref[...] = second_dir
    cross = diag_one * (1.0 - first_sq) / below_one
    second_sq = below_sq / (below_one * below_one)
    scalars_ref[...] = put_scalars(
        [start_len, first_sq, diag_one, below_one, cross, second_sq], rows
    )


def fourth_kernel(charge_starts, *refs):
    parts = len(charge_starts)
    charge_refs = list(zip(refs[:parts], charge_starts))
    dir_ref, next_ref, pre_ref, self_ref, near_ref, maps_ref = refs[parts : parts + 6]
    *coupling_refs, out_ref, charges_ref = refs[parts + 6 :]
    rows = pre_ref.shape[0]
    upper = diag = square = 0.0
    for cols, values in apply_matrix(
        pre_ref, self_ref, near_ref, charge_refs, coupling_refs, maps_ref, charges_ref
    ):
        upper = upper + row_sum(values * dir_ref[:, cols])
        diag = diag + row_sum(values * next_ref[:, cols])
        square = square + row_sum(values * values)
    out_ref[...] = put_scalars([upper, diag, square], rows)


def givens_pair(start_len, diag_one, below_one, upper_two, diag_two, below_two):
    radius_one = jnp.sqrt(diag_one * diag_one + below_one * below_one)
    cos_one = diag_one / radius_one
    sin_one = below_one / radius_one
    upper = cos_one * upper_two + sin_one * diag_two
    lower = cos_one * diag_two - sin_one * upper_two
    radius_two = jnp.sqrt(lower * lower + below_two * below_two)
    step_two = lower / radius_two * (-sin_one * start_len) / radius_two
    step_one = (cos_one * start_len - upper * step_two) / radius_one
    return (step_one, step_two)


def last_kernel(parts, *refs):
    scalars_ref, first_ref, second_ref, out_ref = refs[parts:]
    summed = refs[0][...]
    for ref in refs[1:parts]:
        summed = summed + ref[...]
    start_len, first_sq, diag_one, below_one, cross, second_sq = [
        column(scalars_ref[...], i) for i in range(6)
    ]
    upper_two, diag_two, res_sq = [column(summed, i) for i in range(3)]
    left_sq = (
        res_sq
        - upper_two * upper_two * (2.0 - first_sq)
        - diag_two * diag_two * (2.0 - second_sq)
        + 2.0 * upper_two * diag_two * cross
    )
    below_two = jnp.sqrt(jnp.maximum(left_sq, 0.0) + EPS)
    step_one, step_two = givens_pair(
        start_len, diag_one, below_one, upper_two, diag_two, below_two
    )
    out_ref[...] = step_one * first_ref[...] + step_two * second_ref[...]


def sum_parts(values, count, beside=()):
    if count != 8:
        return [lax.psum(values, AXIS)], beside
    pair = values + swap(values, 1, count)
    pair, *beside = lax.optimization_barrier((pair, *beside))
    return [pair, swap(pair, 2, count), swap(pair, 4, count), swap(pair, 6, count)], beside


def exchange_z(field, onward, pair, panels, count):
    two = swap(onward, 2, count)
    four = swap(pair, 4, count)
    six = swap(onward, 6, count)
    return [field, onward, two, six], [pair, two, four, six], [0, panels, 0, panels]


def exchange(send, panels, count):
    if count == 8:
        near = swap(send, 1, count)
        rows, long = send.shape
        onward, pair = call(
            "onward", onward_kernel, [((rows, long), BF), ((rows, long - panels), BF)], [send, near]
        )
        fields, charges, starts = exchange_z(send, onward, pair, panels, count)
        return [send, near] + fields[2:], charges, starts
    field, charges = send[:, :panels], send[:, panels:]
    ends = count - 1
    lower = lax.ppermute(field, AXIS, [(i, i + 1) for i in range(ends)])
    upper = lax.ppermute(field, AXIS, [(i + 1, i) for i in range(ends)])
    every = lax.all_gather(charges, AXIS)
    every = every.reshape((count // 2, 2) + charges.shape)
    return [lower, send, upper], [every[:, 0] + every[:, 1]], [0]


def gather_quarters(coupling, quarters, count, early):
    if count != 8 or quarters != 4:
        return [lax.all_gather(coupling, "rhs")], early
    coupling, early = lax.optimization_barrier((coupling, early))
    pairs = [[(i, i ^ mask) for i in range(quarters)] for mask in (1, 2)]
    return [coupling] + [lax.ppermute(coupling, "rhs", pair) for pair in pairs], early


def finish_quarters(rows, quarters, late):
    if len(rows) == 1:
        return rows, late
    far, late = lax.optimization_barrier((rows[2], late))
    return rows + [lax.ppermute(far, "rhs", [(i, i ^ 1) for i in range(quarters)])], late


def nbytes(shape, kind):
    return math.prod(shape) * jnp.dtype(kind).itemsize


def room(*arrays):
    return pltpu.CompilerParams(
        vmem_limit_bytes=sum(nbytes(a.shape, a.dtype) for a in arrays) * 5 // 4 + 4 * 2**20
    )


def call(name, kernel, out_shapes, args, scratch=(), far=(), flops=0):
    out_shapes = [jax.ShapeDtypeStruct(shape, kind) for shape, kind in out_shapes]
    args = [pltpu.with_memory_space_constraint(x, pltpu.HBM) if i in far else x
            for i, x in enumerate(args)]
    specs = [
        pl.BlockSpec(
            memory_space=pltpu.HBM if i in far else pltpu.VMEM
        )
        for i in range(len(args))
    ]
    outs = [pl.BlockSpec(memory_space=pltpu.VMEM)] * len(out_shapes)
    held = [x for i, x in enumerate(args) if i not in far]
    held += [x for x in scratch if getattr(x, "memory_space", None) == pltpu.VMEM]
    return pl.pallas_call(
        kernel,
        name=name,
        out_shape=out_shapes,
        in_specs=specs,
        out_specs=outs,
        scratch_shapes=list(scratch),
        cost_estimate=pl.CostEstimate(flops=flops, bytes_accessed=flops // 500, transcendentals=0) if flops else None,
        compiler_params=room(*held, *out_shapes),
    )(*args)


def on_device(
    rhs_vec,
    self_coef,
    near_mats,
    near_ids,
    near_count,
    interp,
    skel_idx,
    coupling,
    diag_prec,
    low_rank,
):
    rows, panels = rhs_vec.shape
    block_count, slots, block, _ = near_mats.shape
    rank = interp.shape[2]
    quarters = lax.axis_size("rhs")
    count = lax.axis_size(AXIS)
    width = low_rank.shape[1]
    sources = 4 if count == 8 else 3
    weights = jnp.swapaxes(interp, 1, 2)
    maps, places = call(
        "maps",
        lambda *refs: maps_kernel(sources, *refs),
        [((quarters, 2 * LANES, panels // quarters), BF), ((block_count, LANES), jnp.int32)],
        [near_ids, near_count[None, :], weights, skel_idx],
    )
    wide = width + LANES
    long = panels + quarters * LANES
    paired = count == 8 and quarters == 4
    parts = 4
    args = [rhs_vec, low_rank, diag_prec[None, :], self_coef[None, :]]
    outs = [((rows, wide), F32), ((rows, panels), F32), ((1, panels), F32),
            ((1, panels), F32), (low_rank.shape, BF), (low_rank.shape, BF)]
    scratch = [pltpu.VMEM((panels, width), F32)]
    if paired:
        args += [weights, skel_idx]
        tall = block_count // quarters * rank * block // width
        packed = panels // quarters + tall + 16 + 2 * rows * panels // width
        outs += [((packed, width), BF)]
        scratch += [pltpu.VMEM(weights.shape, BF), pltpu.VMEM(skel_idx.shape, jnp.int32)]
    payload, rhs_near, diag_row, self_row, high, low, *packs = call(
        "open",
        lambda *refs: open_kernel(parts, paired, *refs),
        outs,
        args,
        scratch + [pltpu.SemaphoreType.DMA((parts + 5,))],
        far=range(len(args)),
    )
    (blocks,) = call(
        "turn_blocks",
        turn_blocks_kernel,
        [((block_count, slots * block, block), BF)],
        [near_mats],
    )
    turned = call("turn", turn_kernel, [((width, panels), BF)] * 2, [high, low])
    some_rows, payload = gather_quarters(coupling[:, 0, :], quarters, count, payload)
    sums, (*turned, blocks) = sum_parts(payload, count, [*turned, blocks])
    if paired:
        mine = swap(packs[0], 1, count)
    first_dir, first_pre, keep, send = call(
        "first",
        lambda *refs: first_kernel(len(sums), *refs),
        [((rows, panels), F32), ((rows, panels), F32), ((rows, wide), F32), ((rows, long), BF)],
        [*sums, rhs_near, diag_row, *turned, maps],
        flops=2*10**9,
    )
    fields, charges, starts = exchange(send, panels, count)
    full_rows, fields[1] = finish_quarters(some_rows, quarters, fields[1])
    if paired:
        mine, fields[1] = lax.optimization_barrier((mine, fields[1]))
        far = lax.ppermute(mine, "rhs", [(i, i ^ 2) for i in range(quarters)])

    def near_product(fields):
        (near,) = call(
            "near",
            lambda *refs: near_kernel(len(fields), *refs),
            [((rows, panels), F32)],
            [*fields, places, blocks],
            [pltpu.VMEM((len(fields) * block_count + 1, rows, block), BF)],
            flops=10**10,
        )
        return near

    near = near_product(fields)
    scratch = [pltpu.VMEM((quarters, count // 2, rows, LANES), BF)]
    residue, scaled, payload = call(
        "second",
        lambda *refs: second_kernel(starts, *refs),
        [((rows, panels), F32), ((rows, panels), F32), ((rows, wide), F32)],
        [*charges, first_dir, first_pre, self_row, diag_row, near, maps, high, low, *full_rows],
        scratch,
        flops=10**10,
    )
    if paired:
        mine, payload = lax.optimization_barrier((mine, payload))
    sums, _ = sum_parts(payload, count)
    outs = [((rows, panels), F32), ((rows, panels), F32), ((rows, LANES), F32)]
    extra = []
    if paired:
        again = swap(scaled, 1, count)
        far, sums[0] = lax.optimization_barrier((far, sums[0]))
        near_pack, last_pack = [
            lax.ppermute(x, "rhs", [(i, i ^ 1) for i in range(quarters)]) for x in (mine, far)
        ]
        mine = [mine, near_pack, far, last_pack]
        extra = call(
            "other_maps",
            lambda *refs: other_maps_kernel(panels // quarters, rank, block, *refs),
            [(maps.shape, BF), ((quarters - 1, width, panels // quarters), BF)],
            mine[:-1],
            flops=10**10,
        )
        extra = [again, *mine, *extra]
        outs = [((rows, long), BF), ((rows, long - panels), BF), *outs, ((rows, panels), BF)]
    else:
        outs += [((rows, long), BF)]
    *onward, second_dir, second_pre, scalars, send = call(
        "third",
        lambda *refs: third_kernel(len(sums), paired * rank, block, *refs),
        outs,
        [*sums, residue, first_dir, keep, diag_row, *turned, maps, *extra],
        [pltpu.VMEM(maps.shape, BF)] if paired else [],
    )
    if paired:
        fields, charges, starts = exchange_z(send, *onward, panels, count)
    else:
        fields, charges, starts = exchange(send, panels, count)
    near = near_product(fields)
    (tail,) = call(
        "fourth",
        lambda *refs: fourth_kernel(starts, *refs),
        [((rows, LANES), F32)],
        [*charges, first_dir, second_dir, second_pre, self_row, near, maps, *full_rows],
        scratch,
    )
    sums, _ = sum_parts(tail, count)
    (result,) = call(
        "last",
        lambda *refs: last_kernel(len(sums), *refs),
        [((rows, panels), F32)],
        [*sums, scalars, first_pre, second_pre],
    )
    return result


def solution(mesh):
    placed = (
        P("rhs", "space"),
        P("space"),
        P("space", None, None, None),
        P("space", None),
        P("space"),
        P("space", None, None),
        P("space", None),
        P("space", "rhs", None),
        P("space"),
        P("space", None),
    )
    return jax.shard_map(
        on_device, mesh=mesh, in_specs=placed, out_specs=P("rhs", "space"), check_vma=False
    )
```
